32 devices in a mesh: batch: 8 (over y, x, core), chan: 4 (over z).
Axes of the slice: x: 2, y: 2, z: 4, core: 2. Of those that a mesh axis runs over, the one named last changes fastest.
Arguments:
- image_big: bfloat16 [512, 14, 14, 256], P(('batch', 'chan')), may hold values from -40 to 40
- image_small: bfloat16 [1024, 6, 6, 256], P(('batch', 'chan')), may hold values from -40 to 40
- slope_big: bfloat16 [512, 7, 7, 512], P('batch', None, None, 'chan'), may hold values from -40 to 40
- slope_small: bfloat16 [1024, 3, 3, 512], P('batch', None, None, 'chan'), may hold values from -40 to 40
- conv1_weight: float32 [3, 3, 256, 512], P(None, None, 'batch', 'chan'), may hold values from -0.125 to 0.125
- conv2_weight: float32 [3, 3, 512, 512], P(None, None, 'batch', 'chan'), may hold values from -0.09375 to 0.09375
- proj_weight: float32 [256, 512], P('batch', 'chan'), may hold values from -0.375 to 0.375
- norm_params: float32 [6, 512], P(None, 'chan'), may hold values from 0.1 to 1.9
- first_conv1: float32 [3, 3, 256, 512], P(None, None, 'batch', 'chan')
- first_conv2: float32 [3, 3, 512, 512], P(None, None, 'batch', 'chan')
- first_proj: float32 [256, 512], P('batch', 'chan')
- first_norms: float32 [6, 512], P(None, 'chan')
- second_conv1: float32 [3, 3, 256, 512], P(None, None, 'batch', 'chan'), as said below
- second_conv2: float32 [3, 3, 512, 512], P(None, None, 'batch', 'chan'), as said below
- second_proj: float32 [256, 512], P('batch', 'chan'), as said below
- second_norms: float32 [6, 512], P(None, 'chan'), as said below
Outputs:
- out_big: bfloat16 [512, 7, 7, 512], P('batch', None, None, 'chan')
- out_small: bfloat16 [1024, 3, 3, 512], P('batch', None, None, 'chan')
- grad_big: bfloat16 [512, 14, 14, 256], P(('batch', 'chan'))
- grad_small: bfloat16 [1024, 6, 6, 256], P(('batch', 'chan'))
- grad_conv1: float32 [3, 3, 256, 512], P(None, None, 'batch', 'chan')
- grad_conv2: float32 [3, 3, 512, 512], P(None, None, 'batch', 'chan')
- grad_proj: float32 [256, 512], P('batch', 'chan')
- grad_norms: float32 [6, 512], P(None, 'chan')
- new_conv1: float32 [3, 3, 256, 512], P(None, None, 'batch', 'chan')
- new_conv2: float32 [3, 3, 512, 512], P(None, None, 'batch', 'chan')
- new_proj: float32 [256, 512], P('batch', 'chan')
- new_norms: float32 [6, 512], P(None, 'chan')
- moment_conv1: float32 [3, 3, 256, 512], P(None, None, 'batch', 'chan')
- moment_conv2: float32 [3, 3, 512, 512], P(None, None, 'batch', 'chan')
- moment_proj: float32 [256, 512], P('batch', 'chan')
- moment_norms: float32 [6, 512], P(None, 'chan')
- square_conv1: float32 [3, 3, 256, 512], P(None, None, 'batch', 'chan')
- square_conv2: float32 [3, 3, 512, 512], P(None, None, 'batch', 'chan')
- square_proj: float32 [256, 512], P('batch', 'chan')
- square_norms: float32 [6, 512], P(None, 'chan')
The draws below stay inside these ranges and needn't reach their ends.
Inputs may be any that keep to these rules, and one draw needn't show every extreme that they name: `second_conv1`: Positive. `second_conv2`: Positive. `second_proj`: Positive. `second_norms`: Positive.
All inputs are finite; a program needn't handle non-finite values.
Results may differ from the reference program's by a relative error of at most 0.0078.
Values may be sent and summed in bfloat16 or wider, within the bound.
A program may use at most 320 MiB of HBM per device.

```python
import jax
import jax.numpy as jnp
from jax import lax

C_IN = 256
C_OUT = 512
MAP_BIG = 14
MAP_SMALL = 6
STEP = 5
OUT_BIG = 7
OUT_SMALL = 3
BIG = 512
SMALL = 1024
POS = 34304


def image_scale(images, ceiling):
    position = jnp.arange(images, dtype=jnp.float32) / (images - 1)
    return jnp.exp(jnp.log(ceiling) * position)


def normal_values(key, extent):
    return jnp.clip(jax.random.normal(key, extent, jnp.float32), -6.0, 6.0)


def scaled_field(values, images, ceiling):
    return values * image_scale(images, ceiling)[:, None, None, None]


def draw_image_big(key, part):
    key = jax.random.fold_in(key, 11)
    extent = (BIG, MAP_BIG, MAP_BIG, C_IN)
    return scaled_field(normal_values(key, extent), BIG, 3.0).astype(jnp.bfloat16)


def draw_image_small(key, part):
    key = jax.random.fold_in(key, 12)
    extent = (SMALL, MAP_SMALL, MAP_SMALL, C_IN)
    return scaled_field(normal_values(key, extent), SMALL, 3.0).astype(jnp.bfloat16)


def draw_slope_big(key, part):
    key = jax.random.fold_in(key, 13)
    extent = (BIG, OUT_BIG, OUT_BIG, C_OUT)
    return scaled_field(normal_values(key, extent), BIG, 3.0).astype(jnp.bfloat16)


def draw_slope_small(key, part):
    key = jax.random.fold_in(key, 14)
    extent = (SMALL, OUT_SMALL, OUT_SMALL, C_OUT)
    return scaled_field(normal_values(key, extent), SMALL, 3.0).astype(jnp.bfloat16)


def first_moment(key, extent, square_size):
    return jnp.clip(jax.random.normal(key, extent, jnp.float32), -5.0, 5.0) * jnp.sqrt(jnp.float32(square_size))


def second_moment(key, extent, square_size):
    return jnp.exp(jax.random.uniform(key, extent, jnp.float32, 0.0, 1.3862944)) * jnp.float32(square_size)


def draw_first_conv1(key, part):
    key = jax.random.fold_in(key, 21)
    return first_moment(key, (3, 3, C_IN, C_OUT), 1.0 * POS)


def draw_first_conv2(key, part):
    key = jax.random.fold_in(key, 22)
    return first_moment(key, (3, 3, C_OUT, C_OUT), 2.0 * POS)


def draw_first_proj(key, part):
    key = jax.random.fold_in(key, 23)
    return first_moment(key, (C_IN, C_OUT), 2.0 * POS)


def draw_first_norms(key, part):
    key = jax.random.fold_in(key, 24)
    return first_moment(key, (6, C_OUT), 2.0 * POS)


def draw_second_conv1(key, part):
    key = jax.random.fold_in(key, 31)
    return second_moment(key, (3, 3, C_IN, C_OUT), 1.0 * POS)


def draw_second_conv2(key, part):
    key = jax.random.fold_in(key, 32)
    return second_moment(key, (3, 3, C_OUT, C_OUT), 2.0 * POS)


def draw_second_proj(key, part):
    key = jax.random.fold_in(key, 33)
    return second_moment(key, (C_IN, C_OUT), 2.0 * POS)


def draw_second_norms(key, part):
    key = jax.random.fold_in(key, 34)
    return second_moment(key, (6, C_OUT), 2.0 * POS)


def block_scale(stream_key, shape, pieces, low, largest):
    def one(dim, shards_of):
        draws = jax.random.uniform(jax.random.fold_in(jax.random.fold_in(stream_key, 6), dim), (shards_of,), jnp.float32, low / len(pieces), largest / len(pieces))
        return jnp.repeat(jnp.exp(draws), shape[dim] // shards_of).reshape((-1,) + (1,) * (len(shape) - dim - 1))

    loudness = one(*pieces[0])
    for cut in pieces[1:]:
        loudness = loudness * one(*cut)
    return loudness


def scatter_about(own_key, shape, deviation, most, split=(), kind=jnp.bfloat16):
    drawn = deviation * jax.random.normal(own_key, shape, jnp.float32)
    if split:
        drawn = drawn * block_scale(own_key, shape, split, -0.22, 0.18)
    return jnp.clip(drawn, -most, most).astype(kind)


def setup_inputs(seed: int = 0) -> dict:
    arg_keys = jax.random.split(jax.random.key(seed), 17)
    return {
        "image_big": draw_image_big(jax.random.fold_in(arg_keys[16], 71), 0),
        "image_small": draw_image_small(jax.random.fold_in(arg_keys[16], 71), 0),
        "slope_big": draw_slope_big(jax.random.fold_in(arg_keys[16], 71), 0),
        "slope_small": draw_slope_small(jax.random.fold_in(arg_keys[16], 71), 0),
        "conv1_weight": scatter_about(arg_keys[4], (3, 3, C_IN, C_OUT), (9 * C_IN) ** -0.5, 0.125, ((2, 8), (3, 4)), jnp.float32),
        "conv2_weight": scatter_about(arg_keys[5], (3, 3, C_OUT, C_OUT), (9 * C_OUT) ** -0.5, 0.09375, ((2, 8), (3, 4)), jnp.float32),
        "proj_weight": scatter_about(arg_keys[6], (C_IN, C_OUT), C_IN ** -0.5, 0.375, ((0, 8), (1, 4)), jnp.float32),
        "norm_params": jnp.clip(1.0 + 0.18 * jax.random.normal(arg_keys[7], (6, C_OUT), jnp.float32), 0.1, 1.9),
        "first_conv1": draw_first_conv1(jax.random.fold_in(arg_keys[16], 71), 0),
        "first_conv2": draw_first_conv2(jax.random.fold_in(arg_keys[16], 71), 0),
        "first_proj": draw_first_proj(jax.random.fold_in(arg_keys[16], 71), 0),
        "first_norms": draw_first_norms(jax.random.fold_in(arg_keys[16], 71), 0),
        "second_conv1": draw_second_conv1(jax.random.fold_in(arg_keys[16], 71), 0),
        "second_conv2": draw_second_conv2(jax.random.fold_in(arg_keys[16], 71), 0),
        "second_proj": draw_second_proj(jax.random.fold_in(arg_keys[16], 71), 0),
        "second_norms": draw_second_norms(jax.random.fold_in(arg_keys[16], 71), 0),
    }


@jax.custom_vjp
def low(v):
    return lax.optimization_barrier(v.astype(jnp.bfloat16)).astype(jnp.float32)

@jax.custom_vjp
def low_back(v):
    return v

def low_keep(v):
    return (low(v), None)

def low_pass(kept, grad):
    return (grad,)

def back_keep(v):
    return (v, None)

def back_low(kept, grad):
    return (low(grad),)
low.defvjp(low_keep, low_pass)
low_back.defvjp(back_keep, back_low)
HIGHEST = lax.Precision.HIGHEST
NORM_EPS = 1e-05
BETA_ONE = 0.5
BETA_TWO = 0.5
ADAM_EPS = 1e-08
DECAY = 0.01
NORM_RATE = 0.3

def conv_taps(inputs, kernel, stride):
    images = inputs.shape[0]
    size_out = (inputs.shape[1] - 1) // stride + 1
    reach = stride * (size_out - 1) + 1
    padded = jnp.pad(inputs, ((0, 0), (1, 1), (1, 1), (0, 0)))
    summed = jnp.zeros((images, size_out, size_out, kernel.shape[3]), jnp.float32)
    for tap_row in range(3):
        for tap_col in range(3):
            window = lax.slice(padded, (0, tap_row, tap_col, 0), (images, tap_row + reach, tap_col + reach, padded.shape[3]), (1, stride, stride, 1))
            summed = summed + jnp.einsum('nhwc,co->nhwo', window, kernel[tap_row, tap_col], precision=HIGHEST)
    return summed

def norm_apply(values, gain, shift):
    center = lax.optimization_barrier(jnp.mean(values, axis=(0, 1, 2)))
    square = lax.optimization_barrier(jnp.mean(values * values, axis=(0, 1, 2)))
    return (values - center) * lax.rsqrt(square - center * center + NORM_EPS) * gain + shift

def forward(image_big, image_small, conv1_weight, conv2_weight, proj_weight, norm_params):
    kernel_one = low(conv1_weight)
    kernel_two = low(conv2_weight)
    kernel_proj = low(proj_weight)
    results = []
    for images in (image_big, image_small):
        first_pre = low_back(conv_taps(images, kernel_one, 2))
        hidden = low(jax.nn.silu(norm_apply(first_pre, norm_params[0], norm_params[1])))
        second_pre = low_back(conv_taps(hidden, kernel_two, 1))
        proj_pre = low_back(jnp.einsum('nhwc,co->nhwo', images[:, ::2, ::2, :], kernel_proj, precision=HIGHEST))
        summed = norm_apply(second_pre, norm_params[2], norm_params[3]) + norm_apply(proj_pre, norm_params[4], norm_params[5])
        results.append(jax.nn.silu(summed))
    return (results[0], results[1])

def adamw_step(weight, gradient, first, second, rate, decay):
    first_new = BETA_ONE * first + (1.0 - BETA_ONE) * gradient
    second_new = BETA_TWO * second + (1.0 - BETA_TWO) * gradient * gradient
    first_hat = first_new / (1.0 - BETA_ONE ** STEP)
    second_hat = second_new / (1.0 - BETA_TWO ** STEP)
    updated = weight - rate * (first_hat / (jnp.sqrt(second_hat) + ADAM_EPS) + decay * weight)
    return (updated, first_new, second_new)

def reference(image_big, image_small, slope_big, slope_small, conv1_weight, conv2_weight, proj_weight, norm_params, first_conv1, first_conv2, first_proj, first_norms, second_conv1, second_conv2, second_proj, second_norms):
    primals = (image_big.astype(jnp.float32), image_small.astype(jnp.float32), conv1_weight, conv2_weight, proj_weight, norm_params)
    outputs, pullback = jax.vjp(forward, *primals)
    grads = pullback((slope_big.astype(jnp.float32), slope_small.astype(jnp.float32)))
    grad_big, grad_small, grad_conv1, grad_conv2, grad_proj, grad_norms = grads
    new_conv1, moment_conv1, square_conv1 = adamw_step(conv1_weight, grad_conv1, first_conv1, second_conv1, (9.0 * C_IN) ** (-0.5), DECAY)
    new_conv2, moment_conv2, square_conv2 = adamw_step(conv2_weight, grad_conv2, first_conv2, second_conv2, (9.0 * C_OUT) ** (-0.5), DECAY)
    new_proj, moment_proj, square_proj = adamw_step(proj_weight, grad_proj, first_proj, second_proj, (1.0 * C_IN) ** (-0.5), DECAY)
    new_norms, moment_norms, square_norms = adamw_step(norm_params, grad_norms, first_norms, second_norms, NORM_RATE, 0.0)
    return (outputs[0].astype(jnp.bfloat16), outputs[1].astype(jnp.bfloat16), grad_big.astype(jnp.bfloat16), grad_small.astype(jnp.bfloat16), grad_conv1, grad_conv2, grad_proj, grad_norms, new_conv1, new_conv2, new_proj, new_norms, moment_conv1, moment_conv2, moment_proj, moment_norms, square_conv1, square_conv2, square_proj, square_norms)
```

```python
import functools

import jax
import jax.numpy as jnp
from jax import lax
from jax.experimental import pallas as pl
from jax.experimental.pallas import tpu as pltpu
from jax.sharding import PartitionSpec as P

C_IN = 256
C_OUT = 512
STEP = 5
NORM_EPS = 1e-05
BETA_ONE = 0.5
BETA_TWO = 0.5
ADAM_EPS = 1e-08
DECAY = 0.01
NORM_RATE = 0.3
MESH = pl.DeviceIdType.MESH
BF16 = jnp.bfloat16
F32 = jnp.float32
COPIES = 176
VMEM_BYTES = 60 << 20


def silu_slope(values):
    gate = jax.nn.sigmoid(values)
    return gate * (1.0 + values * (1.0 - gate))


def adamw_step(weight, gradient, first, second, rate, decay):
    first_new = BETA_ONE * first + (1.0 - BETA_ONE) * gradient
    second_new = BETA_TWO * second + (1.0 - BETA_TWO) * gradient * gradient
    first_hat = first_new / (1.0 - BETA_ONE**STEP)
    second_hat = second_new / (1.0 - BETA_TWO**STEP)
    updated = weight - rate * (first_hat / (jnp.sqrt(second_hat) + ADAM_EPS) + decay * weight)
    return (updated, first_new, second_new)


def fold(values):
    rows, channels = values.shape
    return jnp.sum(values.reshape(rows // 8, 8, channels), axis=0)


def block_kernel(
    cfg,
    img_big, img_small, slo_big, slo_small, w1_in, w2_in, wp_in, norms_in,
    out_big, out_small, grad_big, grad_small, grad_one, grad_two, grad_norms,
    w1, w2, x_big, x_small, h_big, h_small, first_pre, second_pre, proj_pre, work,
    sl_big, sl_small, os_big, os_small, t_big, t_small, p_big, p_small, s_big, s_small,
    norms, norm_rows, stat_a, stat_b, a1, r1, rx1, ry1, rxx1, ryy1, c1, rz1,
    a2, r2, rx2, ry2, rxx2, ryy2, c2, rz2,
    send_sem, recv_sem, local_sem,
):
    nb_img, ns_img, ob, os_, number_big, number_small = cfg
    rows_b, rows_s = ob * ob * nb_img, os_ * os_ * ns_img
    step_b, step_s = ob * nb_img, os_ * ns_img
    b = lax.axis_index("batch")
    z = lax.axis_index("chan")
    core = lax.rem(b, 2)
    x = lax.rem(lax.div(b, 2), 2)
    y = lax.div(b, 4)
    x_peer = (b + 2 - 4 * x, z)
    y_peer = (b + 4 - 8 * y, z)
    sibling = (b + 1 - 2 * core, z)
    z_peers = [(b, lax.rem(z + d, 4)) for d in (1, 2, 3)]
    b_peers = [(lax.rem(b + d, 8), z) for d in range(1, 8)]
    lanes = lambda which: pl.ds(pl.multiple_of(which * 128, 128), 128)
    mine = lanes(z)

    used = [0]
    started = []

    def send(src, dst, peer):
        slot = used[0]
        used[0] += 1
        copy = pltpu.make_async_remote_copy(
            src_ref=src,
            dst_ref=dst,
            send_sem=send_sem.at[slot],
            recv_sem=recv_sem.at[slot],
            device_id=peer,
            device_id_type=MESH,
        )
        copy.start()
        started.append(copy)
        return copy

    barrier = pltpu.get_barrier_semaphore()
    for peer in b_peers + z_peers:
        pl.semaphore_signal(barrier, inc=1, device_id=peer, device_id_type=MESH)

    loads = []

    def load(src, dst):
        copy = pltpu.make_async_copy(src, dst, local_sem.at[len(loads)])
        copy.start()
        loads.append(copy)

    for hp in range(2):
        for wp in range(2):
            load(img_big.at[:, hp, :, wp], x_big.at[hp, wp, pl.ds(hp, ob), pl.ds(wp, ob)])
            load(img_small.at[:, hp, :, wp], x_small.at[hp, wp, pl.ds(hp, os_), pl.ds(wp, os_)])
    load(
        slo_big.at[:, :, pl.ds(pl.multiple_of(z * nb_img, nb_img), nb_img)],
        sl_big.at[:, :, :, mine],
    )
    load(
        slo_small.at[:, :, pl.ds(pl.multiple_of(z * ns_img, ns_img), ns_img)],
        sl_small.at[:, :, :, mine],
    )
    w1[0:9, y, x, core, :, mine] = w1_in[...].astype(BF16)
    w1[9, y, x, core, :, mine] = wp_in[...].astype(BF16)
    w2[:, y, x, core, :, mine] = w2_in[...].astype(BF16)
    norms[z, 0:6] = norms_in[...]

    pl.semaphore_wait(barrier, 10)

    def gather_z(w):
        piece = w.at[:, y, x, core, :, mine]
        return [send(piece, piece, peer) for peer in z_peers]

    def gather_xy(w):
        piece = w.at[:, y, x, core]
        return [
            send(piece, piece, x_peer),
            send(piece, piece, y_peer),
            send(piece, piece, sibling),
        ]

    def gather_forward(w, near):
        near[0].wait_recv()
        piece = w.at[:, y, 1 - x, core]
        part = w.at[:, y, 1 - x, core, :, pl.ds(0, 256)]
        far_a = send(part, part, y_peer)
        sib_x = send(piece, piece, sibling)
        near[1].wait_recv()
        piece = w.at[:, 1 - y, x, core]
        part = w.at[:, 1 - y, x, core, :, pl.ds(256, 256)]
        far_b = send(part, part, x_peer)
        sib_y = send(piece, piece, sibling)
        return [far_a, far_b, near[2], sib_x, sib_y]

    def gather_last(w, far):
        far[0].wait_recv()
        far[1].wait_recv()
        piece = w.at[:, 1 - y, 1 - x, core]
        return far[2:] + [send(piece, piece, sibling)]

    def finish(copies):
        for copy in copies:
            copy.wait_recv()

    z_one = gather_z(w1)
    z_norms = [send(norms.at[z], norms.at[z], peer) for peer in z_peers]
    z_two = gather_z(w2)

    zero = functools.partial(jnp.zeros, dtype=BF16)
    for wp in range(2):
        x_big[1, wp, 0] = zero((ob + 1, nb_img, 256))
        x_small[1, wp, 0] = zero((os_ + 1, ns_img, 256))
    for hp in range(2):
        x_big[hp, 1, :, 0] = zero((ob + 1, nb_img, 256))
        x_small[hp, 1, :, 0] = zero((os_ + 1, ns_img, 256))
    for ref, side, images in (
        (h_big, ob, nb_img), (t_big, ob, nb_img), (h_small, os_, ns_img), (t_small, os_, ns_img),
    ):
        ref[0] = zero((side + 2, images, 512))
        ref[side + 1] = zero((side + 2, images, 512))
        ref[:, 0] = zero((side + 2, images, 512))
        ref[:, side + 1] = zero((side + 2, images, 512))
    for ref, side, images in ((s_big, ob, nb_img), (s_small, os_, ns_img)):
        ref[side] = zero((side + 1, images, 512))
        ref[:, side] = zero((side + 1, images, 512))

    finish(z_one)
    near_one = gather_xy(w1)
    finish(z_two)
    near_two = gather_xy(w2)
    slope_copies = []
    for d in (1, 2, 3):
        to = lax.rem(z + d, 4)
        slope_copies.append(
            send(
                slo_big.at[:, :, pl.ds(pl.multiple_of(to * nb_img, nb_img), nb_img)],
                sl_big.at[:, :, :, mine],
                (b, to),
            )
        )
        slope_copies.append(
            send(
                slo_small.at[:, :, pl.ds(pl.multiple_of(to * ns_img, ns_img), ns_img)],
                sl_small.at[:, :, :, mine],
                (b, to),
            )
        )
    far_one = gather_forward(w1, near_one)
    last_one = gather_last(w1, far_one)
    finish(z_norms)
    gains = [
        jnp.concatenate([norms[q, r : r + 1, :] for q in range(4)], axis=1) for r in range(6)
    ]
    for copy in loads:
        copy.wait()
    finish(last_one)

    def reduce_start(k, rows):
        for r, row in enumerate(rows):
            stat_a[k, b, r : r + 1, :] = jnp.sum(row, axis=0, keepdims=True)
        for r in range(len(rows), 8):
            stat_a[k, b, r : r + 1, :] = jnp.zeros((1, 512), F32)
        return [send(stat_a.at[k, b], stat_a.at[k, b], peer) for peer in b_peers]

    def reduce_middle(k, copies):
        finish(copies)
        stat_b[k, z] = jnp.sum(stat_a[k], axis=0)
        return [send(stat_b.at[k, z], stat_b.at[k, z], peer) for peer in z_peers]

    def reduce_end(k, copies):
        finish(copies)
        total = jnp.sum(stat_b[k], axis=0)
        return [total[r : r + 1, :] for r in range(8)]

    def chunk_big(i):
        return pl.ds(pl.multiple_of(i * step_b, 16), step_b)

    def chunk_small(i):
        return pl.ds(pl.multiple_of(rows_b + i * step_s, 16), step_s)

    def over_groups(body, count):
        start = tuple(jnp.zeros((8, 512), F32) for _ in range(count))
        big = lax.fori_loop(0, ob, lambda i, c: body(0, i, chunk_big(i), c), start)
        small = lax.fori_loop(0, os_, lambda i, c: body(1, i, chunk_small(i), c), start)
        return big, small

    def moments(ref):
        def body(group, i, rows, carry):
            v = ref[rows, :]
            return (carry[0] + fold(v), carry[1] + fold(v * v))

        return over_groups(body, 2)

    def both(big, small):
        return jnp.concatenate([big.reshape(rows_b, -1), small.reshape(rows_s, -1)], axis=0)

    def x_window(ta, tb):
        half, odd = (lambda v: v // 2, lambda v: v % 2) if isinstance(ta, int) else (
            lambda v: lax.div(v, 2), lambda v: lax.rem(v, 2)
        )
        hp, wp, sa, sb = odd(ta + 1), odd(tb + 1), half(ta), half(tb)
        return both(
            x_big[hp, wp, pl.ds(sa, ob), pl.ds(sb, ob)],
            x_small[hp, wp, pl.ds(sa, os_), pl.ds(sb, os_)],
        )

    def dot(left, right):
        return jnp.dot(left, right, preferred_element_type=F32)

    def dot_t(left, right):
        return lax.dot_general(left, right, (((1,), (1,)), ((), ())), preferred_element_type=F32)

    def dot_rows(left, right):
        return lax.dot_general(left, right, (((0,), (0,)), ((), ())), preferred_element_type=F32)

    first_pre[...] = dot(x_window(0, 0), w1[0].reshape(256, 512))

    def conv_one(t, _):
        first_pre[...] += dot(x_window(lax.div(t, 3), lax.rem(t, 3)), w1[t].reshape(256, 512))
        return 0

    lax.fori_loop(1, 9, conv_one, 0)
    proj_pre[...] = dot(x_window(1, 1), w1[9].reshape(256, 512))
    first_big, first_small = moments(first_pre)
    side_big, side_small = moments(proj_pre)
    copies = reduce_start(0, first_big + first_small + side_big + side_small)
    far_two = gather_forward(w2, near_two)
    copies = reduce_middle(0, copies)
    last_two = gather_last(w2, far_two)
    sums = reduce_end(0, copies)

    def centered(total, square, number):
        center = total / number
        return center, lax.rsqrt(square / number - center * center + NORM_EPS)

    numbers = (number_big, number_small)
    first_stat = [centered(sums[2 * g], sums[2 * g + 1], numbers[g]) for g in range(2)]
    side_stat = [centered(sums[4 + 2 * g], sums[5 + 2 * g], numbers[g]) for g in range(2)]

    def place(group, i, value, big, small, shift):
        if group == 0:
            big[i + shift, shift : shift + ob] = value.reshape(ob, nb_img, 512)
        else:
            small[i + shift, shift : shift + os_] = value.reshape(os_, ns_img, 512)

    def hide(group, i, rows, carry):
        center, factor = first_stat[group]
        shaped = (first_pre[rows, :] - center) * factor * gains[0] + gains[1]
        place(group, i, (shaped * jax.nn.sigmoid(shaped)).astype(BF16), h_big, h_small, 1)
        return carry

    over_groups(hide, 0)

    finish(last_two)

    def h_window(ta, tb):
        return both(h_big[pl.ds(ta, ob), pl.ds(tb, ob)], h_small[pl.ds(ta, os_), pl.ds(tb, os_)])

    second_pre[...] = dot(h_window(0, 0), w2[0].reshape(512, 512))

    def conv_two(t, _):
        second_pre[...] += dot(h_window(lax.div(t, 3), lax.rem(t, 3)), w2[t].reshape(512, 512))
        return 0

    lax.fori_loop(1, 9, conv_two, 0)
    second_big, second_small = moments(second_pre)
    copies = reduce_start(1, second_big + second_small)
    finish(slope_copies)
    copies = reduce_middle(1, copies)
    sums = reduce_end(1, copies)
    second_stat = [centered(sums[2 * g], sums[2 * g + 1], numbers[g]) for g in range(2)]

    def normed(ref, stat, rows):
        return (ref[rows, :] - stat[0]) * stat[1]

    def outer(group, i, rows, carry):
        two = normed(second_pre, second_stat[group], rows)
        side = normed(proj_pre, side_stat[group], rows)
        summed = two * gains[2] + gains[3] + side * gains[4] + gains[5]
        gate = jax.nn.sigmoid(summed)
        place(group, i, (summed * gate).astype(BF16), os_big, os_small, 0)
        slope = sl_big[i] if group == 0 else sl_small[i]
        slope = slope.astype(F32).reshape(two.shape)
        upstream = slope * (gate * (1.0 + summed * (1.0 - gate)))
        work[rows, :] = upstream
        return (carry[0] + fold(upstream), carry[1] + fold(upstream * two), carry[2] + fold(upstream * side))

    outer_big, outer_small = over_groups(outer, 3)
    copies = reduce_start(2, outer_big + outer_small)
    stores = []
    for d in (1, 2, 3):
        to = lax.rem(z + d, 4)
        for staged, target, images in ((os_big, out_big, nb_img), (os_small, out_small, ns_img)):
            send(
                staged.at[:, :, :, lanes(to)],
                target.at[:, :, pl.ds(pl.multiple_of(z * images, images), images)],
                (b, to),
            )
            stores.append(started[-1])
    for staged, target, images in ((os_big, out_big, nb_img), (os_small, out_small, ns_img)):
        load(
            staged.at[:, :, :, mine],
            target.at[:, :, pl.ds(pl.multiple_of(z * images, images), images)],
        )
    copies = reduce_middle(2, copies)
    sums_outer = reduce_end(2, copies)

    def slopes(group, i, rows, carry):
        total, cross_two, cross_side = sums_outer[3 * group : 3 * group + 3]
        number = numbers[group]
        two = normed(second_pre, second_stat[group], rows)
        side = normed(proj_pre, side_stat[group], rows)
        base = work[rows, :] - total / number
        slope_two = gains[2] * second_stat[group][1] * (base - two * (cross_two / number))
        slope_side = gains[4] * side_stat[group][1] * (base - side * (cross_side / number))
        place(group, i, slope_two.astype(BF16), t_big, t_small, 1)
        place(group, i, slope_side.astype(BF16), p_big, p_small, 0)
        return carry

    over_groups(slopes, 0)

    def scatter_core(a, r, lo, n):
        part = pl.ds(lo, n)
        return send(a.at[part, :, :, 1 - core], r.at[part], sibling)

    def scatter_near(a, r, rx, ry, lo, n, copy):
        copy.wait_recv()
        part = pl.ds(lo, n)

        def add(t, _):
            r[t] = (r[t].astype(F32) + a[t, :, :, core].astype(F32)).astype(BF16)
            return 0

        lax.fori_loop(lo, lo + n, add, 0)
        return (
            send(r.at[part, :, 1 - x, :, pl.ds(0, 256)], rx.at[part], x_peer),
            send(r.at[part, 1 - y, :, :, pl.ds(256, 256)], ry.at[part], y_peer),
        )

    def scatter_far(r, rx, ry, rxx, ryy, lo, n, copies):
        finish(copies)
        part = pl.ds(lo, n)

        def add(t, _):
            rx[t] = (rx[t].astype(F32) + r[t, :, x, :, 0:256].astype(F32)).astype(BF16)
            ry[t] = (ry[t].astype(F32) + r[t, y, :, :, 256:512].astype(F32)).astype(BF16)
            return 0

        lax.fori_loop(lo, lo + n, add, 0)
        return (
            send(rx.at[part, 1 - y], ryy.at[part], y_peer),
            send(ry.at[part, 1 - x], rxx.at[part], x_peer),
        )

    def scatter_z(rx, ry, rxx, ryy, c, rz, lo, n, copies):
        finish(copies)
        part = pl.ds(lo, n)

        def add(t, _):
            c[t, :, 0:256] = (rx[t, y].astype(F32) + ryy[t].astype(F32)).astype(BF16)
            c[t, :, 256:512] = (ry[t, x].astype(F32) + rxx[t].astype(F32)).astype(BF16)
            return 0

        lax.fori_loop(lo, lo + n, add, 0)
        return [
            send(c.at[part, :, lanes(lax.rem(z + d, 4))], rz.at[d - 1, part], (b, lax.rem(z + d, 4)))
            for d in (1, 2, 3)
        ]

    def scatter_end(c, rz, out, lo, n, copies):
        finish(copies)

        def add(t, _):
            total = c[t, :, mine].astype(F32)
            for d in range(3):
                total = total + rz[d, t].astype(F32)
            out[t] = total
            return 0

        lax.fori_loop(lo, lo + n, add, 0)

    t_flat = lambda: both(t_big[1 : ob + 1, 1 : ob + 1], t_small[1 : os_ + 1, 1 : os_ + 1])

    def grad_two_taps(lo, n):
        def tap(t, _):
            d = dot_rows(h_window(lax.div(t, 3), lax.rem(t, 3)), t_flat())
            a2[t] = d.astype(BF16).reshape(a2.shape[1:])
            return 0

        lax.fori_loop(lo, lo + n, tap, 0)

    grad_two_taps(0, 3)
    core_a = scatter_core(a2, r2, 0, 3)
    grad_two_taps(3, 3)
    core_b = scatter_core(a2, r2, 3, 3)
    near_a = scatter_near(a2, r2, rx2, ry2, 0, 3, core_a)
    grad_two_taps(6, 3)
    core_c = scatter_core(a2, r2, 6, 3)
    near_b = scatter_near(a2, r2, rx2, ry2, 3, 3, core_b)

    def t_window(ta, tb):
        return both(
            t_big[pl.ds(2 - ta, ob), pl.ds(2 - tb, ob)],
            t_small[pl.ds(2 - ta, os_), pl.ds(2 - tb, os_)],
        )

    work[...] = dot_t(t_window(0, 0), w2[0].reshape(512, 512))

    def back_two(t, _):
        work[...] += dot_t(t_window(lax.div(t, 3), lax.rem(t, 3)), w2[t].reshape(512, 512))
        return 0

    lax.fori_loop(1, 3, back_two, 0)
    near_c = scatter_near(a2, r2, rx2, ry2, 6, 3, core_c)
    lax.fori_loop(3, 9, back_two, 0)

    def inner(group, i, rows, carry):
        value = normed(first_pre, first_stat[group], rows)
        e = work[rows, :] * silu_slope(value * gains[0] + gains[1])
        work[rows, :] = e
        return (carry[0] + fold(e), carry[1] + fold(e * value))

    inner_big, inner_small = over_groups(inner, 2)
    copies = reduce_start(3, inner_big + inner_small)
    far_a = scatter_far(r2, rx2, ry2, rxx2, ryy2, 0, 3, near_a)
    copies = reduce_middle(3, copies)
    sums_inner = reduce_end(3, copies)

    def slopes_one(group, i, rows, carry):
        total, cross = sums_inner[2 * group : 2 * group + 2]
        number = numbers[group]
        value = normed(first_pre, first_stat[group], rows)
        slope = gains[0] * first_stat[group][1] * (work[rows, :] - total / number - value * (cross / number))
        place(group, i, slope.astype(BF16), s_big, s_small, 0)
        return carry

    over_groups(slopes_one, 0)

    s_flat = lambda: both(s_big[0:ob, 0:ob], s_small[0:os_, 0:os_])
    p_flat = lambda: both(p_big[...], p_small[...])

    def grad_one_taps(lo, n):
        def tap(t, _):
            d = dot_rows(x_window(lax.div(t, 3), lax.rem(t, 3)), s_flat())
            a1[t] = d.astype(BF16).reshape(a1.shape[1:])
            return 0

        lax.fori_loop(lo, lo + n, tap, 0)

    grad_one_taps(0, 5)
    core_d = scatter_core(a1, r1, 0, 5)
    grad_one_taps(5, 4)
    a1[9] = dot_rows(x_window(1, 1), p_flat()).astype(BF16).reshape(a1.shape[1:])
    core_e = scatter_core(a1, r1, 5, 5)
    near_d = scatter_near(a1, r1, rx1, ry1, 0, 5, core_d)
    near_e = scatter_near(a1, r1, rx1, ry1, 5, 5, core_e)

    def s_window(sa, sb):
        return both(s_big[sa : sa + ob, sb : sb + ob], s_small[sa : sa + os_, sb : sb + os_])

    def back_one(hp, wp):
        total = dot_t(p_flat(), w1[9].reshape(256, 512)) if hp + wp == 0 else None
        for ta in ((1,), (2, 0))[hp]:
            for tb in ((1,), (2, 0))[wp]:
                term = dot_t(
                    s_window(int(ta == 0), int(tb == 0)), w1[3 * ta + tb].reshape(256, 512)
                )
                total = term if total is None else total + term
        total = total.astype(BF16)
        grad_big[:, hp, :, wp] = total[:rows_b].reshape(ob, ob, nb_img, 256)
        grad_small[:, hp, :, wp] = total[rows_b:].reshape(os_, os_, ns_img, 256)

    back_one(0, 0)
    back_one(0, 1)
    far_b = scatter_far(r2, rx2, ry2, rxx2, ryy2, 3, 3, near_b)
    z_a = scatter_z(rx2, ry2, rxx2, ryy2, c2, rz2, 0, 3, far_a)
    back_one(1, 0)
    back_one(1, 1)

    rows = [
        sums_inner[1] + sums_inner[3],
        sums_inner[0] + sums_inner[2],
        sums_outer[1] + sums_outer[4],
        sums_outer[0] + sums_outer[3],
        sums_outer[2] + sums_outer[5],
        sums_outer[0] + sums_outer[3],
    ]
    for r, row in enumerate(rows):
        norm_rows[r : r + 1, :] = row
    grad_norms[...] = norm_rows[0:6, mine]

    far_c = scatter_far(r2, rx2, ry2, rxx2, ryy2, 6, 3, near_c)
    z_b = scatter_z(rx2, ry2, rxx2, ryy2, c2, rz2, 3, 3, far_b)
    far_d = scatter_far(r1, rx1, ry1, rxx1, ryy1, 0, 5, near_d)
    z_c = scatter_z(rx2, ry2, rxx2, ryy2, c2, rz2, 6, 3, far_c)
    far_e = scatter_far(r1, rx1, ry1, rxx1, ryy1, 5, 5, near_e)
    z_d = scatter_z(rx1, ry1, rxx1, ryy1, c1, rz1, 0, 5, far_d)
    scatter_end(c2, rz2, grad_two, 0, 3, z_a)
    scatter_end(c2, rz2, grad_two, 3, 3, z_b)
    z_e = scatter_z(rx1, ry1, rxx1, ryy1, c1, rz1, 5, 5, far_e)
    scatter_end(c2, rz2, grad_two, 6, 3, z_c)
    scatter_end(c1, rz1, grad_one, 0, 5, z_d)
    scatter_end(c1, rz1, grad_one, 5, 5, z_e)
    finish(stores)
    for copy in loads[10:]:
        copy.wait()
    for copy in started:
        copy.wait_send()
    assert used[0] <= COPIES


def tap_window(padded, tap_row, tap_col, stride, size_out):
    reach = stride * (size_out - 1) + 1
    return lax.slice(
        padded,
        (0, tap_row, tap_col, 0),
        (padded.shape[0], tap_row + reach, tap_col + reach, padded.shape[3]),
        (1, stride, stride, 1),
    )


def conv_taps(inputs, kernel, stride):
    size_out = (inputs.shape[1] - 1) // stride + 1
    padded = jnp.pad(inputs, ((0, 0), (1, 1), (1, 1), (0, 0)))
    summed = jnp.zeros((inputs.shape[0], size_out, size_out, kernel.shape[3]), jnp.float32)
    for tap_row in range(3):
        for tap_col in range(3):
            window = tap_window(padded, tap_row, tap_col, stride, size_out)
            summed = summed + jnp.einsum(
                "nhwc,co->nhwo",
                window,
                kernel[tap_row, tap_col],
                preferred_element_type=jnp.float32,
            )
    return summed


def kernel_grad(inputs, slope, stride):
    size_out = slope.shape[1]
    padded = jnp.pad(inputs, ((0, 0), (1, 1), (1, 1), (0, 0)))
    tap_rows = []
    for tap_row in range(3):
        across = []
        for tap_col in range(3):
            window = tap_window(padded, tap_row, tap_col, stride, size_out)
            across.append(
                jnp.einsum("nhwc,nhwo->co", window, slope, preferred_element_type=jnp.float32)
            )
        tap_rows.append(jnp.stack(across))
    return jnp.stack(tap_rows)


def input_grad(slope, kernel, stride, size_in):
    size_out = slope.shape[1]
    full_size = size_in + 2
    reach = stride * (size_out - 1) + 1
    summed = jnp.zeros((slope.shape[0], full_size, full_size, kernel.shape[2]), jnp.float32)
    for tap_row in range(3):
        for tap_col in range(3):
            term = jnp.einsum(
                "nhwo,co->nhwc", slope, kernel[tap_row, tap_col], preferred_element_type=jnp.float32
            )
            summed = summed + lax.pad(
                term,
                jnp.float32(0.0),
                (
                    (0, 0, 0),
                    (tap_row, full_size - tap_row - reach, stride - 1),
                    (tap_col, full_size - tap_col - reach, stride - 1),
                    (0, 0, 0),
                ),
            )
    return summed[:, 1:-1, 1:-1, :]


def proj_input_grad(slope, kernel, size_in):
    term = jnp.einsum("nhwo,co->nhwc", slope, kernel, preferred_element_type=jnp.float32)
    margin = size_in - 2 * slope.shape[1] + 1
    return lax.pad(term, jnp.float32(0.0), ((0, 0, 0), (0, margin, 1), (0, margin, 1), (0, 0, 0)))


def moments(values):
    return (jnp.sum(values, axis=(0, 1, 2)), jnp.sum(values * values, axis=(0, 1, 2)))


def normalize(values, total, square_total, number):
    center = total / number
    factor = lax.rsqrt(square_total / number - center * center + NORM_EPS)
    return ((values - center) * factor, factor)


def norm_back(upstream, normed, factor, gain, total, cross, number):
    return gain * factor * (upstream - total / number - normed * (cross / number))


def plain_body(
    image_big,
    image_small,
    slope_big,
    slope_small,
    conv1_weight,
    conv2_weight,
    proj_weight,
    norm_params,
    first_conv1,
    first_conv2,
    first_proj,
    first_norms,
    second_conv1,
    second_conv2,
    second_proj,
    second_norms,
):
    bfloat = jnp.bfloat16
    kernel_one, kernel_two, kernel_proj = (
        lax.all_gather(conv1_weight.astype(bfloat), "batch", axis=2, tiled=True),
        lax.all_gather(conv2_weight.astype(bfloat), "batch", axis=2, tiled=True),
        lax.all_gather(proj_weight.astype(bfloat), "batch", axis=0, tiled=True),
    )
    inputs_big, inputs_small = (
        lax.all_gather(image_big, "chan", axis=0, tiled=True),
        lax.all_gather(image_small, "chan", axis=0, tiled=True),
    )
    groups = (inputs_big, inputs_small)
    batch_width = lax.axis_size("batch")
    first_pre = [conv_taps(images, kernel_one, 2) for images in groups]
    numbers = [
        values.shape[0] * values.shape[1] * values.shape[2] * batch_width for values in first_pre
    ]
    sum_big, square_big = moments(first_pre[0])
    sum_small, square_small = moments(first_pre[1])
    sum_big, square_big, sum_small, square_small = lax.psum(
        (sum_big, square_big, sum_small, square_small), "batch"
    )
    first_norm = [
        normalize(first_pre[0], sum_big, square_big, numbers[0]),
        normalize(first_pre[1], sum_small, square_small, numbers[1]),
    ]
    shaped = [normed * norm_params[0] + norm_params[1] for normed, factor in first_norm]
    hidden = [jax.nn.silu(values).astype(bfloat) for values in shaped]
    hidden_big, hidden_small = (
        lax.all_gather(hidden[0], "chan", axis=3, tiled=True),
        lax.all_gather(hidden[1], "chan", axis=3, tiled=True),
    )
    hidden_full = (hidden_big, hidden_small)
    second_pre = [conv_taps(values, kernel_two, 1) for values in hidden_full]
    proj_pre = [
        jnp.einsum(
            "nhwc,co->nhwo", images[:, ::2, ::2, :], kernel_proj, preferred_element_type=jnp.float32
        )
        for images in groups
    ]
    two_big, two_sq_big = moments(second_pre[0])
    two_small, two_sq_small = moments(second_pre[1])
    side_big, side_sq_big = moments(proj_pre[0])
    side_small, side_sq_small = moments(proj_pre[1])
    (
        two_big,
        two_sq_big,
        two_small,
        two_sq_small,
        side_big,
        side_sq_big,
        side_small,
        side_sq_small,
    ) = lax.psum(
        (
            two_big,
            two_sq_big,
            two_small,
            two_sq_small,
            side_big,
            side_sq_big,
            side_small,
            side_sq_small,
        ),
        "batch",
    )
    second_norm = [
        normalize(second_pre[0], two_big, two_sq_big, numbers[0]),
        normalize(second_pre[1], two_small, two_sq_small, numbers[1]),
    ]
    proj_norm = [
        normalize(proj_pre[0], side_big, side_sq_big, numbers[0]),
        normalize(proj_pre[1], side_small, side_sq_small, numbers[1]),
    ]
    summed = [
        second_norm[which][0] * norm_params[2]
        + norm_params[3]
        + proj_norm[which][0] * norm_params[4]
        + norm_params[5]
        for which in range(2)
    ]
    out_big = jax.nn.silu(summed[0]).astype(bfloat)
    out_small = jax.nn.silu(summed[1]).astype(bfloat)
    slopes = (slope_big, slope_small)
    upstream = [slopes[which].astype(jnp.float32) * silu_slope(summed[which]) for which in range(2)]
    outer_big = jnp.sum(upstream[0], axis=(0, 1, 2))
    cross_two_big = jnp.sum(upstream[0] * second_norm[0][0], axis=(0, 1, 2))
    cross_side_big = jnp.sum(upstream[0] * proj_norm[0][0], axis=(0, 1, 2))
    outer_small = jnp.sum(upstream[1], axis=(0, 1, 2))
    cross_two_small = jnp.sum(upstream[1] * second_norm[1][0], axis=(0, 1, 2))
    cross_side_small = jnp.sum(upstream[1] * proj_norm[1][0], axis=(0, 1, 2))
    outer_big, cross_two_big, cross_side_big, outer_small, cross_two_small, cross_side_small = (
        lax.psum(
            (
                outer_big,
                cross_two_big,
                cross_side_big,
                outer_small,
                cross_two_small,
                cross_side_small,
            ),
            "batch",
        )
    )
    outer_sums = (outer_big, outer_small)
    cross_two = (cross_two_big, cross_two_small)
    cross_side = (cross_side_big, cross_side_small)
    slope_two = [
        norm_back(
            upstream[which],
            second_norm[which][0],
            second_norm[which][1],
            norm_params[2],
            outer_sums[which],
            cross_two[which],
            numbers[which],
        ).astype(bfloat)
        for which in range(2)
    ]
    slope_proj = [
        norm_back(
            upstream[which],
            proj_norm[which][0],
            proj_norm[which][1],
            norm_params[4],
            outer_sums[which],
            cross_side[which],
            numbers[which],
        ).astype(bfloat)
        for which in range(2)
    ]
    part_big = input_grad(slope_two[0], kernel_two, 1, hidden_big.shape[1])
    part_small = input_grad(slope_two[1], kernel_two, 1, hidden_small.shape[1])
    back_big, back_small = (
        lax.psum_scatter(part_big, "chan", scatter_dimension=3, tiled=True),
        lax.psum_scatter(part_small, "chan", scatter_dimension=3, tiled=True),
    )
    inner = [back_big * silu_slope(shaped[0]), back_small * silu_slope(shaped[1])]
    inner_big = jnp.sum(inner[0], axis=(0, 1, 2))
    cross_one_big = jnp.sum(inner[0] * first_norm[0][0], axis=(0, 1, 2))
    inner_small = jnp.sum(inner[1], axis=(0, 1, 2))
    cross_one_small = jnp.sum(inner[1] * first_norm[1][0], axis=(0, 1, 2))
    inner_big, cross_one_big, inner_small, cross_one_small = lax.psum(
        (inner_big, cross_one_big, inner_small, cross_one_small), "batch"
    )
    inner_sums = (inner_big, inner_small)
    cross_one = (cross_one_big, cross_one_small)
    slope_one = [
        norm_back(
            inner[which],
            first_norm[which][0],
            first_norm[which][1],
            norm_params[0],
            inner_sums[which],
            cross_one[which],
            numbers[which],
        ).astype(bfloat)
        for which in range(2)
    ]
    size_big = image_big.shape[1]
    size_small = image_small.shape[1]
    input_part_big = input_grad(slope_one[0], kernel_one, 2, size_big) + proj_input_grad(
        slope_proj[0], kernel_proj, size_big
    )
    input_part_small = input_grad(slope_one[1], kernel_one, 2, size_small) + proj_input_grad(
        slope_proj[1], kernel_proj, size_small
    )
    grad_big, grad_small = (
        lax.psum_scatter(input_part_big, "chan", scatter_dimension=0, tiled=True),
        lax.psum_scatter(input_part_small, "chan", scatter_dimension=0, tiled=True),
    )
    part_conv1 = kernel_grad(groups[0], slope_one[0], 2) + kernel_grad(groups[1], slope_one[1], 2)
    part_conv2 = kernel_grad(hidden_full[0], slope_two[0], 1) + kernel_grad(
        hidden_full[1], slope_two[1], 1
    )
    part_proj = jnp.einsum(
        "nhwc,nhwo->co",
        groups[0][:, ::2, ::2, :],
        slope_proj[0],
        preferred_element_type=jnp.float32,
    ) + jnp.einsum(
        "nhwc,nhwo->co",
        groups[1][:, ::2, ::2, :],
        slope_proj[1],
        preferred_element_type=jnp.float32,
    )
    grad_conv1, grad_conv2, grad_proj = (
        lax.psum_scatter(part_conv1, "batch", scatter_dimension=2, tiled=True),
        lax.psum_scatter(part_conv2, "batch", scatter_dimension=2, tiled=True),
        lax.psum_scatter(part_proj, "batch", scatter_dimension=0, tiled=True),
    )
    grad_norms = jnp.stack(
        [
            cross_one_big + cross_one_small,
            inner_big + inner_small,
            cross_two_big + cross_two_small,
            outer_big + outer_small,
            cross_side_big + cross_side_small,
            outer_big + outer_small,
        ]
    )
    new_conv1, moment_conv1, square_conv1 = adamw_step(
        conv1_weight, grad_conv1, first_conv1, second_conv1, (9.0 * C_IN) ** (-0.5), DECAY
    )
    new_conv2, moment_conv2, square_conv2 = adamw_step(
        conv2_weight, grad_conv2, first_conv2, second_conv2, (9.0 * C_OUT) ** (-0.5), DECAY
    )
    new_proj, moment_proj, square_proj = adamw_step(
        proj_weight, grad_proj, first_proj, second_proj, (1.0 * C_IN) ** (-0.5), DECAY
    )
    new_norms, moment_norms, square_norms = adamw_step(
        norm_params, grad_norms, first_norms, second_norms, NORM_RATE, 0.0
    )
    return (
        out_big,
        out_small,
        grad_big.astype(bfloat),
        grad_small.astype(bfloat),
        grad_conv1,
        grad_conv2,
        grad_proj,
        grad_norms,
        new_conv1,
        new_conv2,
        new_proj,
        new_norms,
        moment_conv1,
        moment_conv2,
        moment_proj,
        moment_norms,
        square_conv1,
        square_conv2,
        square_proj,
        square_norms,
    )


def update_kernel(
    g1, g2, gn,
    w1, w2, wp, wn, f1, f2, fp, fn, s1, s2, sp, sn,
    *outs,
):
    shape = w1.shape
    grads = [
        (g1[0:9].reshape(shape), w1, f1, s1, (9.0 * C_IN) ** (-0.5), DECAY),
        (g2[...].reshape(w2.shape), w2, f2, s2, (9.0 * C_OUT) ** (-0.5), DECAY),
        (g1[9], wp, fp, sp, (1.0 * C_IN) ** (-0.5), DECAY),
        (gn[...], wn, fn, sn, NORM_RATE, 0.0),
    ]
    for i, (gradient, weight, first, second, rate, decay) in enumerate(grads):
        new, moment, square = adamw_step(weight[...], gradient, first[...], second[...], rate, decay)
        outs[i][...] = gradient
        outs[4 + i][...] = new
        outs[8 + i][...] = moment
        outs[12 + i][...] = square


def fused_body(
    devices,
    image_big, image_small, slope_big, slope_small,
    conv1_weight, conv2_weight, proj_weight, norm_params,
    first_conv1, first_conv2, first_proj, first_norms,
    second_conv1, second_conv2, second_proj, second_norms,
):
    nb_img, side_b = image_big.shape[0], image_big.shape[1]
    ns_img, side_s = image_small.shape[0], image_small.shape[1]
    ob, os_ = side_b // 2, side_s // 2
    rows = ob * ob * nb_img + os_ * os_ * ns_img
    cfg = (nb_img, ns_img, ob, os_, ob * ob * nb_img * devices, os_ * os_ * ns_img * devices)
    r1, r2 = conv1_weight.shape[2], conv2_weight.shape[2]

    def parity(images, side):
        images = jnp.transpose(images, (1, 2, 0, 3))
        return images.reshape(side // 2, 2, side // 2, 2, images.shape[2], C_IN)

    def flat(weight):
        return weight.reshape((9,) + weight.shape[2:])

    vmem = pl.BlockSpec(memory_space=pltpu.VMEM)
    anywhere = pl.BlockSpec(memory_space=pl.ANY)
    shape = jax.ShapeDtypeStruct
    out_shape = (
        shape((ob, ob, slope_big.shape[0], 128), BF16),
        shape((os_, os_, slope_small.shape[0], 128), BF16),
        shape((ob, 2, ob, 2, nb_img, C_IN), BF16),
        shape((os_, 2, os_, 2, ns_img, C_IN), BF16),
        shape((10, r1, 128), F32),
        shape((9, r2, 128), F32),
        shape((6, 128), F32),
    )

    def sum_buffers(taps, r):
        return [
            pltpu.VMEM((taps, 2, 2, 2, r, 512), BF16),
            pltpu.VMEM((taps, 2, 2, r, 512), BF16),
            pltpu.VMEM((taps, 2, r, 256), BF16),
            pltpu.VMEM((taps, 2, r, 256), BF16),
            pltpu.VMEM((taps, r, 256), BF16),
            pltpu.VMEM((taps, r, 256), BF16),
            pltpu.VMEM((taps, r, 512), BF16),
            pltpu.VMEM((3, taps, r, 128), BF16),
        ]

    def maps(extra):
        return [
            pltpu.VMEM((ob + extra, ob + extra, nb_img, 512), BF16),
            pltpu.VMEM((os_ + extra, os_ + extra, ns_img, 512), BF16),
        ]

    scratch = (
        [
            pltpu.VMEM((10, 2, 2, 2, r1, 512), BF16),
            pltpu.VMEM((9, 2, 2, 2, r2, 512), BF16),
            pltpu.VMEM((2, 2, ob + 1, ob + 1, nb_img, C_IN), BF16),
            pltpu.VMEM((2, 2, os_ + 1, os_ + 1, ns_img, C_IN), BF16),
        ]
        + maps(2)
        + [pltpu.VMEM((rows, 512), F32) for _ in range(4)]
        + maps(0)
        + maps(0)
        + maps(2)
        + maps(0)
        + maps(1)
        + [
            pltpu.VMEM((4, 8, 128), F32),
            pltpu.VMEM((8, 512), F32),
            pltpu.VMEM((4, 8, 8, 512), F32),
            pltpu.VMEM((4, 4, 8, 512), F32),
        ]
        + sum_buffers(10, r1)
        + sum_buffers(9, r2)
        + [
            pltpu.SemaphoreType.DMA((COPIES,)),
            pltpu.SemaphoreType.DMA((COPIES,)),
            pltpu.SemaphoreType.DMA((12,)),
        ]
    )
    macs = rows * 512 * (9 * C_IN + 9 * C_OUT + C_IN) * 3
    out_big, out_small, grad_big, grad_small, grad_one, grad_two, grad_norms = pl.pallas_call(
        functools.partial(block_kernel, cfg),
        out_shape=out_shape,
        in_specs=[anywhere] * 4 + [vmem] * 4,
        out_specs=[anywhere] * 2 + [vmem] * 5,
        scratch_shapes=scratch,
        compiler_params=pltpu.CompilerParams(
            collective_id=0, has_side_effects=True, vmem_limit_bytes=VMEM_BYTES
        ),
        cost_estimate=pl.CostEstimate(flops=2 * macs, bytes_accessed=1 << 23, transcendentals=rows * 2048),
    )(
        parity(image_big, side_b),
        parity(image_small, side_s),
        jnp.transpose(slope_big, (1, 2, 0, 3)),
        jnp.transpose(slope_small, (1, 2, 0, 3)),
        flat(conv1_weight),
        flat(conv2_weight),
        proj_weight,
        norm_params,
    )
    weights = (conv1_weight, conv2_weight, proj_weight, norm_params)
    updated = pl.pallas_call(
        update_kernel,
        out_shape=[shape(w.shape, F32) for w in weights] * 4,
        in_specs=[vmem] * 15,
        out_specs=[vmem] * 16,
        compiler_params=pltpu.CompilerParams(vmem_limit_bytes=32 << 20),
    )(
        grad_one, grad_two, grad_norms,
        *weights,
        first_conv1, first_conv2, first_proj, first_norms,
        second_conv1, second_conv2, second_proj, second_norms,
    )

    def unparity(images, side):
        images = images.reshape(side, side, images.shape[4], C_IN)
        return jnp.transpose(images, (2, 0, 1, 3))

    return (
        jnp.transpose(out_big, (2, 0, 1, 3)),
        jnp.transpose(out_small, (2, 0, 1, 3)),
        unparity(grad_big, side_b),
        unparity(grad_small, side_s),
        *updated,
    )


def solution(mesh):
    images = P(("batch", "chan"), None, None, None)
    maps = P("batch", None, None, "chan")
    convs = P(None, None, "batch", "chan")
    proj = P("batch", "chan")
    norms = P(None, "chan")
    states = (convs, convs, proj, norms)
    fused = mesh.shape["batch"] == 8 and mesh.shape["chan"] == 4
    return jax.shard_map(
        functools.partial(fused_body, 32) if fused else plain_body,
        mesh=mesh,
        in_specs=(images, images, maps, maps) + states * 3,
        out_specs=(maps, maps, images, images) + states * 4,
        check_vma=False,
    )
```

```python
import functools

import jax
import jax.numpy as jnp
from jax import lax
from jax.experimental import pallas as pl
from jax.experimental.pallas import tpu as pltpu
from jax.sharding import PartitionSpec as P

C_IN = 256
C_OUT = 512
STEP = 5
NORM_EPS = 1e-05
BETA_ONE = 0.5
BETA_TWO = 0.5
ADAM_EPS = 1e-08
DECAY = 0.01
NORM_RATE = 0.3
MESH = pl.DeviceIdType.MESH
BF16 = jnp.bfloat16
F32 = jnp.float32
COPIES = 176
VMEM_BYTES = 60 << 20


def silu_slope(values):
    gate = jax.nn.sigmoid(values)
    return gate * (1.0 + values * (1.0 - gate))


def adamw_step(weight, gradient, first, second, rate, decay):
    first_new = BETA_ONE * first + (1.0 - BETA_ONE) * gradient
    second_new = BETA_TWO * second + (1.0 - BETA_TWO) * gradient * gradient
    first_hat = first_new / (1.0 - BETA_ONE**STEP)
    second_hat = second_new / (1.0 - BETA_TWO**STEP)
    updated = weight - rate * (first_hat / (jnp.sqrt(second_hat) + ADAM_EPS) + decay * weight)
    return (updated, first_new, second_new)


def fold(values):
    rows, channels = values.shape
    return jnp.sum(values.reshape(rows // 8, 8, channels), axis=0)


def block_kernel(
    cfg,
    img_big, img_small, slo_big, slo_small, w1_in, w2_in, wp_in, norms_in,
    out_big, out_small, grad_big, grad_small, grad_one, grad_two, grad_norms,
    w1, w2, x_big, x_small, h_big, h_small, first_pre, second_pre, proj_pre, work,
    sl_big, sl_small, os_big, os_small, t_big, t_small, p_big, p_small, s_big, s_small,
    norms, norm_rows, stat_a, stat_b, a1, r1, rx1, ry1, rxx1, ryy1, c1, rz1,
    a2, r2, rx2, ry2, rxx2, ryy2, c2, rz2,
    send_sem, recv_sem, local_sem,
):
    nb_img, ns_img, ob, os_, number_big, number_small = cfg
    rows_b, rows_s = ob * ob * nb_img, os_ * os_ * ns_img
    step_b, step_s = ob * nb_img, os_ * ns_img
    b = lax.axis_index("batch")
    z = lax.axis_index("chan")
    core = lax.rem(b, 2)
    x = lax.rem(lax.div(b, 2), 2)
    y = lax.div(b, 4)
    x_peer = (b + 2 - 4 * x, z)
    y_peer = (b + 4 - 8 * y, z)
    sibling = (b + 1 - 2 * core, z)
    z_peers = [(b, lax.rem(z + d, 4)) for d in (1, 2, 3)]
    b_peers = [(lax.rem(b + d, 8), z) for d in range(1, 8)]
    lanes = lambda which: pl.ds(pl.multiple_of(which * 128, 128), 128)
    mine = lanes(z)

    used = [0]
    started = []

    def send(src, dst, peer):
        slot = used[0]
        used[0] += 1
        copy = pltpu.make_async_remote_copy(
            src_ref=src,
            dst_ref=dst,
            send_sem=send_sem.at[slot],
            recv_sem=recv_sem.at[slot],
            device_id=peer,
            device_id_type=MESH,
        )
        copy.start()
        started.append(copy)
        return copy

    barrier = pltpu.get_barrier_semaphore()
    for peer in b_peers + z_peers:
        pl.semaphore_signal(barrier, inc=1, device_id=peer, device_id_type=MESH)

    loads = []

    def load(src, dst):
        copy = pltpu.make_async_copy(src, dst, local_sem.at[len(loads)])
        copy.start()
        loads.append(copy)

    for hp in range(2):
        for wp in range(2):
            load(img_big.at[:, hp, :, wp], x_big.at[hp, wp, pl.ds(hp, ob), pl.ds(wp, ob)])
            load(img_small.at[:, hp, :, wp], x_small.at[hp, wp, pl.ds(hp, os_), pl.ds(wp, os_)])
    load(
        slo_big.at[:, :, pl.ds(pl.multiple_of(z * nb_img, nb_img), nb_img)],
        sl_big.at[:, :, :, mine],
    )
    load(
        slo_small.at[:, :, pl.ds(pl.multiple_of(z * ns_img, ns_img), ns_img)],
        sl_small.at[:, :, :, mine],
    )
    w1[0:9, y, x, core, :, mine] = w1_in[...].astype(BF16)
    w1[9, y, x, core, :, mine] = wp_in[...].astype(BF16)
    w2[:, y, x, core, :, mine] = w2_in[...].astype(BF16)
    norms[z, 0:6] = norms_in[...]

    pl.semaphore_wait(barrier, 10)

    def finish(copies):
        for copy in copies:
            copy.wait_recv()

    class Gather:
        def __init__(self, w, lo, n):
            self.w, self.taps = w, pl.ds(lo, n)
            piece = w.at[self.taps, y, x, core, :, mine]
            self.over_z = [send(piece, piece, peer) for peer in z_peers]

        def near(self):
            finish(self.over_z)
            piece = self.w.at[self.taps, y, x, core]
            self.x_copy = send(piece, piece, x_peer)
            self.y_copy = send(piece, piece, y_peer)
            self.rest = [send(piece, piece, sibling)]

        def far(self):
            self.x_copy.wait_recv()
            part = self.w.at[self.taps, y, 1 - x, core, :, pl.ds(0, 256)]
            self.far_a = send(part, part, y_peer)
            self.y_copy.wait_recv()
            part = self.w.at[self.taps, 1 - y, x, core, :, pl.ds(256, 256)]
            self.far_b = send(part, part, x_peer)
            piece = self.w.at[self.taps, y, 1 - x, core]
            self.rest.append(send(piece, piece, sibling))
            piece = self.w.at[self.taps, 1 - y, x, core]
            self.rest.append(send(piece, piece, sibling))

        def last(self):
            finish([self.far_a, self.far_b])
            piece = self.w.at[self.taps, 1 - y, 1 - x, core]
            self.rest.append(send(piece, piece, sibling))

        def done(self):
            finish(self.rest)

    one_a = Gather(w1, 0, 5)
    z_norms = [send(norms.at[z], norms.at[z], peer) for peer in z_peers]
    one_b = Gather(w1, 5, 5)
    two_a, two_b, two_c = (Gather(w2, lo, 3) for lo in (0, 3, 6))

    zero = functools.partial(jnp.zeros, dtype=BF16)
    for wp in range(2):
        x_big[1, wp, 0] = zero((ob + 1, nb_img, 256))
        x_small[1, wp, 0] = zero((os_ + 1, ns_img, 256))
    for hp in range(2):
        x_big[hp, 1, :, 0] = zero((ob + 1, nb_img, 256))
        x_small[hp, 1, :, 0] = zero((os_ + 1, ns_img, 256))
    for ref, side, images in (
        (h_big, ob, nb_img), (t_big, ob, nb_img), (h_small, os_, ns_img), (t_small, os_, ns_img),
    ):
        ref[0] = zero((side + 2, images, 512))
        ref[side + 1] = zero((side + 2, images, 512))
        ref[:, 0] = zero((side + 2, images, 512))
        ref[:, side + 1] = zero((side + 2, images, 512))
    for ref, side, images in ((s_big, ob, nb_img), (s_small, os_, ns_img)):
        ref[side] = zero((side + 1, images, 512))
        ref[:, side] = zero((side + 1, images, 512))

    slope_copies = []

    def slopes_over_z(source, target, lo, n, images):
        for d in (1, 2, 3):
            to = lax.rem(z + d, 4)
            rows = pl.ds(pl.multiple_of(to * images, images), images)
            slope_copies.append(
                send(source.at[pl.ds(lo, n), :, rows], target.at[pl.ds(lo, n), :, :, mine], (b, to))
            )

    big_parts = ((0, 4), (4, ob - 4))
    one_a.near()
    one_b.near()
    one_a.far()
    one_b.far()
    two_a.near()
    two_b.near()
    slopes_over_z(slo_big, sl_big, *big_parts[0], nb_img)
    one_a.last()
    one_b.last()
    finish(z_norms)
    gains = [
        jnp.concatenate([norms[q, r : r + 1, :] for q in range(4)], axis=1) for r in range(6)
    ]
    for copy in loads:
        copy.wait()
    one_a.done()
    one_b.done()

    def reduce_start(k, rows):
        for r, row in enumerate(rows):
            stat_a[k, b, r : r + 1, :] = jnp.sum(row, axis=0, keepdims=True)
        part = stat_a.at[k, b, pl.ds(0, len(rows))]
        return [send(part, part, peer) for peer in b_peers]

    def reduce_middle(k, n, copies):
        finish(copies)
        stat_b[k, z, 0:n] = jnp.sum(stat_a[k, :, 0:n], axis=0)
        part = stat_b.at[k, z, pl.ds(0, n)]
        return [send(part, part, peer) for peer in z_peers]

    def reduce_end(k, n, copies):
        finish(copies)
        total = jnp.sum(stat_b[k, :, 0:n], axis=0)
        return [total[r : r + 1, :] for r in range(n)]

    def chunk_big(i):
        return pl.ds(pl.multiple_of(i * step_b, 16), step_b)

    def chunk_small(i):
        return pl.ds(pl.multiple_of(rows_b + i * step_s, 16), step_s)

    def over_groups(body, count):
        start = tuple(jnp.zeros((8, 512), F32) for _ in range(count))
        big = lax.fori_loop(0, ob, lambda i, c: body(0, i, chunk_big(i), c), start)
        small = lax.fori_loop(0, os_, lambda i, c: body(1, i, chunk_small(i), c), start)
        return big, small

    def moments(ref):
        def body(group, i, rows, carry):
            v = ref[rows, :]
            return (carry[0] + fold(v), carry[1] + fold(v * v))

        return over_groups(body, 2)

    def both(big, small):
        return jnp.concatenate([big.reshape(rows_b, -1), small.reshape(rows_s, -1)], axis=0)

    def x_window(ta, tb):
        half, odd = (lambda v: v // 2, lambda v: v % 2) if isinstance(ta, int) else (
            lambda v: lax.div(v, 2), lambda v: lax.rem(v, 2)
        )
        hp, wp, sa, sb = odd(ta + 1), odd(tb + 1), half(ta), half(tb)
        return both(
            x_big[hp, wp, pl.ds(sa, ob), pl.ds(sb, ob)],
            x_small[hp, wp, pl.ds(sa, os_), pl.ds(sb, os_)],
        )

    def dot(left, right):
        return jnp.dot(left, right, preferred_element_type=F32)

    def dot_t(left, right):
        return lax.dot_general(left, right, (((1,), (1,)), ((), ())), preferred_element_type=F32)

    def dot_rows(left, right):
        return lax.dot_general(left, right, (((0,), (0,)), ((), ())), preferred_element_type=F32)

    first_pre[...] = dot(x_window(0, 0), w1[0].reshape(256, 512))

    def conv_one(t, _):
        first_pre[...] += dot(x_window(lax.div(t, 3), lax.rem(t, 3)), w1[t].reshape(256, 512))
        return 0

    lax.fori_loop(1, 9, conv_one, 0)
    proj_pre[...] = dot(x_window(1, 1), w1[9].reshape(256, 512))
    first_big, first_small = moments(first_pre)
    side_big, side_small = moments(proj_pre)
    copies = reduce_start(0, first_big + first_small + side_big + side_small)
    two_c.near()
    two_a.far()
    copies = reduce_middle(0, 8, copies)
    slopes_over_z(slo_big, sl_big, *big_parts[1], nb_img)
    slopes_over_z(slo_small, sl_small, 0, os_, ns_img)
    two_b.far()
    sums = reduce_end(0, 8, copies)

    def centered(total, square, number):
        center = total / number
        return center, lax.rsqrt(square / number - center * center + NORM_EPS)

    numbers = (number_big, number_small)
    first_stat = [centered(sums[2 * g], sums[2 * g + 1], numbers[g]) for g in range(2)]
    side_stat = [centered(sums[4 + 2 * g], sums[5 + 2 * g], numbers[g]) for g in range(2)]

    def place(group, i, value, big, small, shift):
        if group == 0:
            big[i + shift, shift : shift + ob] = value.reshape(ob, nb_img, 512)
        else:
            small[i + shift, shift : shift + os_] = value.reshape(os_, ns_img, 512)

    def hide(group, i, rows, carry):
        center, factor = first_stat[group]
        shaped = (first_pre[rows, :] - center) * factor * gains[0] + gains[1]
        place(group, i, (shaped * jax.nn.sigmoid(shaped)).astype(BF16), h_big, h_small, 1)
        return carry

    over_groups(hide, 0)

    two_a.last()
    two_a.done()

    def h_window(ta, tb):
        return both(h_big[pl.ds(ta, ob), pl.ds(tb, ob)], h_small[pl.ds(ta, os_), pl.ds(tb, os_)])

    second_pre[...] = dot(h_window(0, 0), w2[0].reshape(512, 512))

    def conv_two(t, _):
        second_pre[...] += dot(h_window(lax.div(t, 3), lax.rem(t, 3)), w2[t].reshape(512, 512))
        return 0

    lax.fori_loop(1, 3, conv_two, 0)
    two_c.far()
    two_b.last()
    two_b.done()
    lax.fori_loop(3, 6, conv_two, 0)
    two_c.last()
    two_c.done()
    lax.fori_loop(6, 9, conv_two, 0)
    second_big, second_small = moments(second_pre)
    copies = reduce_start(1, second_big + second_small)
    finish(slope_copies)
    copies = reduce_middle(1, 4, copies)
    sums = reduce_end(1, 4, copies)
    second_stat = [centered(sums[2 * g], sums[2 * g + 1], numbers[g]) for g in range(2)]

    def normed(ref, stat, rows):
        return (ref[rows, :] - stat[0]) * stat[1]

    def outer(group, i, rows, carry):
        two = normed(second_pre, second_stat[group], rows)
        side = normed(proj_pre, side_stat[group], rows)
        summed = two * gains[2] + gains[3] + side * gains[4] + gains[5]
        gate = jax.nn.sigmoid(summed)
        place(group, i, (summed * gate).astype(BF16), os_big, os_small, 0)
        slope = sl_big[i] if group == 0 else sl_small[i]
        slope = slope.astype(F32).reshape(two.shape)
        upstream = slope * (gate * (1.0 + summed * (1.0 - gate)))
        work[rows, :] = upstream
        return (carry[0] + fold(upstream), carry[1] + fold(upstream * two), carry[2] + fold(upstream * side))

    outer_big, outer_small = over_groups(outer, 3)
    copies = reduce_start(2, outer_big + outer_small)
    stores = []

    def outputs_over_z(staged, target, lo, n, images):
        rows = pl.ds(pl.multiple_of(z * images, images), images)
        for d in (1, 2, 3):
            to = lax.rem(z + d, 4)
            stores.append(
                send(staged.at[pl.ds(lo, n), :, :, lanes(to)], target.at[pl.ds(lo, n), :, rows], (b, to))
            )

    copies = reduce_middle(2, 6, copies)
    outputs_over_z(os_small, out_small, 0, os_, ns_img)
    for staged, target, images in ((os_big, out_big, nb_img), (os_small, out_small, ns_img)):
        load(
            staged.at[:, :, :, mine],
            target.at[:, :, pl.ds(pl.multiple_of(z * images, images), images)],
        )
    sums_outer = reduce_end(2, 6, copies)

    def slopes(group, i, rows, carry):
        total, cross_two, cross_side = sums_outer[3 * group : 3 * group + 3]
        number = numbers[group]
        two = normed(second_pre, second_stat[group], rows)
        side = normed(proj_pre, side_stat[group], rows)
        base = work[rows, :] - total / number
        slope_two = gains[2] * second_stat[group][1] * (base - two * (cross_two / number))
        slope_side = gains[4] * side_stat[group][1] * (base - side * (cross_side / number))
        place(group, i, slope_two.astype(BF16), t_big, t_small, 1)
        place(group, i, slope_side.astype(BF16), p_big, p_small, 0)
        return carry

    over_groups(slopes, 0)

    def scatter_core(a, r, lo, n):
        part = pl.ds(lo, n)
        return send(a.at[part, :, :, 1 - core], r.at[part], sibling)

    def scatter_near(a, r, rx, ry, lo, n, copy):
        copy.wait_recv()
        part = pl.ds(lo, n)

        def add(t, _):
            r[t] = (r[t].astype(F32) + a[t, :, :, core].astype(F32)).astype(BF16)
            return 0

        lax.fori_loop(lo, lo + n, add, 0)
        return (
            send(r.at[part, :, 1 - x, :, pl.ds(0, 256)], rx.at[part], x_peer),
            send(r.at[part, 1 - y, :, :, pl.ds(256, 256)], ry.at[part], y_peer),
        )

    def scatter_far(r, rx, ry, rxx, ryy, lo, n, copies):
        finish(copies)
        part = pl.ds(lo, n)

        def add(t, _):
            rx[t] = (rx[t].astype(F32) + r[t, :, x, :, 0:256].astype(F32)).astype(BF16)
            ry[t] = (ry[t].astype(F32) + r[t, y, :, :, 256:512].astype(F32)).astype(BF16)
            return 0

        lax.fori_loop(lo, lo + n, add, 0)
        return (
            send(rx.at[part, 1 - y], ryy.at[part], y_peer),
            send(ry.at[part, 1 - x], rxx.at[part], x_peer),
        )

    def scatter_z(rx, ry, rxx, ryy, c, rz, lo, n, copies):
        finish(copies)
        part = pl.ds(lo, n)

        def add(t, _):
            c[t, :, 0:256] = (rx[t, y].astype(F32) + ryy[t].astype(F32)).astype(BF16)
            c[t, :, 256:512] = (ry[t, x].astype(F32) + rxx[t].astype(F32)).astype(BF16)
            return 0

        lax.fori_loop(lo, lo + n, add, 0)
        return [
            send(c.at[part, :, lanes(lax.rem(z + d, 4))], rz.at[d - 1, part], (b, lax.rem(z + d, 4)))
            for d in (1, 2, 3)
        ]

    def scatter_end(c, rz, out, lo, n, copies):
        finish(copies)

        def add(t, _):
            total = c[t, :, mine].astype(F32)
            for d in range(3):
                total = total + rz[d, t].astype(F32)
            out[t] = total
            return 0

        lax.fori_loop(lo, lo + n, add, 0)

    t_flat = lambda: both(t_big[1 : ob + 1, 1 : ob + 1], t_small[1 : os_ + 1, 1 : os_ + 1])

    def grad_two_taps(lo, n):
        def tap(t, _):
            d = dot_rows(h_window(lax.div(t, 3), lax.rem(t, 3)), t_flat())
            a2[t] = d.astype(BF16).reshape(a2.shape[1:])
            return 0

        lax.fori_loop(lo, lo + n, tap, 0)

    def t_window(ta, tb):
        return both(
            t_big[pl.ds(2 - ta, ob), pl.ds(2 - tb, ob)],
            t_small[pl.ds(2 - ta, os_), pl.ds(2 - tb, os_)],
        )

    def back_two(t, _):
        work[...] += dot_t(t_window(lax.div(t, 3), lax.rem(t, 3)), w2[t].reshape(512, 512))
        return 0

    grad_two_taps(0, 3)
    core_a = scatter_core(a2, r2, 0, 3)
    outputs_over_z(os_big, out_big, *big_parts[0], nb_img)
    grad_two_taps(3, 3)
    core_b = scatter_core(a2, r2, 3, 3)
    near_a = scatter_near(a2, r2, rx2, ry2, 0, 3, core_a)
    work[...] = dot_t(t_window(0, 0), w2[0].reshape(512, 512))
    lax.fori_loop(1, 3, back_two, 0)
    near_b = scatter_near(a2, r2, rx2, ry2, 3, 3, core_b)
    lax.fori_loop(3, 9, back_two, 0)

    def inner(group, i, rows, carry):
        value = normed(first_pre, first_stat[group], rows)
        e = work[rows, :] * silu_slope(value * gains[0] + gains[1])
        work[rows, :] = e
        return (carry[0] + fold(e), carry[1] + fold(e * value))

    inner_big, inner_small = over_groups(inner, 2)
    copies = reduce_start(3, inner_big + inner_small)
    far_a = scatter_far(r2, rx2, ry2, rxx2, ryy2, 0, 3, near_a)
    grad_two_taps(6, 3)
    core_c = scatter_core(a2, r2, 6, 3)
    copies = reduce_middle(3, 4, copies)
    near_c = scatter_near(a2, r2, rx2, ry2, 6, 3, core_c)
    far_b = scatter_far(r2, rx2, ry2, rxx2, ryy2, 3, 3, near_b)
    z_a = scatter_z(rx2, ry2, rxx2, ryy2, c2, rz2, 0, 3, far_a)
    sums_inner = reduce_end(3, 4, copies)

    def slopes_one(group, i, rows, carry):
        total, cross = sums_inner[2 * group : 2 * group + 2]
        number = numbers[group]
        value = normed(first_pre, first_stat[group], rows)
        slope = gains[0] * first_stat[group][1] * (work[rows, :] - total / number - value * (cross / number))
        place(group, i, slope.astype(BF16), s_big, s_small, 0)
        return carry

    over_groups(slopes_one, 0)

    s_flat = lambda: both(s_big[0:ob, 0:ob], s_small[0:os_, 0:os_])
    p_flat = lambda: both(p_big[...], p_small[...])

    def grad_one_taps(lo, n):
        def tap(t, _):
            d = dot_rows(x_window(lax.div(t, 3), lax.rem(t, 3)), s_flat())
            a1[t] = d.astype(BF16).reshape(a1.shape[1:])
            return 0

        lax.fori_loop(lo, lo + n, tap, 0)

    grad_one_taps(0, 5)
    core_d = scatter_core(a1, r1, 0, 5)
    grad_one_taps(5, 4)
    a1[9] = dot_rows(x_window(1, 1), p_flat()).astype(BF16).reshape(a1.shape[1:])
    core_e = scatter_core(a1, r1, 5, 5)
    near_d = scatter_near(a1, r1, rx1, ry1, 0, 5, core_d)
    near_e = scatter_near(a1, r1, rx1, ry1, 5, 5, core_e)
    z_b = scatter_z(rx2, ry2, rxx2, ryy2, c2, rz2, 3, 3, far_b)
    outputs_over_z(os_big, out_big, *big_parts[1], nb_img)

    def s_window(sa, sb):
        return both(s_big[sa : sa + ob, sb : sb + ob], s_small[sa : sa + os_, sb : sb + os_])

    def back_one(hp, wp):
        total = dot_t(p_flat(), w1[9].reshape(256, 512)) if hp + wp == 0 else None
        for ta in ((1,), (2, 0))[hp]:
            for tb in ((1,), (2, 0))[wp]:
                term = dot_t(
                    s_window(int(ta == 0), int(tb == 0)), w1[3 * ta + tb].reshape(256, 512)
                )
                total = term if total is None else total + term
        total = total.astype(BF16)
        grad_big[:, hp, :, wp] = total[:rows_b].reshape(ob, ob, nb_img, 256)
        grad_small[:, hp, :, wp] = total[rows_b:].reshape(os_, os_, ns_img, 256)

    back_one(0, 0)
    back_one(0, 1)
    far_c = scatter_far(r2, rx2, ry2, rxx2, ryy2, 6, 3, near_c)
    back_one(1, 0)
    far_d = scatter_far(r1, rx1, ry1, rxx1, ryy1, 0, 5, near_d)
    z_c = scatter_z(rx2, ry2, rxx2, ryy2, c2, rz2, 6, 3, far_c)
    back_one(1, 1)

    rows = [
        sums_inner[1] + sums_inner[3],
        sums_inner[0] + sums_inner[2],
        sums_outer[1] + sums_outer[4],
        sums_outer[0] + sums_outer[3],
        sums_outer[2] + sums_outer[5],
        sums_outer[0] + sums_outer[3],
    ]
    for r, row in enumerate(rows):
        norm_rows[r : r + 1, :] = row
    grad_norms[...] = norm_rows[0:6, mine]

    far_e = scatter_far(r1, rx1, ry1, rxx1, ryy1, 5, 5, near_e)
    z_d = scatter_z(rx1, ry1, rxx1, ryy1, c1, rz1, 0, 5, far_d)
    scatter_end(c2, rz2, grad_two, 0, 3, z_a)
    scatter_end(c2, rz2, grad_two, 3, 3, z_b)
    z_e = scatter_z(rx1, ry1, rxx1, ryy1, c1, rz1, 5, 5, far_e)
    scatter_end(c2, rz2, grad_two, 6, 3, z_c)
    scatter_end(c1, rz1, grad_one, 0, 5, z_d)
    scatter_end(c1, rz1, grad_one, 5, 5, z_e)
    finish(stores)
    for copy in loads[10:]:
        copy.wait()
    for copy in started:
        copy.wait_send()
    assert used[0] <= COPIES


def tap_window(padded, tap_row, tap_col, stride, size_out):
    reach = stride * (size_out - 1) + 1
    return lax.slice(
        padded,
        (0, tap_row, tap_col, 0),
        (padded.shape[0], tap_row + reach, tap_col + reach, padded.shape[3]),
        (1, stride, stride, 1),
    )


def conv_taps(inputs, kernel, stride):
    size_out = (inputs.shape[1] - 1) // stride + 1
    padded = jnp.pad(inputs, ((0, 0), (1, 1), (1, 1), (0, 0)))
    summed = jnp.zeros((inputs.shape[0], size_out, size_out, kernel.shape[3]), jnp.float32)
    for tap_row in range(3):
        for tap_col in range(3):
            window = tap_window(padded, tap_row, tap_col, stride, size_out)
            summed = summed + jnp.einsum(
                "nhwc,co->nhwo",
                window,
                kernel[tap_row, tap_col],
                preferred_element_type=jnp.float32,
            )
    return summed


def kernel_grad(inputs, slope, stride):
    size_out = slope.shape[1]
    padded = jnp.pad(inputs, ((0, 0), (1, 1), (1, 1), (0, 0)))
    tap_rows = []
    for tap_row in range(3):
        across = []
        for tap_col in range(3):
            window = tap_window(padded, tap_row, tap_col, stride, size_out)
            across.append(
                jnp.einsum("nhwc,nhwo->co", window, slope, preferred_element_type=jnp.float32)
            )
        tap_rows.append(jnp.stack(across))
    return jnp.stack(tap_rows)


def input_grad(slope, kernel, stride, size_in):
    size_out = slope.shape[1]
    full_size = size_in + 2
    reach = stride * (size_out - 1) + 1
    summed = jnp.zeros((slope.shape[0], full_size, full_size, kernel.shape[2]), jnp.float32)
    for tap_row in range(3):
        for tap_col in range(3):
            term = jnp.einsum(
                "nhwo,co->nhwc", slope, kernel[tap_row, tap_col], preferred_element_type=jnp.float32
            )
            summed = summed + lax.pad(
                term,
                jnp.float32(0.0),
                (
                    (0, 0, 0),
                    (tap_row, full_size - tap_row - reach, stride - 1),
                    (tap_col, full_size - tap_col - reach, stride - 1),
                    (0, 0, 0),
                ),
            )
    return summed[:, 1:-1, 1:-1, :]


def proj_input_grad(slope, kernel, size_in):
    term = jnp.einsum("nhwo,co->nhwc", slope, kernel, preferred_element_type=jnp.float32)
    margin = size_in - 2 * slope.shape[1] + 1
    return lax.pad(term, jnp.float32(0.0), ((0, 0, 0), (0, margin, 1), (0, margin, 1), (0, 0, 0)))


def moments(values):
    return (jnp.sum(values, axis=(0, 1, 2)), jnp.sum(values * values, axis=(0, 1, 2)))


def normalize(values, total, square_total, number):
    center = total / number
    factor = lax.rsqrt(square_total / number - center * center + NORM_EPS)
    return ((values - center) * factor, factor)


def norm_back(upstream, normed, factor, gain, total, cross, number):
    return gain * factor * (upstream - total / number - normed * (cross / number))


def plain_body(
    image_big,
    image_small,
    slope_big,
    slope_small,
    conv1_weight,
    conv2_weight,
    proj_weight,
    norm_params,
    first_conv1,
    first_conv2,
    first_proj,
    first_norms,
    second_conv1,
    second_conv2,
    second_proj,
    second_norms,
):
    bfloat = jnp.bfloat16
    kernel_one, kernel_two, kernel_proj = (
        lax.all_gather(conv1_weight.astype(bfloat), "batch", axis=2, tiled=True),
        lax.all_gather(conv2_weight.astype(bfloat), "batch", axis=2, tiled=True),
        lax.all_gather(proj_weight.astype(bfloat), "batch", axis=0, tiled=True),
    )
    inputs_big, inputs_small = (
        lax.all_gather(image_big, "chan", axis=0, tiled=True),
        lax.all_gather(image_small, "chan", axis=0, tiled=True),
    )
    groups = (inputs_big, inputs_small)
    batch_width = lax.axis_size("batch")
    first_pre = [conv_taps(images, kernel_one, 2) for images in groups]
    numbers = [
        values.shape[0] * values.shape[1] * values.shape[2] * batch_width for values in first_pre
    ]
    sum_big, square_big = moments(first_pre[0])
    sum_small, square_small = moments(first_pre[1])
    sum_big, square_big, sum_small, square_small = lax.psum(
        (sum_big, square_big, sum_small, square_small), "batch"
    )
    first_norm = [
        normalize(first_pre[0], sum_big, square_big, numbers[0]),
        normalize(first_pre[1], sum_small, square_small, numbers[1]),
    ]
    shaped = [normed * norm_params[0] + norm_params[1] for normed, factor in first_norm]
    hidden = [jax.nn.silu(values).astype(bfloat) for values in shaped]
    hidden_big, hidden_small = (
        lax.all_gather(hidden[0], "chan", axis=3, tiled=True),
        lax.all_gather(hidden[1], "chan", axis=3, tiled=True),
    )
    hidden_full = (hidden_big, hidden_small)
    second_pre = [conv_taps(values, kernel_two, 1) for values in hidden_full]
    proj_pre = [
        jnp.einsum(
            "nhwc,co->nhwo", images[:, ::2, ::2, :], kernel_proj, preferred_element_type=jnp.float32
        )
        for images in groups
    ]
    two_big, two_sq_big = moments(second_pre[0])
    two_small, two_sq_small = moments(second_pre[1])
    side_big, side_sq_big = moments(proj_pre[0])
    side_small, side_sq_small = moments(proj_pre[1])
    (
        two_big,
        two_sq_big,
        two_small,
        two_sq_small,
        side_big,
        side_sq_big,
        side_small,
        side_sq_small,
    ) = lax.psum(
        (
            two_big,
            two_sq_big,
            two_small,
            two_sq_small,
            side_big,
            side_sq_big,
            side_small,
            side_sq_small,
        ),
        "batch",
    )
    second_norm = [
        normalize(second_pre[0], two_big, two_sq_big, numbers[0]),
        normalize(second_pre[1], two_small, two_sq_small, numbers[1]),
    ]
    proj_norm = [
        normalize(proj_pre[0], side_big, side_sq_big, numbers[0]),
        normalize(proj_pre[1], side_small, side_sq_small, numbers[1]),
    ]
    summed = [
        second_norm[which][0] * norm_params[2]
        + norm_params[3]
        + proj_norm[which][0] * norm_params[4]
        + norm_params[5]
        for which in range(2)
    ]
    out_big = jax.nn.silu(summed[0]).astype(bfloat)
    out_small = jax.nn.silu(summed[1]).astype(bfloat)
    slopes = (slope_big, slope_small)
    upstream = [slopes[which].astype(jnp.float32) * silu_slope(summed[which]) for which in range(2)]
    outer_big = jnp.sum(upstream[0], axis=(0, 1, 2))
    cross_two_big = jnp.sum(upstream[0] * second_norm[0][0], axis=(0, 1, 2))
    cross_side_big = jnp.sum(upstream[0] * proj_norm[0][0], axis=(0, 1, 2))
    outer_small = jnp.sum(upstream[1], axis=(0, 1, 2))
    cross_two_small = jnp.sum(upstream[1] * second_norm[1][0], axis=(0, 1, 2))
    cross_side_small = jnp.sum(upstream[1] * proj_norm[1][0], axis=(0, 1, 2))
    outer_big, cross_two_big, cross_side_big, outer_small, cross_two_small, cross_side_small = (
        lax.psum(
            (
                outer_big,
                cross_two_big,
                cross_side_big,
                outer_small,
                cross_two_small,
                cross_side_small,
            ),
            "batch",
        )
    )
    outer_sums = (outer_big, outer_small)
    cross_two = (cross_two_big, cross_two_small)
    cross_side = (cross_side_big, cross_side_small)
    slope_two = [
        norm_back(
            upstream[which],
            second_norm[which][0],
            second_norm[which][1],
            norm_params[2],
            outer_sums[which],
            cross_two[which],
            numbers[which],
        ).astype(bfloat)
        for which in range(2)
    ]
    slope_proj = [
        norm_back(
            upstream[which],
            proj_norm[which][0],
            proj_norm[which][1],
            norm_params[4],
            outer_sums[which],
            cross_side[which],
            numbers[which],
        ).astype(bfloat)
        for which in range(2)
    ]
    part_big = input_grad(slope_two[0], kernel_two, 1, hidden_big.shape[1])
    part_small = input_grad(slope_two[1], kernel_two, 1, hidden_small.shape[1])
    back_big, back_small = (
        lax.psum_scatter(part_big, "chan", scatter_dimension=3, tiled=True),
        lax.psum_scatter(part_small, "chan", scatter_dimension=3, tiled=True),
    )
    inner = [back_big * silu_slope(shaped[0]), back_small * silu_slope(shaped[1])]
    inner_big = jnp.sum(inner[0], axis=(0, 1, 2))
    cross_one_big = jnp.sum(inner[0] * first_norm[0][0], axis=(0, 1, 2))
    inner_small = jnp.sum(inner[1], axis=(0, 1, 2))
    cross_one_small = jnp.sum(inner[1] * first_norm[1][0], axis=(0, 1, 2))
    inner_big, cross_one_big, inner_small, cross_one_small = lax.psum(
        (inner_big, cross_one_big, inner_small, cross_one_small), "batch"
    )
    inner_sums = (inner_big, inner_small)
    cross_one = (cross_one_big, cross_one_small)
    slope_one = [
        norm_back(
            inner[which],
            first_norm[which][0],
            first_norm[which][1],
            norm_params[0],
            inner_sums[which],
            cross_one[which],
            numbers[which],
        ).astype(bfloat)
        for which in range(2)
    ]
    size_big = image_big.shape[1]
    size_small = image_small.shape[1]
    input_part_big = input_grad(slope_one[0], kernel_one, 2, size_big) + proj_input_grad(
        slope_proj[0], kernel_proj, size_big
    )
    input_part_small = input_grad(slope_one[1], kernel_one, 2, size_small) + proj_input_grad(
        slope_proj[1], kernel_proj, size_small
    )
    grad_big, grad_small = (
        lax.psum_scatter(input_part_big, "chan", scatter_dimension=0, tiled=True),
        lax.psum_scatter(input_part_small, "chan", scatter_dimension=0, tiled=True),
    )
    part_conv1 = kernel_grad(groups[0], slope_one[0], 2) + kernel_grad(groups[1], slope_one[1], 2)
    part_conv2 = kernel_grad(hidden_full[0], slope_two[0], 1) + kernel_grad(
        hidden_full[1], slope_two[1], 1
    )
    part_proj = jnp.einsum(
        "nhwc,nhwo->co",
        groups[0][:, ::2, ::2, :],
        slope_proj[0],
        preferred_element_type=jnp.float32,
    ) + jnp.einsum(
        "nhwc,nhwo->co",
        groups[1][:, ::2, ::2, :],
        slope_proj[1],
        preferred_element_type=jnp.float32,
    )
    grad_conv1, grad_conv2, grad_proj = (
        lax.psum_scatter(part_conv1, "batch", scatter_dimension=2, tiled=True),
        lax.psum_scatter(part_conv2, "batch", scatter_dimension=2, tiled=True),
        lax.psum_scatter(part_proj, "batch", scatter_dimension=0, tiled=True),
    )
    grad_norms = jnp.stack(
        [
            cross_one_big + cross_one_small,
            inner_big + inner_small,
            cross_two_big + cross_two_small,
            outer_big + outer_small,
            cross_side_big + cross_side_small,
            outer_big + outer_small,
        ]
    )
    new_conv1, moment_conv1, square_conv1 = adamw_step(
        conv1_weight, grad_conv1, first_conv1, second_conv1, (9.0 * C_IN) ** (-0.5), DECAY
    )
    new_conv2, moment_conv2, square_conv2 = adamw_step(
        conv2_weight, grad_conv2, first_conv2, second_conv2, (9.0 * C_OUT) ** (-0.5), DECAY
    )
    new_proj, moment_proj, square_proj = adamw_step(
        proj_weight, grad_proj, first_proj, second_proj, (1.0 * C_IN) ** (-0.5), DECAY
    )
    new_norms, moment_norms, square_norms = adamw_step(
        norm_params, grad_norms, first_norms, second_norms, NORM_RATE, 0.0
    )
    return (
        out_big,
        out_small,
        grad_big.astype(bfloat),
        grad_small.astype(bfloat),
        grad_conv1,
        grad_conv2,
        grad_proj,
        grad_norms,
        new_conv1,
        new_conv2,
        new_proj,
        new_norms,
        moment_conv1,
        moment_conv2,
        moment_proj,
        moment_norms,
        square_conv1,
        square_conv2,
        square_proj,
        square_norms,
    )


def update_kernel(*refs):
    passed, sums, states, rest = refs[:4], refs[4:7], refs[7:19], refs[19:]
    passed_out, outs, (g1, g2, gn, sem) = rest[:4], rest[4:20], rest[20:]
    copies = [
        pltpu.make_async_copy(src, dst, sem.at[i])
        for i, (src, dst) in enumerate(zip(sums + passed, (g1, g2, gn) + passed_out))
    ]
    for copy in copies:
        copy.start()
    for copy in copies[:3]:
        copy.wait()
    w1, w2 = states[0], states[1]
    grads = (g1[0:9].reshape(w1.shape), g2[...].reshape(w2.shape), g1[9], gn[...])
    rates = ((9.0 * C_IN) ** (-0.5), (9.0 * C_OUT) ** (-0.5), (1.0 * C_IN) ** (-0.5), NORM_RATE)
    for i in range(4):
        weight, first, second = (states[i + 4 * k][...] for k in range(3))
        new, moment, square = adamw_step(
            weight, grads[i], first, second, rates[i], DECAY if i < 3 else 0.0
        )
        for k, value in enumerate((grads[i], new, moment, square)):
            outs[i + 4 * k][...] = value
    for copy in copies[3:]:
        copy.wait()


def fused_body(
    devices,
    image_big, image_small, slope_big, slope_small,
    conv1_weight, conv2_weight, proj_weight, norm_params,
    first_conv1, first_conv2, first_proj, first_norms,
    second_conv1, second_conv2, second_proj, second_norms,
):
    nb_img, side_b = image_big.shape[0], image_big.shape[1]
    ns_img, side_s = image_small.shape[0], image_small.shape[1]
    ob, os_ = side_b // 2, side_s // 2
    rows = ob * ob * nb_img + os_ * os_ * ns_img
    cfg = (nb_img, ns_img, ob, os_, ob * ob * nb_img * devices, os_ * os_ * ns_img * devices)
    r1, r2 = conv1_weight.shape[2], conv2_weight.shape[2]

    def parity(images, side):
        images = jnp.transpose(images, (1, 2, 0, 3))
        return images.reshape(side // 2, 2, side // 2, 2, images.shape[2], C_IN)

    def flat(weight):
        return weight.reshape((9,) + weight.shape[2:])

    vmem = pl.BlockSpec(memory_space=pltpu.VMEM)
    anywhere = pl.BlockSpec(memory_space=pl.ANY)
    shape = jax.ShapeDtypeStruct
    out_shape = (
        shape((ob, ob, slope_big.shape[0], 128), BF16),
        shape((os_, os_, slope_small.shape[0], 128), BF16),
        shape((ob, 2, ob, 2, nb_img, C_IN), BF16),
        shape((os_, 2, os_, 2, ns_img, C_IN), BF16),
        shape((10, r1, 128), F32),
        shape((9, r2, 128), F32),
        shape((6, 128), F32),
    )

    def sum_buffers(taps, r):
        return [
            pltpu.VMEM((taps, 2, 2, 2, r, 512), BF16),
            pltpu.VMEM((taps, 2, 2, r, 512), BF16),
            pltpu.VMEM((taps, 2, r, 256), BF16),
            pltpu.VMEM((taps, 2, r, 256), BF16),
            pltpu.VMEM((taps, r, 256), BF16),
            pltpu.VMEM((taps, r, 256), BF16),
            pltpu.VMEM((taps, r, 512), BF16),
            pltpu.VMEM((3, taps, r, 128), BF16),
        ]

    def maps(extra):
        return [
            pltpu.VMEM((ob + extra, ob + extra, nb_img, 512), BF16),
            pltpu.VMEM((os_ + extra, os_ + extra, ns_img, 512), BF16),
        ]

    scratch = (
        [
            pltpu.VMEM((10, 2, 2, 2, r1, 512), BF16),
            pltpu.VMEM((9, 2, 2, 2, r2, 512), BF16),
            pltpu.VMEM((2, 2, ob + 1, ob + 1, nb_img, C_IN), BF16),
            pltpu.VMEM((2, 2, os_ + 1, os_ + 1, ns_img, C_IN), BF16),
        ]
        + maps(2)
        + [pltpu.VMEM((rows, 512), F32) for _ in range(4)]
        + maps(0)
        + maps(0)
        + maps(2)
        + maps(0)
        + maps(1)
        + [
            pltpu.VMEM((4, 8, 128), F32),
            pltpu.VMEM((8, 512), F32),
            pltpu.VMEM((4, 8, 8, 512), F32),
            pltpu.VMEM((4, 4, 8, 512), F32),
        ]
        + sum_buffers(10, r1)
        + sum_buffers(9, r2)
        + [
            pltpu.SemaphoreType.DMA((COPIES,)),
            pltpu.SemaphoreType.DMA((COPIES,)),
            pltpu.SemaphoreType.DMA((12,)),
        ]
    )
    macs = rows * 512 * (9 * C_IN + 9 * C_OUT + C_IN) * 3
    out_big, out_small, grad_big, grad_small, grad_one, grad_two, grad_norms = pl.pallas_call(
        functools.partial(block_kernel, cfg),
        out_shape=out_shape,
        in_specs=[anywhere] * 4 + [vmem] * 4,
        out_specs=[anywhere] * 2 + [vmem] * 5,
        scratch_shapes=scratch,
        compiler_params=pltpu.CompilerParams(
            collective_id=0, has_side_effects=True, vmem_limit_bytes=VMEM_BYTES
        ),
        cost_estimate=pl.CostEstimate(flops=2 * macs, bytes_accessed=1 << 23, transcendentals=rows * 2048),
    )(
        parity(image_big, side_b),
        parity(image_small, side_s),
        jnp.transpose(slope_big, (1, 2, 0, 3)),
        jnp.transpose(slope_small, (1, 2, 0, 3)),
        flat(conv1_weight),
        flat(conv2_weight),
        proj_weight,
        norm_params,
    )
    weights = (conv1_weight, conv2_weight, proj_weight, norm_params)
    passed = (out_big, out_small, grad_big, grad_small)
    sums = (grad_one, grad_two, grad_norms)
    out_big, out_small, grad_big, grad_small, *updated = pl.pallas_call(
        update_kernel,
        out_shape=[shape(v.shape, v.dtype) for v in passed] + [shape(w.shape, F32) for w in weights] * 4,
        in_specs=[anywhere] * 7 + [vmem] * 12,
        out_specs=[anywhere] * 4 + [vmem] * 16,
        scratch_shapes=[pltpu.VMEM(v.shape, F32) for v in sums] + [pltpu.SemaphoreType.DMA((7,))],
        compiler_params=pltpu.CompilerParams(vmem_limit_bytes=32 << 20),
    )(
        *passed, *sums, *weights,
        first_conv1, first_conv2, first_proj, first_norms,
        second_conv1, second_conv2, second_proj, second_norms,
    )

    def unparity(images, side):
        images = images.reshape(side, side, images.shape[4], C_IN)
        return jnp.transpose(images, (2, 0, 1, 3))

    return (
        jnp.transpose(out_big, (2, 0, 1, 3)),
        jnp.transpose(out_small, (2, 0, 1, 3)),
        unparity(grad_big, side_b),
        unparity(grad_small, side_s),
        *updated,
    )


def solution(mesh):
    images = P(("batch", "chan"), None, None, None)
    maps = P("batch", None, None, "chan")
    convs = P(None, None, "batch", "chan")
    proj = P("batch", "chan")
    norms = P(None, "chan")
    states = (convs, convs, proj, norms)
    fused = mesh.shape["batch"] == 8 and mesh.shape["chan"] == 4
    return jax.shard_map(
        functools.partial(fused_body, 32) if fused else plain_body,
        mesh=mesh,
        in_specs=(images, images, maps, maps) + states * 3,
        out_specs=(maps, maps, images, images) + states * 4,
        check_vma=False,
    )
```

```python
import functools

import jax
import jax.numpy as jnp
from jax import lax
from jax.experimental import pallas as pl
from jax.experimental.pallas import tpu as pltpu
from jax.sharding import PartitionSpec as P

C_IN = 256
C_OUT = 512
STEP = 5
NORM_EPS = 1e-05
BETA_ONE = 0.5
BETA_TWO = 0.5
ADAM_EPS = 1e-08
DECAY = 0.01
NORM_RATE = 0.3
MESH = pl.DeviceIdType.MESH
BF16 = jnp.bfloat16
F32 = jnp.float32
COPIES = 192
VMEM_BYTES = 58 << 20


def silu_slope(values):
    gate = jax.nn.sigmoid(values)
    return gate * (1.0 + values * (1.0 - gate))


def adamw_step(weight, gradient, first, second, rate, decay):
    first_new = BETA_ONE * first + (1.0 - BETA_ONE) * gradient
    second_new = BETA_TWO * second + (1.0 - BETA_TWO) * gradient * gradient
    first_hat = first_new / (1.0 - BETA_ONE**STEP)
    second_hat = second_new / (1.0 - BETA_TWO**STEP)
    updated = weight - rate * (first_hat / (jnp.sqrt(second_hat) + ADAM_EPS) + decay * weight)
    return (updated, first_new, second_new)


def fold(values):
    rows, channels = values.shape
    return jnp.sum(values.reshape(rows // 8, 8, channels), axis=0)


def block_kernel(
    cfg,
    img_big, img_small, slo_big, slo_small, w1_hbm, w2_hbm, wp_hbm, norms_hbm,
    out_big, out_small, grad_big, grad_small, grad_one_out, grad_two_out, grad_norms,
    w1_in, w2_in, wp_in, norms_in, w1, w2, x_big, x_small, h_big, h_small, first_pre, second_pre, proj_pre, work, act,
    sl_big, sl_small, os_big, os_small, t_big, t_small, p_big, p_small, s_big, s_small,
    norms, norm_rows, stat_a, stat_b, a1, r1, rx1, ry1, rxx1, ryy1, c1, rz1,
    a2, r2, rx2, ry2, rxx2, ryy2, c2, rz2,
    send_sem, recv_sem, local_sem,
):
    nb_img, ns_img, ob, os_, number_big, number_small = cfg
    rows_b, rows_s = ob * ob * nb_img, os_ * os_ * ns_img
    step_b, step_s = ob * nb_img, os_ * ns_img
    b = lax.axis_index("batch")
    z = lax.axis_index("chan")
    core = lax.rem(b, 2)
    x = lax.rem(lax.div(b, 2), 2)
    y = lax.div(b, 4)
    x_peer = (b + 2 - 4 * x, z)
    y_peer = (b + 4 - 8 * y, z)
    sibling = (b + 1 - 2 * core, z)
    z_peers = [(b, lax.rem(z + d, 4)) for d in (1, 2, 3)]
    b_peers = [(lax.rem(b + d, 8), z) for d in range(1, 8)]
    lanes = lambda which: pl.ds(pl.multiple_of(which * 128, 128), 128)
    mine = lanes(z)

    used = [0]
    started = []

    def send(src, dst, peer):
        slot = used[0]
        used[0] += 1
        copy = pltpu.make_async_remote_copy(
            src_ref=src,
            dst_ref=dst,
            send_sem=send_sem.at[slot],
            recv_sem=recv_sem.at[slot],
            device_id=peer,
            device_id_type=MESH,
        )
        copy.start()
        started.append(copy)
        return copy

    barrier = pltpu.get_barrier_semaphore()
    for peer in b_peers + z_peers:
        pl.semaphore_signal(barrier, inc=1, device_id=peer, device_id_type=MESH)

    loads = []

    def load(src, dst):
        copy = pltpu.make_async_copy(src, dst, local_sem.at[len(loads)])
        copy.start()
        loads.append(copy)

    for source, held in ((w1_hbm, w1_in), (w2_hbm, w2_in), (wp_hbm, wp_in), (norms_hbm, norms_in)):
        load(source, held)
    for hp in range(2):
        for wp in range(2):
            load(img_big.at[:, hp, :, wp], x_big.at[hp, wp, pl.ds(hp, ob), pl.ds(wp, ob)])
            load(img_small.at[:, hp, :, wp], x_small.at[hp, wp, pl.ds(hp, os_), pl.ds(wp, os_)])
    load(
        slo_big.at[:, :, pl.ds(pl.multiple_of(z * nb_img, nb_img), nb_img)],
        sl_big.at[:, :, :, mine],
    )
    load(
        slo_small.at[:, :, pl.ds(pl.multiple_of(z * ns_img, ns_img), ns_img)],
        sl_small.at[:, :, :, mine],
    )
    for copy in loads[:4]:
        copy.wait()
    w1[0:9, y, x, core, :, mine] = w1_in[...].astype(BF16)
    w1[9, y, x, core, :, mine] = wp_in[...].astype(BF16)
    w2[:, y, x, core, :, mine] = w2_in[...].astype(BF16)
    norms[z, 0:6] = norms_in[...]

    pl.semaphore_wait(barrier, 10)

    def finish(copies):
        for copy in copies:
            copy.wait_recv()

    class Gather:
        def __init__(self, w, lo, n):
            self.w, self.taps = w, pl.ds(lo, n)
            piece = w.at[self.taps, y, x, core, :, mine]
            self.over_z = [send(piece, piece, peer) for peer in z_peers]

        def near(self):
            finish(self.over_z)
            piece = self.w.at[self.taps, y, x, core]
            self.x_copy = send(piece, piece, x_peer)
            self.y_copy = send(piece, piece, y_peer)
            self.rest = [send(piece, piece, sibling)]

        def far(self):
            self.x_copy.wait_recv()
            part = self.w.at[self.taps, y, 1 - x, core, :, pl.ds(0, 256)]
            self.far_a = send(part, part, y_peer)
            self.y_copy.wait_recv()
            part = self.w.at[self.taps, 1 - y, x, core, :, pl.ds(256, 256)]
            self.far_b = send(part, part, x_peer)
            piece = self.w.at[self.taps, y, 1 - x, core]
            self.rest.append(send(piece, piece, sibling))
            piece = self.w.at[self.taps, 1 - y, x, core]
            self.rest.append(send(piece, piece, sibling))

        def last(self):
            finish([self.far_a, self.far_b])
            piece = self.w.at[self.taps, 1 - y, 1 - x, core]
            self.rest.append(send(piece, piece, sibling))

        def done(self):
            finish(self.rest)

    one_a = Gather(w1, 0, 3)
    z_norms = [send(norms.at[z], norms.at[z], peer) for peer in z_peers]
    one_b, one_c = Gather(w1, 3, 3), Gather(w1, 6, 4)
    two_a, two_b, two_c = (Gather(w2, lo, 3) for lo in (0, 3, 6))

    zero = functools.partial(jnp.zeros, dtype=BF16)
    for wp in range(2):
        x_big[1, wp, 0] = zero((ob + 1, nb_img, 256))
        x_small[1, wp, 0] = zero((os_ + 1, ns_img, 256))
    for hp in range(2):
        x_big[hp, 1, :, 0] = zero((ob + 1, nb_img, 256))
        x_small[hp, 1, :, 0] = zero((os_ + 1, ns_img, 256))
    for ref, side, images in (
        (h_big, ob, nb_img), (t_big, ob, nb_img), (h_small, os_, ns_img), (t_small, os_, ns_img),
    ):
        ref[0] = zero((side + 2, images, 512))
        ref[side + 1] = zero((side + 2, images, 512))
        ref[:, 0] = zero((side + 2, images, 512))
        ref[:, side + 1] = zero((side + 2, images, 512))
    for ref, side, images in ((s_big, ob, nb_img), (s_small, os_, ns_img)):
        ref[side] = zero((side + 1, images, 512))
        ref[:, side] = zero((side + 1, images, 512))

    slope_copies = []

    def slopes_over_z(source, target, lo, n, images):
        for d in (1, 2, 3):
            to = lax.rem(z + d, 4)
            rows = pl.ds(pl.multiple_of(to * images, images), images)
            slope_copies.append(
                send(source.at[pl.ds(lo, n), :, rows], target.at[pl.ds(lo, n), :, :, mine], (b, to))
            )

    big_parts = ((0, 4), (4, ob - 4))
    one_a.near()
    one_b.near()
    one_a.far()
    one_c.near()
    one_b.far()
    two_a.near()
    one_c.far()
    two_b.near()
    slopes_over_z(slo_big, sl_big, *big_parts[0], nb_img)
    one_a.last()
    one_b.last()
    one_c.last()
    finish(z_norms)
    gains = [
        jnp.concatenate([norms[q, r : r + 1, :] for q in range(4)], axis=1) for r in range(6)
    ]
    for copy in loads[4:]:
        copy.wait()
    two_c.near()
    one_a.done()
    one_b.done()
    one_c.done()

    def reduce_start(k, rows):
        for r, row in enumerate(rows):
            stat_a[k, b, r : r + 1, :] = jnp.sum(row, axis=0, keepdims=True)
        part = stat_a.at[k, b, pl.ds(0, len(rows))]
        return [send(part, part, peer) for peer in b_peers]

    def reduce_middle(k, n, copies):
        finish(copies)
        stat_b[k, z, 0:n] = jnp.sum(stat_a[k, :, 0:n], axis=0)
        part = stat_b.at[k, z, pl.ds(0, n)]
        return [send(part, part, peer) for peer in z_peers]

    def reduce_end(k, n, copies):
        finish(copies)
        total = jnp.sum(stat_b[k, :, 0:n], axis=0)
        return [total[r : r + 1, :] for r in range(n)]

    def chunk_big(i):
        return pl.ds(pl.multiple_of(i * step_b, 16), step_b)

    def chunk_small(i):
        return pl.ds(pl.multiple_of(rows_b + i * step_s, 16), step_s)

    def over_groups(body, count):
        start = tuple(jnp.zeros((8, 512), F32) for _ in range(count))
        big = lax.fori_loop(0, ob, lambda i, c: body(0, i, chunk_big(i), c), start)
        small = lax.fori_loop(0, os_, lambda i, c: body(1, i, chunk_small(i), c), start)
        return big, small

    def moments(ref):
        def body(group, i, rows, carry):
            v = ref[rows, :]
            return (carry[0] + fold(v), carry[1] + fold(v * v))

        return over_groups(body, 2)

    def both(big, small):
        return jnp.concatenate([big.reshape(rows_b, -1), small.reshape(rows_s, -1)], axis=0)

    def x_window(ta, tb):
        hp, wp, sa, sb = (ta + 1) % 2, (tb + 1) % 2, ta // 2, tb // 2
        return both(
            x_big[hp, wp, sa : sa + ob, sb : sb + ob],
            x_small[hp, wp, sa : sa + os_, sb : sb + os_],
        )

    def h_window(ta, tb):
        return both(h_big[ta : ta + ob, tb : tb + ob], h_small[ta : ta + os_, tb : tb + os_])

    def t_window(ta, tb):
        ta, tb = 2 - ta, 2 - tb
        return both(t_big[ta : ta + ob, tb : tb + ob], t_small[ta : ta + os_, tb : tb + os_])

    def s_window(sa, sb):
        return both(s_big[sa : sa + ob, sb : sb + ob], s_small[sa : sa + os_, sb : sb + os_])

    def row_of(window, ta):
        return jnp.concatenate([window(ta, tb) for tb in range(3)], axis=1)

    def dot(left, right):
        return jnp.dot(left, right, preferred_element_type=F32)

    def dot_t(left, right):
        return lax.dot_general(left, right, (((1,), (1,)), ((), ())), preferred_element_type=F32)

    def dot_rows(left, right):
        return lax.dot_general(left, right, (((0,), (0,)), ((), ())), preferred_element_type=F32)

    def conv_row(ref, window, w, depth, ta):
        term = dot(row_of(window, ta), w[3 * ta : 3 * ta + 3].reshape(3 * depth, 512))
        if ta == 0:
            ref[...] = term
        else:
            ref[...] += term

    for ta in range(3):
        conv_row(first_pre, x_window, w1, 256, ta)
    proj_pre[...] = dot(x_window(1, 1), w1[9].reshape(256, 512))
    first_big, first_small = moments(first_pre)
    side_big, side_small = moments(proj_pre)
    copies = reduce_start(0, first_big + first_small + side_big + side_small)
    two_a.far()
    two_b.far()
    copies = reduce_middle(0, 8, copies)
    slopes_over_z(slo_big, sl_big, *big_parts[1], nb_img)
    slopes_over_z(slo_small, sl_small, 0, os_, ns_img)
    two_a.last()
    two_c.far()
    two_b.last()
    sums = reduce_end(0, 8, copies)

    def centered(total, square, number):
        center = total / number
        return center, lax.rsqrt(square / number - center * center + NORM_EPS)

    numbers = (number_big, number_small)
    first_stat = [centered(sums[2 * g], sums[2 * g + 1], numbers[g]) for g in range(2)]
    side_stat = [centered(sums[4 + 2 * g], sums[5 + 2 * g], numbers[g]) for g in range(2)]

    def place(group, i, value, big, small, shift):
        if group == 0:
            big[i + shift, shift : shift + ob] = value.reshape(ob, nb_img, 512)
        else:
            small[i + shift, shift : shift + os_] = value.reshape(os_, ns_img, 512)

    def normed(ref, stat, rows):
        return (ref[rows, :] - stat[0]) * stat[1]

    def hide(group, i, rows, carry):
        value = normed(first_pre, first_stat[group], rows)
        first_pre[rows, :] = value
        shaped = value * gains[0] + gains[1]
        place(group, i, (shaped * jax.nn.sigmoid(shaped)).astype(BF16), h_big, h_small, 1)
        return carry

    over_groups(hide, 0)

    two_a.done()
    conv_row(second_pre, h_window, w2, 512, 0)
    two_c.last()
    two_b.done()
    conv_row(second_pre, h_window, w2, 512, 1)
    two_c.done()
    conv_row(second_pre, h_window, w2, 512, 2)
    second_big, second_small = moments(second_pre)
    copies = reduce_start(1, second_big + second_small)

    def prepare(group, i, rows, carry):
        proj_pre[rows, :] = normed(proj_pre, side_stat[group], rows)
        act[rows, :] = silu_slope(first_pre[rows, :] * gains[0] + gains[1])
        return carry

    over_groups(prepare, 0)
    copies = reduce_middle(1, 4, copies)
    finish(slope_copies)
    sums = reduce_end(1, 4, copies)
    second_stat = [centered(sums[2 * g], sums[2 * g + 1], numbers[g]) for g in range(2)]

    def outer(group, i, rows, carry):
        two = normed(second_pre, second_stat[group], rows)
        second_pre[rows, :] = two
        side = proj_pre[rows, :]
        summed = two * gains[2] + gains[3] + side * gains[4] + gains[5]
        gate = jax.nn.sigmoid(summed)
        place(group, i, (summed * gate).astype(BF16), os_big, os_small, 0)
        slope = sl_big[i] if group == 0 else sl_small[i]
        slope = slope.astype(F32).reshape(two.shape)
        upstream = slope * (gate * (1.0 + summed * (1.0 - gate)))
        work[rows, :] = upstream
        return (carry[0] + fold(upstream), carry[1] + fold(upstream * two), carry[2] + fold(upstream * side))

    outer_big, outer_small = over_groups(outer, 3)
    copies = reduce_start(2, outer_big + outer_small)
    stores = []

    def outputs_over_z(staged, target, lo, n, images):
        rows = pl.ds(pl.multiple_of(z * images, images), images)
        for d in (1, 2, 3):
            to = lax.rem(z + d, 4)
            stores.append(
                send(staged.at[pl.ds(lo, n), :, :, lanes(to)], target.at[pl.ds(lo, n), :, rows], (b, to))
            )

    copies = reduce_middle(2, 6, copies)
    outputs_over_z(os_small, out_small, 0, os_, ns_img)
    for staged, target, images in ((os_big, out_big, nb_img), (os_small, out_small, ns_img)):
        load(
            staged.at[:, :, :, mine],
            target.at[:, :, pl.ds(pl.multiple_of(z * images, images), images)],
        )
    sums_outer = reduce_end(2, 6, copies)

    def slopes(group, i, rows, carry):
        total, cross_two, cross_side = sums_outer[3 * group : 3 * group + 3]
        number = numbers[group]
        base = work[rows, :] - total / number
        slope_two = gains[2] * second_stat[group][1] * (base - second_pre[rows, :] * (cross_two / number))
        slope_side = gains[4] * side_stat[group][1] * (base - proj_pre[rows, :] * (cross_side / number))
        place(group, i, slope_two.astype(BF16), t_big, t_small, 1)
        place(group, i, slope_side.astype(BF16), p_big, p_small, 0)
        return carry

    over_groups(slopes, 0)

    class Scatter:
        def __init__(self, bufs, lo, n):
            self.bufs, self.taps = bufs, pl.ds(lo, n)
            self.loop = lambda body: lax.fori_loop(lo, lo + n, lambda t, c: (body(t), c)[1], 0)
            a, r = bufs[0], bufs[1]
            self.copies = [send(a.at[self.taps, :, :, 1 - core], r.at[self.taps], sibling)]

        def near(self):
            finish(self.copies)
            a, r, rx, ry = self.bufs[:4]

            def add(t):
                r[t] = (r[t].astype(F32) + a[t, :, :, core].astype(F32)).astype(BF16)

            self.loop(add)
            taps = self.taps
            self.copies = [
                send(r.at[taps, :, 1 - x, :, pl.ds(0, 256)], rx.at[taps], x_peer),
                send(r.at[taps, 1 - y, :, :, pl.ds(256, 256)], ry.at[taps], y_peer),
            ]

        def far(self):
            finish(self.copies)
            _, r, rx, ry, rxx, ryy = self.bufs[:6]

            def add(t):
                rx[t] = (rx[t].astype(F32) + r[t, :, x, :, 0:256].astype(F32)).astype(BF16)
                ry[t] = (ry[t].astype(F32) + r[t, y, :, :, 256:512].astype(F32)).astype(BF16)

            self.loop(add)
            taps = self.taps
            self.copies = [
                send(rx.at[taps, 1 - y], ryy.at[taps], y_peer),
                send(ry.at[taps, 1 - x], rxx.at[taps], x_peer),
            ]

        def over_z(self):
            finish(self.copies)
            rx, ry, rxx, ryy, c, rz = self.bufs[2:8]

            def add(t):
                c[t, :, 0:256] = (rx[t, y].astype(F32) + ryy[t].astype(F32)).astype(BF16)
                c[t, :, 256:512] = (ry[t, x].astype(F32) + rxx[t].astype(F32)).astype(BF16)

            self.loop(add)
            self.copies = [
                send(
                    c.at[self.taps, :, lanes(lax.rem(z + d, 4))],
                    rz.at[d - 1, self.taps],
                    (b, lax.rem(z + d, 4)),
                )
                for d in (1, 2, 3)
            ]

        def end(self):
            finish(self.copies)
            c, rz, out = self.bufs[6:]

            def add(t):
                total = c[t, :, mine].astype(F32)
                for d in range(3):
                    total = total + rz[d, t].astype(F32)
                out[t] = total

            self.loop(add)

    t_flat = lambda: both(t_big[1 : ob + 1, 1 : ob + 1], t_small[1 : os_ + 1, 1 : os_ + 1])
    s_flat = lambda: both(s_big[0:ob, 0:ob], s_small[0:os_, 0:os_])
    p_flat = lambda: both(p_big[...], p_small[...])

    def grad_two(lo, n):
        for t in range(lo, lo + n):
            a2[t] = dot_rows(h_window(t // 3, t % 3), t_flat()).astype(BF16).reshape(a2.shape[1:])
        return Scatter((a2, r2, rx2, ry2, rxx2, ryy2, c2, rz2, grad_two_out), lo, n)

    def grad_one(ta, proj):
        sums = dot_rows(row_of(x_window, ta), s_flat()).astype(BF16)
        a1[3 * ta : 3 * ta + 3] = sums.reshape((3,) + a1.shape[1:])
        if proj:
            a1[9] = dot_rows(x_window(1, 1), p_flat()).astype(BF16).reshape(a1.shape[1:])
        return Scatter((a1, r1, rx1, ry1, rxx1, ryy1, c1, rz1, grad_one_out), 3 * ta, 4 if proj else 3)

    def back_row(ta):
        term = None
        for tb in range(3):
            part = dot_t(t_window(ta, tb), w2[3 * ta + tb].reshape(512, 512))
            term = part if term is None else term + part
        if ta == 0:
            work[...] = term
        else:
            work[...] += term

    sum_a = grad_two(0, 2)
    sum_b = grad_two(2, 2)
    sum_a.near()
    back_row(0)
    sum_b.near()
    outputs_over_z(os_big, out_big, *big_parts[0], nb_img)
    back_row(1)
    back_row(2)

    def inner(group, i, rows, carry):
        e = work[rows, :] * act[rows, :]
        work[rows, :] = e
        return (carry[0] + fold(e), carry[1] + fold(e * first_pre[rows, :]))

    inner_big, inner_small = over_groups(inner, 2)
    copies = reduce_start(3, inner_big + inner_small)
    sum_a.far()
    sum_c = grad_two(4, 2)
    sum_b.far()
    sum_d = grad_two(6, 3)
    sum_c.near()
    copies = reduce_middle(3, 4, copies)
    sum_d.near()
    sum_a.over_z()
    sum_b.over_z()
    sums_inner = reduce_end(3, 4, copies)

    def slopes_one(group, i, rows, carry):
        total, cross = sums_inner[2 * group : 2 * group + 2]
        number = numbers[group]
        slope = gains[0] * first_stat[group][1] * (
            work[rows, :] - total / number - first_pre[rows, :] * (cross / number)
        )
        place(group, i, slope.astype(BF16), s_big, s_small, 0)
        return carry

    over_groups(slopes_one, 0)

    sum_e = grad_one(0, False)
    outputs_over_z(os_big, out_big, *big_parts[1], nb_img)
    sum_c.far()
    sum_f = grad_one(1, False)
    sum_e.near()
    sum_g = grad_one(2, True)
    sum_f.near()
    sum_d.far()
    sum_g.near()

    def back_one(hp, wp):
        total = dot_t(p_flat(), w1[9].reshape(256, 512)) if hp + wp == 0 else None
        for ta in ((1,), (2, 0))[hp]:
            for tb in ((1,), (2, 0))[wp]:
                term = dot_t(
                    s_window(int(ta == 0), int(tb == 0)), w1[3 * ta + tb].reshape(256, 512)
                )
                total = term if total is None else total + term
        total = total.astype(BF16)
        grad_big[:, hp, :, wp] = total[:rows_b].reshape(ob, ob, nb_img, 256)
        grad_small[:, hp, :, wp] = total[rows_b:].reshape(os_, os_, ns_img, 256)

    back_one(0, 0)
    back_one(0, 1)
    sum_e.far()
    back_one(1, 0)
    sum_f.far()
    sum_c.over_z()
    sum_g.far()
    back_one(1, 1)
    rows = [
        sums_inner[1] + sums_inner[3],
        sums_inner[0] + sums_inner[2],
        sums_outer[1] + sums_outer[4],
        sums_outer[0] + sums_outer[3],
        sums_outer[2] + sums_outer[5],
        sums_outer[0] + sums_outer[3],
    ]
    for r, row in enumerate(rows):
        norm_rows[r : r + 1, :] = row
    grad_norms[...] = norm_rows[0:6, mine]
    sum_d.over_z()
    sum_e.over_z()
    sum_f.over_z()
    sum_a.end()
    sum_b.end()
    sum_g.over_z()
    sum_c.end()
    sum_d.end()
    sum_e.end()
    sum_f.end()
    sum_g.end()
    finish(stores)
    for copy in loads[14:]:
        copy.wait()
    for copy in started:
        copy.wait_send()
    assert used[0] <= COPIES


def tap_window(padded, tap_row, tap_col, stride, size_out):
    reach = stride * (size_out - 1) + 1
    return lax.slice(
        padded,
        (0, tap_row, tap_col, 0),
        (padded.shape[0], tap_row + reach, tap_col + reach, padded.shape[3]),
        (1, stride, stride, 1),
    )


def conv_taps(inputs, kernel, stride):
    size_out = (inputs.shape[1] - 1) // stride + 1
    padded = jnp.pad(inputs, ((0, 0), (1, 1), (1, 1), (0, 0)))
    summed = jnp.zeros((inputs.shape[0], size_out, size_out, kernel.shape[3]), jnp.float32)
    for tap_row in range(3):
        for tap_col in range(3):
            window = tap_window(padded, tap_row, tap_col, stride, size_out)
            summed = summed + jnp.einsum(
                "nhwc,co->nhwo",
                window,
                kernel[tap_row, tap_col],
                preferred_element_type=jnp.float32,
            )
    return summed


def kernel_grad(inputs, slope, stride):
    size_out = slope.shape[1]
    padded = jnp.pad(inputs, ((0, 0), (1, 1), (1, 1), (0, 0)))
    tap_rows = []
    for tap_row in range(3):
        across = []
        for tap_col in range(3):
            window = tap_window(padded, tap_row, tap_col, stride, size_out)
            across.append(
                jnp.einsum("nhwc,nhwo->co", window, slope, preferred_element_type=jnp.float32)
            )
        tap_rows.append(jnp.stack(across))
    return jnp.stack(tap_rows)


def input_grad(slope, kernel, stride, size_in):
    size_out = slope.shape[1]
    full_size = size_in + 2
    reach = stride * (size_out - 1) + 1
    summed = jnp.zeros((slope.shape[0], full_size, full_size, kernel.shape[2]), jnp.float32)
    for tap_row in range(3):
        for tap_col in range(3):
            term = jnp.einsum(
                "nhwo,co->nhwc", slope, kernel[tap_row, tap_col], preferred_element_type=jnp.float32
            )
            summed = summed + lax.pad(
                term,
                jnp.float32(0.0),
                (
                    (0, 0, 0),
                    (tap_row, full_size - tap_row - reach, stride - 1),
                    (tap_col, full_size - tap_col - reach, stride - 1),
                    (0, 0, 0),
                ),
            )
    return summed[:, 1:-1, 1:-1, :]


def proj_input_grad(slope, kernel, size_in):
    term = jnp.einsum("nhwo,co->nhwc", slope, kernel, preferred_element_type=jnp.float32)
    margin = size_in - 2 * slope.shape[1] + 1
    return lax.pad(term, jnp.float32(0.0), ((0, 0, 0), (0, margin, 1), (0, margin, 1), (0, 0, 0)))


def moments(values):
    return (jnp.sum(values, axis=(0, 1, 2)), jnp.sum(values * values, axis=(0, 1, 2)))


def normalize(values, total, square_total, number):
    center = total / number
    factor = lax.rsqrt(square_total / number - center * center + NORM_EPS)
    return ((values - center) * factor, factor)


def norm_back(upstream, normed, factor, gain, total, cross, number):
    return gain * factor * (upstream - total / number - normed * (cross / number))


def plain_body(
    image_big,
    image_small,
    slope_big,
    slope_small,
    conv1_weight,
    conv2_weight,
    proj_weight,
    norm_params,
    first_conv1,
    first_conv2,
    first_proj,
    first_norms,
    second_conv1,
    second_conv2,
    second_proj,
    second_norms,
):
    bfloat = jnp.bfloat16
    kernel_one, kernel_two, kernel_proj = (
        lax.all_gather(conv1_weight.astype(bfloat), "batch", axis=2, tiled=True),
        lax.all_gather(conv2_weight.astype(bfloat), "batch", axis=2, tiled=True),
        lax.all_gather(proj_weight.astype(bfloat), "batch", axis=0, tiled=True),
    )
    inputs_big, inputs_small = (
        lax.all_gather(image_big, "chan", axis=0, tiled=True),
        lax.all_gather(image_small, "chan", axis=0, tiled=True),
    )
    groups = (inputs_big, inputs_small)
    batch_width = lax.axis_size("batch")
    first_pre = [conv_taps(images, kernel_one, 2) for images in groups]
    numbers = [
        values.shape[0] * values.shape[1] * values.shape[2] * batch_width for values in first_pre
    ]
    sum_big, square_big = moments(first_pre[0])
    sum_small, square_small = moments(first_pre[1])
    sum_big, square_big, sum_small, square_small = lax.psum(
        (sum_big, square_big, sum_small, square_small), "batch"
    )
    first_norm = [
        normalize(first_pre[0], sum_big, square_big, numbers[0]),
        normalize(first_pre[1], sum_small, square_small, numbers[1]),
    ]
    shaped = [normed * norm_params[0] + norm_params[1] for normed, factor in first_norm]
    hidden = [jax.nn.silu(values).astype(bfloat) for values in shaped]
    hidden_big, hidden_small = (
        lax.all_gather(hidden[0], "chan", axis=3, tiled=True),
        lax.all_gather(hidden[1], "chan", axis=3, tiled=True),
    )
    hidden_full = (hidden_big, hidden_small)
    second_pre = [conv_taps(values, kernel_two, 1) for values in hidden_full]
    proj_pre = [
        jnp.einsum(
            "nhwc,co->nhwo", images[:, ::2, ::2, :], kernel_proj, preferred_element_type=jnp.float32
        )
        for images in groups
    ]
    two_big, two_sq_big = moments(second_pre[0])
    two_small, two_sq_small = moments(second_pre[1])
    side_big, side_sq_big = moments(proj_pre[0])
    side_small, side_sq_small = moments(proj_pre[1])
    (
        two_big,
        two_sq_big,
        two_small,
        two_sq_small,
        side_big,
        side_sq_big,
        side_small,
        side_sq_small,
    ) = lax.psum(
        (
            two_big,
            two_sq_big,
            two_small,
            two_sq_small,
            side_big,
            side_sq_big,
            side_small,
            side_sq_small,
        ),
        "batch",
    )
    second_norm = [
        normalize(second_pre[0], two_big, two_sq_big, numbers[0]),
        normalize(second_pre[1], two_small, two_sq_small, numbers[1]),
    ]
    proj_norm = [
        normalize(proj_pre[0], side_big, side_sq_big, numbers[0]),
        normalize(proj_pre[1], side_small, side_sq_small, numbers[1]),
    ]
    summed = [
        second_norm[which][0] * norm_params[2]
        + norm_params[3]
        + proj_norm[which][0] * norm_params[4]
        + norm_params[5]
        for which in range(2)
    ]
    out_big = jax.nn.silu(summed[0]).astype(bfloat)
    out_small = jax.nn.silu(summed[1]).astype(bfloat)
    slopes = (slope_big, slope_small)
    upstream = [slopes[which].astype(jnp.float32) * silu_slope(summed[which]) for which in range(2)]
    outer_big = jnp.sum(upstream[0], axis=(0, 1, 2))
    cross_two_big = jnp.sum(upstream[0] * second_norm[0][0], axis=(0, 1, 2))
    cross_side_big = jnp.sum(upstream[0] * proj_norm[0][0], axis=(0, 1, 2))
    outer_small = jnp.sum(upstream[1], axis=(0, 1, 2))
    cross_two_small = jnp.sum(upstream[1] * second_norm[1][0], axis=(0, 1, 2))
    cross_side_small = jnp.sum(upstream[1] * proj_norm[1][0], axis=(0, 1, 2))
    outer_big, cross_two_big, cross_side_big, outer_small, cross_two_small, cross_side_small = (
        lax.psum(
            (
                outer_big,
                cross_two_big,
                cross_side_big,
                outer_small,
                cross_two_small,
                cross_side_small,
            ),
            "batch",
        )
    )
    outer_sums = (outer_big, outer_small)
    cross_two = (cross_two_big, cross_two_small)
    cross_side = (cross_side_big, cross_side_small)
    slope_two = [
        norm_back(
            upstream[which],
            second_norm[which][0],
            second_norm[which][1],
            norm_params[2],
            outer_sums[which],
            cross_two[which],
            numbers[which],
        ).astype(bfloat)
        for which in range(2)
    ]
    slope_proj = [
        norm_back(
            upstream[which],
            proj_norm[which][0],
            proj_norm[which][1],
            norm_params[4],
            outer_sums[which],
            cross_side[which],
            numbers[which],
        ).astype(bfloat)
        for which in range(2)
    ]
    part_big = input_grad(slope_two[0], kernel_two, 1, hidden_big.shape[1])
    part_small = input_grad(slope_two[1], kernel_two, 1, hidden_small.shape[1])
    back_big, back_small = (
        lax.psum_scatter(part_big, "chan", scatter_dimension=3, tiled=True),
        lax.psum_scatter(part_small, "chan", scatter_dimension=3, tiled=True),
    )
    inner = [back_big * silu_slope(shaped[0]), back_small * silu_slope(shaped[1])]
    inner_big = jnp.sum(inner[0], axis=(0, 1, 2))
    cross_one_big = jnp.sum(inner[0] * first_norm[0][0], axis=(0, 1, 2))
    inner_small = jnp.sum(inner[1], axis=(0, 1, 2))
    cross_one_small = jnp.sum(inner[1] * first_norm[1][0], axis=(0, 1, 2))
    inner_big, cross_one_big, inner_small, cross_one_small = lax.psum(
        (inner_big, cross_one_big, inner_small, cross_one_small), "batch"
    )
    inner_sums = (inner_big, inner_small)
    cross_one = (cross_one_big, cross_one_small)
    slope_one = [
        norm_back(
            inner[which],
            first_norm[which][0],
            first_norm[which][1],
            norm_params[0],
            inner_sums[which],
            cross_one[which],
            numbers[which],
        ).astype(bfloat)
        for which in range(2)
    ]
    size_big = image_big.shape[1]
    size_small = image_small.shape[1]
    input_part_big = input_grad(slope_one[0], kernel_one, 2, size_big) + proj_input_grad(
        slope_proj[0], kernel_proj, size_big
    )
    input_part_small = input_grad(slope_one[1], kernel_one, 2, size_small) + proj_input_grad(
        slope_proj[1], kernel_proj, size_small
    )
    grad_big, grad_small = (
        lax.psum_scatter(input_part_big, "chan", scatter_dimension=0, tiled=True),
        lax.psum_scatter(input_part_small, "chan", scatter_dimension=0, tiled=True),
    )
    part_conv1 = kernel_grad(groups[0], slope_one[0], 2) + kernel_grad(groups[1], slope_one[1], 2)
    part_conv2 = kernel_grad(hidden_full[0], slope_two[0], 1) + kernel_grad(
        hidden_full[1], slope_two[1], 1
    )
    part_proj = jnp.einsum(
        "nhwc,nhwo->co",
        groups[0][:, ::2, ::2, :],
        slope_proj[0],
        preferred_element_type=jnp.float32,
    ) + jnp.einsum(
        "nhwc,nhwo->co",
        groups[1][:, ::2, ::2, :],
        slope_proj[1],
        preferred_element_type=jnp.float32,
    )
    grad_conv1, grad_conv2, grad_proj = (
        lax.psum_scatter(part_conv1, "batch", scatter_dimension=2, tiled=True),
        lax.psum_scatter(part_conv2, "batch", scatter_dimension=2, tiled=True),
        lax.psum_scatter(part_proj, "batch", scatter_dimension=0, tiled=True),
    )
    grad_norms = jnp.stack(
        [
            cross_one_big + cross_one_small,
            inner_big + inner_small,
            cross_two_big + cross_two_small,
            outer_big + outer_small,
            cross_side_big + cross_side_small,
            outer_big + outer_small,
        ]
    )
    new_conv1, moment_conv1, square_conv1 = adamw_step(
        conv1_weight, grad_conv1, first_conv1, second_conv1, (9.0 * C_IN) ** (-0.5), DECAY
    )
    new_conv2, moment_conv2, square_conv2 = adamw_step(
        conv2_weight, grad_conv2, first_conv2, second_conv2, (9.0 * C_OUT) ** (-0.5), DECAY
    )
    new_proj, moment_proj, square_proj = adamw_step(
        proj_weight, grad_proj, first_proj, second_proj, (1.0 * C_IN) ** (-0.5), DECAY
    )
    new_norms, moment_norms, square_norms = adamw_step(
        norm_params, grad_norms, first_norms, second_norms, NORM_RATE, 0.0
    )
    return (
        out_big,
        out_small,
        grad_big.astype(bfloat),
        grad_small.astype(bfloat),
        grad_conv1,
        grad_conv2,
        grad_proj,
        grad_norms,
        new_conv1,
        new_conv2,
        new_proj,
        new_norms,
        moment_conv1,
        moment_conv2,
        moment_proj,
        moment_norms,
        square_conv1,
        square_conv2,
        square_proj,
        square_norms,
    )


def update_kernel(*refs):
    passed, sums, states, rest = refs[:4], refs[4:7], refs[7:19], refs[19:]
    passed_out, outs, (sem,) = rest[:4], rest[4:20], rest[20:]
    g1, g2, gn = sums
    copies = [
        pltpu.make_async_copy(src, dst, sem.at[i])
        for i, (src, dst) in enumerate(zip(passed, passed_out))
    ]
    for copy in copies:
        copy.start()
    w1, w2 = states[0], states[1]
    grads = (g1[0:9].reshape(w1.shape), g2[...].reshape(w2.shape), g1[9], gn[...])
    rates = ((9.0 * C_IN) ** (-0.5), (9.0 * C_OUT) ** (-0.5), (1.0 * C_IN) ** (-0.5), NORM_RATE)
    for i in range(4):
        weight, first, second = (states[i + 4 * k][...] for k in range(3))
        new, moment, square = adamw_step(
            weight, grads[i], first, second, rates[i], DECAY if i < 3 else 0.0
        )
        for k, value in enumerate((grads[i], new, moment, square)):
            outs[i + 4 * k][...] = value
    for copy in copies:
        copy.wait()


def fused_body(
    devices,
    image_big, image_small, slope_big, slope_small,
    conv1_weight, conv2_weight, proj_weight, norm_params,
    first_conv1, first_conv2, first_proj, first_norms,
    second_conv1, second_conv2, second_proj, second_norms,
):
    nb_img, side_b = image_big.shape[0], image_big.shape[1]
    ns_img, side_s = image_small.shape[0], image_small.shape[1]
    ob, os_ = side_b // 2, side_s // 2
    rows = ob * ob * nb_img + os_ * os_ * ns_img
    cfg = (nb_img, ns_img, ob, os_, ob * ob * nb_img * devices, os_ * os_ * ns_img * devices)
    r1, r2 = conv1_weight.shape[2], conv2_weight.shape[2]

    def parity(images, side):
        images = jnp.transpose(images, (1, 2, 0, 3))
        return images.reshape(side // 2, 2, side // 2, 2, images.shape[2], C_IN)

    def flat(weight):
        return weight.reshape((9,) + weight.shape[2:])

    vmem = pl.BlockSpec(memory_space=pltpu.VMEM)
    anywhere = pl.BlockSpec(memory_space=pl.ANY)
    hbm = pl.BlockSpec(memory_space=pltpu.HBM)
    shape = jax.ShapeDtypeStruct
    out_shape = (
        pltpu.VMEM((ob, ob, slope_big.shape[0], 128), BF16),
        pltpu.VMEM((os_, os_, slope_small.shape[0], 128), BF16),
        pltpu.VMEM((ob, 2, ob, 2, nb_img, C_IN), BF16),
        pltpu.VMEM((os_, 2, os_, 2, ns_img, C_IN), BF16),
        pltpu.VMEM((10, r1, 128), F32),
        pltpu.VMEM((9, r2, 128), F32),
        pltpu.VMEM((6, 128), F32),
    )

    def sum_buffers(taps, r):
        return [
            pltpu.VMEM((taps, 2, 2, 2, r, 512), BF16),
            pltpu.VMEM((taps, 2, 2, r, 512), BF16),
            pltpu.VMEM((taps, 2, r, 256), BF16),
            pltpu.VMEM((taps, 2, r, 256), BF16),
            pltpu.VMEM((taps, r, 256), BF16),
            pltpu.VMEM((taps, r, 256), BF16),
            pltpu.VMEM((taps, r, 512), BF16),
            pltpu.VMEM((3, taps, r, 128), BF16),
        ]

    def maps(extra):
        return [
            pltpu.VMEM((ob + extra, ob + extra, nb_img, 512), BF16),
            pltpu.VMEM((os_ + extra, os_ + extra, ns_img, 512), BF16),
        ]

    scratch = (
        [
            pltpu.VMEM((9, r1, 128), F32),
            pltpu.VMEM((9, r2, 128), F32),
            pltpu.VMEM((r1, 128), F32),
            pltpu.VMEM((6, 128), F32),
            pltpu.VMEM((10, 2, 2, 2, r1, 512), BF16),
            pltpu.VMEM((9, 2, 2, 2, r2, 512), BF16),
            pltpu.VMEM((2, 2, ob + 1, ob + 1, nb_img, C_IN), BF16),
            pltpu.VMEM((2, 2, os_ + 1, os_ + 1, ns_img, C_IN), BF16),
        ]
        + maps(2)
        + [pltpu.VMEM((rows, 512), F32) for _ in range(5)]
        + maps(0)
        + maps(0)
        + maps(2)
        + maps(0)
        + maps(1)
        + [
            pltpu.VMEM((4, 8, 128), F32),
            pltpu.VMEM((8, 512), F32),
            pltpu.VMEM((4, 8, 8, 512), F32),
            pltpu.VMEM((4, 4, 8, 512), F32),
        ]
        + sum_buffers(10, r1)
        + sum_buffers(9, r2)
        + [
            pltpu.SemaphoreType.DMA((COPIES,)),
            pltpu.SemaphoreType.DMA((COPIES,)),
            pltpu.SemaphoreType.DMA((16,)),
        ]
    )
    macs = rows * 512 * (9 * C_IN + 9 * C_OUT + C_IN) * 3
    out_big, out_small, grad_big, grad_small, grad_one, grad_two, grad_norms = pl.pallas_call(
        functools.partial(block_kernel, cfg),
        out_shape=out_shape,
        in_specs=[hbm] * 8,
        out_specs=[anywhere] * 2 + [vmem] * 5,
        scratch_shapes=scratch,
        compiler_params=pltpu.CompilerParams(
            collective_id=0, has_side_effects=True, vmem_limit_bytes=VMEM_BYTES
        ),
        cost_estimate=pl.CostEstimate(flops=2 * macs, bytes_accessed=1 << 23, transcendentals=rows * 2048),
    )(
        parity(image_big, side_b),
        parity(image_small, side_s),
        jnp.transpose(slope_big, (1, 2, 0, 3)),
        jnp.transpose(slope_small, (1, 2, 0, 3)),
        flat(conv1_weight),
        flat(conv2_weight),
        proj_weight,
        norm_params,
    )
    weights = (conv1_weight, conv2_weight, proj_weight, norm_params)
    passed = (out_big, out_small, grad_big, grad_small)
    sums = (grad_one, grad_two, grad_norms)
    out_big, out_small, grad_big, grad_small, *updated = pl.pallas_call(
        update_kernel,
        out_shape=[shape(v.shape, v.dtype) for v in passed] + [shape(w.shape, F32) for w in weights] * 4,
        in_specs=[vmem] * 19,
        out_specs=[anywhere] * 4 + [vmem] * 16,
        scratch_shapes=[pltpu.SemaphoreType.DMA((4,))],
        compiler_params=pltpu.CompilerParams(vmem_limit_bytes=16 << 20),
    )(
        *passed, *sums, *weights,
        first_conv1, first_conv2, first_proj, first_norms,
        second_conv1, second_conv2, second_proj, second_norms,
    )

    def unparity(images, side):
        images = images.reshape(side, side, images.shape[4], C_IN)
        return jnp.transpose(images, (2, 0, 1, 3))

    return (
        jnp.transpose(out_big, (2, 0, 1, 3)),
        jnp.transpose(out_small, (2, 0, 1, 3)),
        unparity(grad_big, side_b),
        unparity(grad_small, side_s),
        *updated,
    )


def solution(mesh):
    images = P(("batch", "chan"), None, None, None)
    maps = P("batch", None, None, "chan")
    convs = P(None, None, "batch", "chan")
    proj = P("batch", "chan")
    norms = P(None, "chan")
    states = (convs, convs, proj, norms)
    fused = mesh.shape["batch"] == 8 and mesh.shape["chan"] == 4
    return jax.shard_map(
        functools.partial(fused_body, 32) if fused else plain_body,
        mesh=mesh,
        in_specs=(images, images, maps, maps) + states * 3,
        out_specs=(maps, maps, images, images) + states * 4,
        check_vma=False,
    )
```

```python
import functools

import jax
import jax.numpy as jnp
from jax import lax
from jax.experimental import pallas as pl
from jax.experimental.pallas import tpu as pltpu
from jax.sharding import PartitionSpec as P

C_IN = 256
C_OUT = 512
STEP = 5
NORM_EPS = 1e-05
BETA_ONE = 0.5
BETA_TWO = 0.5
ADAM_EPS = 1e-08
DECAY = 0.01
NORM_RATE = 0.3
MESH = pl.DeviceIdType.MESH
BF16 = jnp.bfloat16
F32 = jnp.float32
COPIES = 240
VMEM_BYTES = 58 << 20


def silu_slope(values):
    gate = jax.nn.sigmoid(values)
    return gate * (1.0 + values * (1.0 - gate))


def adamw_step(weight, gradient, first, second, rate, decay):
    first_new = BETA_ONE * first + (1.0 - BETA_ONE) * gradient
    second_new = BETA_TWO * second + (1.0 - BETA_TWO) * gradient * gradient
    first_hat = first_new / (1.0 - BETA_ONE**STEP)
    second_hat = second_new / (1.0 - BETA_TWO**STEP)
    updated = weight - rate * (first_hat / (jnp.sqrt(second_hat) + ADAM_EPS) + decay * weight)
    return (updated, first_new, second_new)


def fold(values):
    rows, channels = values.shape
    return jnp.sum(values.reshape(rows // 8, 8, channels), axis=0)


def block_kernel(
    cfg,
    img_big, img_small, slo_big, slo_small, w1_hbm, w2_hbm, wp_hbm, norms_hbm,
    out_big, out_small, grad_big, grad_small, grad_one_out, grad_two_out, grad_norms,
    w1_in, w2_in, wp_in, norms_in, w1, w2, x_big, x_small, h_big, h_small, first_pre, second_pre, proj_pre, work, act,
    sl_big, sl_small, os_big, os_small, t_big, t_small, p_big, p_small, s_big, s_small,
    norms, norm_rows, stat_a, stat_b, a1, r1, rx1, ry1, rxx1, ryy1, c1, rz1,
    a2, r2, rx2, ry2, rxx2, ryy2, c2, rz2,
    send_sem, recv_sem, local_sem,
):
    nb_img, ns_img, ob, os_, number_big, number_small = cfg
    rows_b, rows_s = ob * ob * nb_img, os_ * os_ * ns_img
    step_b, step_s = ob * nb_img, os_ * ns_img
    b = lax.axis_index("batch")
    z = lax.axis_index("chan")
    core = lax.rem(b, 2)
    x = lax.rem(lax.div(b, 2), 2)
    y = lax.div(b, 4)
    x_peer = (b + 2 - 4 * x, z)
    y_peer = (b + 4 - 8 * y, z)
    sibling = (b + 1 - 2 * core, z)
    odd, upper = lax.rem(z, 2), lax.div(z, 2)
    pair_peer, cross_peer = (b, z + 1 - 2 * odd), (b, lax.rem(z + 2, 4))
    z_peers = [(b, lax.rem(z + d, 4)) for d in (1, 2, 3)]
    b_peers = [(lax.rem(b + d, 8), z) for d in range(1, 8)]
    lanes = lambda which: pl.ds(pl.multiple_of(which * 128, 128), 128)
    mine = lanes(z)

    used = [0]
    started = []

    def send(src, dst, peer):
        slot = used[0]
        used[0] += 1
        copy = pltpu.make_async_remote_copy(
            src_ref=src,
            dst_ref=dst,
            send_sem=send_sem.at[slot],
            recv_sem=recv_sem.at[slot],
            device_id=peer,
            device_id_type=MESH,
        )
        copy.start()
        started.append(copy)
        return copy

    barrier = pltpu.get_barrier_semaphore()
    for peer in b_peers + z_peers:
        pl.semaphore_signal(barrier, inc=1, device_id=peer, device_id_type=MESH)

    loads = []

    def load(src, dst):
        copy = pltpu.make_async_copy(src, dst, local_sem.at[len(loads)])
        copy.start()
        loads.append(copy)

    for source, held in ((w1_hbm, w1_in), (w2_hbm, w2_in), (wp_hbm, wp_in), (norms_hbm, norms_in)):
        load(source, held)
    for hp in range(2):
        for wp in range(2):
            load(img_big.at[:, hp, :, wp], x_big.at[hp, wp, pl.ds(hp, ob), pl.ds(wp, ob)])
            load(img_small.at[:, hp, :, wp], x_small.at[hp, wp, pl.ds(hp, os_), pl.ds(wp, os_)])
    load(
        slo_big.at[:, :, pl.ds(pl.multiple_of(z * nb_img, nb_img), nb_img)],
        sl_big.at[:, :, :, mine],
    )
    load(
        slo_small.at[:, :, pl.ds(pl.multiple_of(z * ns_img, ns_img), ns_img)],
        sl_small.at[:, :, :, mine],
    )
    for copy in loads[:4]:
        copy.wait()
    w1[0:9, y, x, core, :, mine] = w1_in[...].astype(BF16)
    w1[9, y, x, core, :, mine] = wp_in[...].astype(BF16)
    w2[:, y, x, core, :, mine] = w2_in[...].astype(BF16)
    norms[z, 0:6] = norms_in[...]

    pl.semaphore_wait(barrier, 10)

    def finish(copies):
        for copy in copies:
            copy.wait_recv()

    class Gather:
        def __init__(self, w, lo, n):
            self.w, self.taps = w, pl.ds(lo, n)
            piece = w.at[self.taps, y, x, core, :, mine]
            self.over_z = [send(piece, piece, peer) for peer in z_peers]

        def near(self):
            finish(self.over_z)
            piece = self.w.at[self.taps, y, x, core]
            self.x_copy = send(piece, piece, x_peer)
            self.y_copy = send(piece, piece, y_peer)
            self.rest = [send(piece, piece, sibling)]

        def far(self):
            self.x_copy.wait_recv()
            part = self.w.at[self.taps, y, 1 - x, core, :, pl.ds(0, 256)]
            self.far_a = send(part, part, y_peer)
            self.y_copy.wait_recv()
            part = self.w.at[self.taps, 1 - y, x, core, :, pl.ds(256, 256)]
            self.far_b = send(part, part, x_peer)
            piece = self.w.at[self.taps, y, 1 - x, core]
            self.rest.append(send(piece, piece, sibling))
            piece = self.w.at[self.taps, 1 - y, x, core]
            self.rest.append(send(piece, piece, sibling))

        def last(self):
            finish([self.far_a, self.far_b])
            piece = self.w.at[self.taps, 1 - y, 1 - x, core]
            self.rest.append(send(piece, piece, sibling))

        def done(self):
            finish(self.rest)

    one_a = Gather(w1, 0, 3)
    z_norms = [send(norms.at[z], norms.at[z], peer) for peer in z_peers]
    one_b, one_c = Gather(w1, 3, 3), Gather(w1, 6, 4)
    two_a, two_b, two_c = (Gather(w2, lo, 3) for lo in (0, 3, 6))

    zero = functools.partial(jnp.zeros, dtype=BF16)
    for wp in range(2):
        x_big[1, wp, 0] = zero((ob + 1, nb_img, 256))
        x_small[1, wp, 0] = zero((os_ + 1, ns_img, 256))
    for hp in range(2):
        x_big[hp, 1, :, 0] = zero((ob + 1, nb_img, 256))
        x_small[hp, 1, :, 0] = zero((os_ + 1, ns_img, 256))
    for ref, side, images in (
        (h_big, ob, nb_img), (t_big, ob, nb_img), (h_small, os_, ns_img), (t_small, os_, ns_img),
    ):
        ref[0] = zero((side + 2, images, 512))
        ref[side + 1] = zero((side + 2, images, 512))
        ref[:, 0] = zero((side + 2, images, 512))
        ref[:, side + 1] = zero((side + 2, images, 512))
    for ref, side, images in ((s_big, ob, nb_img), (s_small, os_, ns_img)):
        ref[side] = zero((side + 1, images, 512))
        ref[:, side] = zero((side + 1, images, 512))

    slope_copies = []

    def slopes_over_z(source, target, lo, n, images):
        for d in (1, 2, 3):
            to = lax.rem(z + d, 4)
            rows = pl.ds(pl.multiple_of(to * images, images), images)
            slope_copies.append(
                send(source.at[pl.ds(lo, n), :, rows], target.at[pl.ds(lo, n), :, :, mine], (b, to))
            )

    big_parts = ((0, 4), (4, ob - 4))
    out_parts = ((0, 3), (3, 2), (5, ob - 5))
    one_a.near()
    one_b.near()
    one_a.far()
    one_c.near()
    one_b.far()
    one_c.far()
    two_a.near()
    one_a.last()
    one_b.last()
    one_c.last()
    two_b.near()
    slopes_over_z(slo_big, sl_big, *big_parts[0], nb_img)
    finish(z_norms)
    gains = [
        jnp.concatenate([norms[q, r : r + 1, :] for q in range(4)], axis=1) for r in range(6)
    ]
    for copy in loads[4:]:
        copy.wait()
    one_a.done()
    one_b.done()
    one_c.done()

    def reduce_start(k, rows):
        for r, row in enumerate(rows):
            stat_a[k, b, r : r + 1, :] = jnp.sum(row, axis=0, keepdims=True)
        part = stat_a.at[k, b, pl.ds(0, len(rows))]
        return [send(part, part, peer) for peer in b_peers]

    def reduce_middle(k, n, copies):
        finish(copies)
        stat_b[k, z, 0:n] = jnp.sum(stat_a[k, :, 0:n], axis=0)
        part = stat_b.at[k, z, pl.ds(0, n)]
        return [send(part, part, peer) for peer in z_peers]

    def reduce_end(k, n, copies):
        finish(copies)
        total = jnp.sum(stat_b[k, :, 0:n], axis=0)
        return [total[r : r + 1, :] for r in range(n)]

    def chunk_big(i):
        return pl.ds(pl.multiple_of(i * step_b, 16), step_b)

    def chunk_small(i):
        return pl.ds(pl.multiple_of(rows_b + i * step_s, 16), step_s)

    def over_groups(body, count):
        start = tuple(jnp.zeros((8, 512), F32) for _ in range(count))
        big = lax.fori_loop(0, ob, lambda i, c: body(0, i, chunk_big(i), c), start)
        small = lax.fori_loop(0, os_, lambda i, c: body(1, i, chunk_small(i), c), start)
        return big, small

    def moments(ref):
        def body(group, i, rows, carry):
            v = ref[rows, :]
            return (carry[0] + fold(v), carry[1] + fold(v * v))

        return over_groups(body, 2)

    def both(big, small):
        return jnp.concatenate([big.reshape(rows_b, -1), small.reshape(rows_s, -1)], axis=0)

    def x_window(ta, tb):
        hp, wp, sa, sb = (ta + 1) % 2, (tb + 1) % 2, ta // 2, tb // 2
        return both(
            x_big[hp, wp, sa : sa + ob, sb : sb + ob],
            x_small[hp, wp, sa : sa + os_, sb : sb + os_],
        )

    def h_window(ta, tb):
        return both(h_big[ta : ta + ob, tb : tb + ob], h_small[ta : ta + os_, tb : tb + os_])

    def t_window(ta, tb):
        ta, tb = 2 - ta, 2 - tb
        return both(t_big[ta : ta + ob, tb : tb + ob], t_small[ta : ta + os_, tb : tb + os_])

    def s_window(sa, sb):
        return both(s_big[sa : sa + ob, sb : sb + ob], s_small[sa : sa + os_, sb : sb + os_])

    def row_of(window, ta):
        return jnp.concatenate([window(ta, tb) for tb in range(3)], axis=1)

    def dot(left, right):
        return jnp.dot(left, right, preferred_element_type=F32)

    def dot_t(left, right):
        return lax.dot_general(left, right, (((1,), (1,)), ((), ())), preferred_element_type=F32)

    def dot_rows(left, right):
        return lax.dot_general(left, right, (((0,), (0,)), ((), ())), preferred_element_type=F32)

    def conv_row(ref, window, w, depth, ta):
        term = dot(row_of(window, ta), w[3 * ta : 3 * ta + 3].reshape(3 * depth, 512))
        if ta == 0:
            ref[...] = term
        else:
            ref[...] += term

    conv_row(first_pre, x_window, w1, 256, 0)
    conv_row(first_pre, x_window, w1, 256, 1)
    two_a.far()
    conv_row(first_pre, x_window, w1, 256, 2)
    first_big, first_small = moments(first_pre)
    copies = reduce_start(0, first_big + first_small)
    proj_pre[...] = dot(x_window(1, 1), w1[9].reshape(256, 512))
    side_big, side_small = moments(proj_pre)
    two_c.near()
    two_b.far()
    copies = reduce_middle(0, 4, copies)
    slopes_over_z(slo_big, sl_big, *big_parts[1], nb_img)
    slopes_over_z(slo_small, sl_small, 0, os_, ns_img)
    two_a.last()
    two_c.far()
    sums = reduce_end(0, 4, copies)

    def centered(total, square, number):
        center = total / number
        return center, lax.rsqrt(square / number - center * center + NORM_EPS)

    numbers = (number_big, number_small)
    first_stat = [centered(sums[2 * g], sums[2 * g + 1], numbers[g]) for g in range(2)]
    side_copies = reduce_start(4, side_big + side_small)

    def place(group, i, value, big, small, shift):
        if group == 0:
            big[i + shift, shift : shift + ob] = value.reshape(ob, nb_img, 512)
        else:
            small[i + shift, shift : shift + os_] = value.reshape(os_, ns_img, 512)

    def normed(ref, stat, rows):
        return (ref[rows, :] - stat[0]) * stat[1]

    def hide(group, i, rows, carry):
        value = normed(first_pre, first_stat[group], rows)
        first_pre[rows, :] = value
        shaped = value * gains[0] + gains[1]
        place(group, i, (shaped * jax.nn.sigmoid(shaped)).astype(BF16), h_big, h_small, 1)
        return carry

    over_groups(hide, 0)

    two_a.done()
    two_b.last()
    conv_row(second_pre, h_window, w2, 512, 0)
    two_b.done()
    conv_row(second_pre, h_window, w2, 512, 1)
    side_copies = reduce_middle(4, 4, side_copies)
    two_c.last()
    two_c.done()
    conv_row(second_pre, h_window, w2, 512, 2)
    second_big, second_small = moments(second_pre)
    copies = reduce_start(1, second_big + second_small)

    def prepare(group, i, rows, carry):
        act[rows, :] = silu_slope(first_pre[rows, :] * gains[0] + gains[1])
        return carry

    over_groups(prepare, 0)
    copies = reduce_middle(1, 4, copies)
    sums = reduce_end(4, 4, side_copies)
    side_stat = [centered(sums[2 * g], sums[2 * g + 1], numbers[g]) for g in range(2)]

    def prepare_side(group, i, rows, carry):
        proj_pre[rows, :] = normed(proj_pre, side_stat[group], rows)
        return carry

    over_groups(prepare_side, 0)
    finish(slope_copies)
    sums = reduce_end(1, 4, copies)
    second_stat = [centered(sums[2 * g], sums[2 * g + 1], numbers[g]) for g in range(2)]

    def outer(group, i, rows, carry):
        two = normed(second_pre, second_stat[group], rows)
        second_pre[rows, :] = two
        side = proj_pre[rows, :]
        summed = two * gains[2] + gains[3] + side * gains[4] + gains[5]
        gate = jax.nn.sigmoid(summed)
        place(group, i, (summed * gate).astype(BF16), os_big, os_small, 0)
        slope = sl_big[i] if group == 0 else sl_small[i]
        slope = slope.astype(F32).reshape(two.shape)
        upstream = slope * (gate * (1.0 + summed * (1.0 - gate)))
        work[rows, :] = upstream
        return (carry[0] + fold(upstream), carry[1] + fold(upstream * two), carry[2] + fold(upstream * side))

    outer_big, outer_small = over_groups(outer, 3)
    copies = reduce_start(2, outer_big + outer_small)
    stores = []

    def outputs_over_z(staged, target, lo, n, images):
        rows = pl.ds(pl.multiple_of(z * images, images), images)
        for d in (1, 2, 3):
            to = lax.rem(z + d, 4)
            stores.append(
                send(staged.at[pl.ds(lo, n), :, :, lanes(to)], target.at[pl.ds(lo, n), :, rows], (b, to))
            )

    copies = reduce_middle(2, 6, copies)
    outputs_over_z(os_small, out_small, 0, os_, ns_img)
    for staged, target, images in ((os_big, out_big, nb_img), (os_small, out_small, ns_img)):
        load(
            staged.at[:, :, :, mine],
            target.at[:, :, pl.ds(pl.multiple_of(z * images, images), images)],
        )
    sums_outer = reduce_end(2, 6, copies)
    outputs_over_z(os_big, out_big, *out_parts[0], nb_img)

    def slopes(group, i, rows, carry):
        total, cross_two, cross_side = sums_outer[3 * group : 3 * group + 3]
        number = numbers[group]
        base = work[rows, :] - total / number
        slope_two = gains[2] * second_stat[group][1] * (base - second_pre[rows, :] * (cross_two / number))
        place(group, i, slope_two.astype(BF16), t_big, t_small, 1)
        return carry

    def slopes_side(group, i, rows, carry):
        total, cross_two, cross_side = sums_outer[3 * group : 3 * group + 3]
        number = numbers[group]
        base = work[rows, :] - total / number
        slope_side = gains[4] * side_stat[group][1] * (base - proj_pre[rows, :] * (cross_side / number))
        place(group, i, slope_side.astype(BF16), p_big, p_small, 0)
        return carry

    over_groups(slopes, 0)

    class Scatter:
        def __init__(self, bufs, lo, n, pairs=False):
            self.bufs, self.taps, self.pairs = bufs, pl.ds(lo, n), pairs
            self.loop = lambda body: lax.fori_loop(lo, lo + n, lambda t, c: (body(t), c)[1], 0)
            a, r = bufs[0], bufs[1]
            self.copies = [send(a.at[self.taps, :, :, 1 - core], r.at[self.taps], sibling)]

        def near(self):
            finish(self.copies)
            a, r, rx, ry = self.bufs[:4]

            def add(t):
                r[t] = (r[t].astype(F32) + a[t, :, :, core].astype(F32)).astype(BF16)

            self.loop(add)
            taps = self.taps
            self.copies = [
                send(r.at[taps, :, 1 - x, :, pl.ds(0, 256)], rx.at[taps], x_peer),
                send(r.at[taps, 1 - y, :, :, pl.ds(256, 256)], ry.at[taps], y_peer),
            ]

        def far(self):
            finish(self.copies)
            _, r, rx, ry, rxx, ryy = self.bufs[:6]

            def add(t):
                rx[t] = (rx[t].astype(F32) + r[t, :, x, :, 0:256].astype(F32)).astype(BF16)
                ry[t] = (ry[t].astype(F32) + r[t, y, :, :, 256:512].astype(F32)).astype(BF16)

            self.loop(add)
            taps = self.taps
            self.copies = [
                send(rx.at[taps, 1 - y], ryy.at[taps], y_peer),
                send(ry.at[taps, 1 - x], rxx.at[taps], x_peer),
            ]

        def over_z(self):
            finish(self.copies)
            rx, ry, rxx, ryy, c, rz = self.bufs[2:8]

            def add(t):
                c[t, :, 0:256] = (rx[t, y].astype(F32) + ryy[t].astype(F32)).astype(BF16)
                c[t, :, 256:512] = (ry[t, x].astype(F32) + rxx[t].astype(F32)).astype(BF16)

            self.loop(add)
            to_z = lambda d: c.at[self.taps, :, lanes(lax.rem(z + d, 4))]
            if self.pairs:
                self.copies = [
                    send(c.at[self.taps, :, lanes(2 * far + 1 - odd)], rz.at[far, self.taps], pair_peer)
                    for far in range(2)
                ]
            else:
                self.copies = [
                    send(to_z(d), rz.at[d - 1, self.taps], (b, lax.rem(z + d, 4))) for d in (1, 2, 3)
                ]

        def cross(self):
            finish(self.copies)
            c, rz = self.bufs[6:8]

            def add(t):
                kept = c[t, :, lanes(2 * (1 - upper) + odd)].astype(F32)
                rz[1 - upper, t] = (rz[1 - upper, t].astype(F32) + kept).astype(BF16)

            self.loop(add)
            self.copies = [send(rz.at[1 - upper, self.taps], rz.at[2, self.taps], cross_peer)]

        def end(self):
            finish(self.copies)
            c, rz, out = self.bufs[6:]

            def add(t):
                total = c[t, :, mine].astype(F32)
                if self.pairs:
                    total = total + rz[upper, t].astype(F32) + rz[2, t].astype(F32)
                else:
                    for d in range(3):
                        total = total + rz[d, t].astype(F32)
                out[t] = total

            self.loop(add)

    t_flat = lambda: both(t_big[1 : ob + 1, 1 : ob + 1], t_small[1 : os_ + 1, 1 : os_ + 1])
    s_flat = lambda: both(s_big[0:ob, 0:ob], s_small[0:os_, 0:os_])
    p_flat = lambda: both(p_big[...], p_small[...])

    def grad_two(lo, n, pairs=False):
        for t in range(lo, lo + n):
            a2[t] = dot_rows(h_window(t // 3, t % 3), t_flat()).astype(BF16).reshape(a2.shape[1:])
        return Scatter((a2, r2, rx2, ry2, rxx2, ryy2, c2, rz2, grad_two_out), lo, n, pairs)

    one_bufs = (a1, r1, rx1, ry1, rxx1, ryy1, c1, rz1, grad_one_out)

    def grad_one(lo, n):
        windows = jnp.concatenate([x_window(t // 3, t % 3) for t in range(lo, lo + n)], axis=1)
        a1[lo : lo + n] = dot_rows(windows, s_flat()).astype(BF16).reshape((n,) + a1.shape[1:])
        return Scatter(one_bufs, lo, n)

    def grad_proj():
        a1[9] = dot_rows(x_window(1, 1), p_flat()).astype(BF16).reshape(a1.shape[1:])
        return Scatter(one_bufs, 9, 1)

    def back_row(ta):
        term = None
        for tb in range(3):
            part = dot_t(t_window(ta, tb), w2[3 * ta + tb].reshape(512, 512))
            term = part if term is None else term + part
        if ta == 0:
            second_pre[...] = term
        else:
            second_pre[...] += term

    sum_a = grad_two(0, 1)
    sum_b = grad_two(1, 2)
    sum_a.near()
    back_row(0)
    sum_b.near()
    back_row(1)
    sum_a.far()
    back_row(2)

    def inner(group, i, rows, carry):
        e = second_pre[rows, :] * act[rows, :]
        second_pre[rows, :] = e
        return (carry[0] + fold(e), carry[1] + fold(e * first_pre[rows, :]))

    inner_big, inner_small = over_groups(inner, 2)
    copies = reduce_start(3, inner_big + inner_small)
    sum_c = grad_two(3, 2)
    sum_b.far()
    sum_d = grad_two(5, 2)
    copies = reduce_middle(3, 4, copies)
    outputs_over_z(os_big, out_big, *out_parts[1], nb_img)
    sum_c.near()
    sum_e = grad_two(7, 2)
    sum_d.near()
    over_groups(slopes_side, 0)
    sums_inner = reduce_end(3, 4, copies)
    sum_a.over_z()
    sum_b.over_z()
    outputs_over_z(os_big, out_big, *out_parts[2], nb_img)

    def slopes_one(group, i, rows, carry):
        total, cross = sums_inner[2 * group : 2 * group + 2]
        number = numbers[group]
        slope = gains[0] * first_stat[group][1] * (
            second_pre[rows, :] - total / number - first_pre[rows, :] * (cross / number)
        )
        place(group, i, slope.astype(BF16), s_big, s_small, 0)
        return carry

    over_groups(slopes_one, 0)

    sum_f = grad_one(0, 2)
    sum_e.near()
    sum_c.far()
    sum_g = grad_one(2, 3)
    sum_f.near()
    sum_d.far()
    sum_p = grad_proj()
    sum_h = grad_one(5, 3)
    sum_g.near()
    sum_p.near()
    sum_c.over_z()
    sum_e.far()
    sum_i = grad_one(8, 1)
    sum_f.far()
    sum_h.near()
    sum_i.near()
    sum_d.over_z()

    def back_one(hp, wp):
        total = dot_t(p_flat(), w1[9].reshape(256, 512)) if hp + wp == 0 else None
        for ta in ((1,), (2, 0))[hp]:
            for tb in ((1,), (2, 0))[wp]:
                term = dot_t(
                    s_window(int(ta == 0), int(tb == 0)), w1[3 * ta + tb].reshape(256, 512)
                )
                total = term if total is None else total + term
        total = total.astype(BF16)
        grad_big[:, hp, :, wp] = total[:rows_b].reshape(ob, ob, nb_img, 256)
        grad_small[:, hp, :, wp] = total[rows_b:].reshape(os_, os_, ns_img, 256)

    back_one(0, 0)
    sum_g.far()
    sum_p.far()
    sum_e.over_z()
    back_one(0, 1)
    sum_f.over_z()
    sum_h.far()
    sum_i.far()
    back_one(1, 0)
    sum_p.over_z()
    sum_g.over_z()
    sum_h.over_z()
    sum_i.over_z()
    back_one(1, 1)
    rows = [
        sums_inner[1] + sums_inner[3],
        sums_inner[0] + sums_inner[2],
        sums_outer[1] + sums_outer[4],
        sums_outer[0] + sums_outer[3],
        sums_outer[2] + sums_outer[5],
        sums_outer[0] + sums_outer[3],
    ]
    for r, row in enumerate(rows):
        norm_rows[r : r + 1, :] = row
    grad_norms[...] = norm_rows[0:6, mine]
    sum_a.end()
    sum_b.end()
    sum_c.end()
    sum_d.end()
    sum_e.end()
    sum_f.end()
    sum_p.end()
    sum_g.end()
    sum_h.end()
    sum_i.end()
    finish(stores)
    for copy in loads[14:]:
        copy.wait()
    for copy in started:
        copy.wait_send()
    assert used[0] <= COPIES


def tap_window(padded, tap_row, tap_col, stride, size_out):
    reach = stride * (size_out - 1) + 1
    return lax.slice(
        padded,
        (0, tap_row, tap_col, 0),
        (padded.shape[0], tap_row + reach, tap_col + reach, padded.shape[3]),
        (1, stride, stride, 1),
    )


def conv_taps(inputs, kernel, stride):
    size_out = (inputs.shape[1] - 1) // stride + 1
    padded = jnp.pad(inputs, ((0, 0), (1, 1), (1, 1), (0, 0)))
    summed = jnp.zeros((inputs.shape[0], size_out, size_out, kernel.shape[3]), jnp.float32)
    for tap_row in range(3):
        for tap_col in range(3):
            window = tap_window(padded, tap_row, tap_col, stride, size_out)
            summed = summed + jnp.einsum(
                "nhwc,co->nhwo",
                window,
                kernel[tap_row, tap_col],
                preferred_element_type=jnp.float32,
            )
    return summed


def kernel_grad(inputs, slope, stride):
    size_out = slope.shape[1]
    padded = jnp.pad(inputs, ((0, 0), (1, 1), (1, 1), (0, 0)))
    tap_rows = []
    for tap_row in range(3):
        across = []
        for tap_col in range(3):
            window = tap_window(padded, tap_row, tap_col, stride, size_out)
            across.append(
                jnp.einsum("nhwc,nhwo->co", window, slope, preferred_element_type=jnp.float32)
            )
        tap_rows.append(jnp.stack(across))
    return jnp.stack(tap_rows)


def input_grad(slope, kernel, stride, size_in):
    size_out = slope.shape[1]
    full_size = size_in + 2
    reach = stride * (size_out - 1) + 1
    summed = jnp.zeros((slope.shape[0], full_size, full_size, kernel.shape[2]), jnp.float32)
    for tap_row in range(3):
        for tap_col in range(3):
            term = jnp.einsum(
                "nhwo,co->nhwc", slope, kernel[tap_row, tap_col], preferred_element_type=jnp.float32
            )
            summed = summed + lax.pad(
                term,
                jnp.float32(0.0),
                (
                    (0, 0, 0),
                    (tap_row, full_size - tap_row - reach, stride - 1),
                    (tap_col, full_size - tap_col - reach, stride - 1),
                    (0, 0, 0),
                ),
            )
    return summed[:, 1:-1, 1:-1, :]


def proj_input_grad(slope, kernel, size_in):
    term = jnp.einsum("nhwo,co->nhwc", slope, kernel, preferred_element_type=jnp.float32)
    margin = size_in - 2 * slope.shape[1] + 1
    return lax.pad(term, jnp.float32(0.0), ((0, 0, 0), (0, margin, 1), (0, margin, 1), (0, 0, 0)))


def moments(values):
    return (jnp.sum(values, axis=(0, 1, 2)), jnp.sum(values * values, axis=(0, 1, 2)))


def normalize(values, total, square_total, number):
    center = total / number
    factor = lax.rsqrt(square_total / number - center * center + NORM_EPS)
    return ((values - center) * factor, factor)


def norm_back(upstream, normed, factor, gain, total, cross, number):
    return gain * factor * (upstream - total / number - normed * (cross / number))


def plain_body(
    image_big,
    image_small,
    slope_big,
    slope_small,
    conv1_weight,
    conv2_weight,
    proj_weight,
    norm_params,
    first_conv1,
    first_conv2,
    first_proj,
    first_norms,
    second_conv1,
    second_conv2,
    second_proj,
    second_norms,
):
    bfloat = jnp.bfloat16
    kernel_one, kernel_two, kernel_proj = (
        lax.all_gather(conv1_weight.astype(bfloat), "batch", axis=2, tiled=True),
        lax.all_gather(conv2_weight.astype(bfloat), "batch", axis=2, tiled=True),
        lax.all_gather(proj_weight.astype(bfloat), "batch", axis=0, tiled=True),
    )
    inputs_big, inputs_small = (
        lax.all_gather(image_big, "chan", axis=0, tiled=True),
        lax.all_gather(image_small, "chan", axis=0, tiled=True),
    )
    groups = (inputs_big, inputs_small)
    batch_width = lax.axis_size("batch")
    first_pre = [conv_taps(images, kernel_one, 2) for images in groups]
    numbers = [
        values.shape[0] * values.shape[1] * values.shape[2] * batch_width for values in first_pre
    ]
    sum_big, square_big = moments(first_pre[0])
    sum_small, square_small = moments(first_pre[1])
    sum_big, square_big, sum_small, square_small = lax.psum(
        (sum_big, square_big, sum_small, square_small), "batch"
    )
    first_norm = [
        normalize(first_pre[0], sum_big, square_big, numbers[0]),
        normalize(first_pre[1], sum_small, square_small, numbers[1]),
    ]
    shaped = [normed * norm_params[0] + norm_params[1] for normed, factor in first_norm]
    hidden = [jax.nn.silu(values).astype(bfloat) for values in shaped]
    hidden_big, hidden_small = (
        lax.all_gather(hidden[0], "chan", axis=3, tiled=True),
        lax.all_gather(hidden[1], "chan", axis=3, tiled=True),
    )
    hidden_full = (hidden_big, hidden_small)
    second_pre = [conv_taps(values, kernel_two, 1) for values in hidden_full]
    proj_pre = [
        jnp.einsum(
            "nhwc,co->nhwo", images[:, ::2, ::2, :], kernel_proj, preferred_element_type=jnp.float32
        )
        for images in groups
    ]
    two_big, two_sq_big = moments(second_pre[0])
    two_small, two_sq_small = moments(second_pre[1])
    side_big, side_sq_big = moments(proj_pre[0])
    side_small, side_sq_small = moments(proj_pre[1])
    (
        two_big,
        two_sq_big,
        two_small,
        two_sq_small,
        side_big,
        side_sq_big,
        side_small,
        side_sq_small,
    ) = lax.psum(
        (
            two_big,
            two_sq_big,
            two_small,
            two_sq_small,
            side_big,
            side_sq_big,
            side_small,
            side_sq_small,
        ),
        "batch",
    )
    second_norm = [
        normalize(second_pre[0], two_big, two_sq_big, numbers[0]),
        normalize(second_pre[1], two_small, two_sq_small, numbers[1]),
    ]
    proj_norm = [
        normalize(proj_pre[0], side_big, side_sq_big, numbers[0]),
        normalize(proj_pre[1], side_small, side_sq_small, numbers[1]),
    ]
    summed = [
        second_norm[which][0] * norm_params[2]
        + norm_params[3]
        + proj_norm[which][0] * norm_params[4]
        + norm_params[5]
        for which in range(2)
    ]
    out_big = jax.nn.silu(summed[0]).astype(bfloat)
    out_small = jax.nn.silu(summed[1]).astype(bfloat)
    slopes = (slope_big, slope_small)
    upstream = [slopes[which].astype(jnp.float32) * silu_slope(summed[which]) for which in range(2)]
    outer_big = jnp.sum(upstream[0], axis=(0, 1, 2))
    cross_two_big = jnp.sum(upstream[0] * second_norm[0][0], axis=(0, 1, 2))
    cross_side_big = jnp.sum(upstream[0] * proj_norm[0][0], axis=(0, 1, 2))
    outer_small = jnp.sum(upstream[1], axis=(0, 1, 2))
    cross_two_small = jnp.sum(upstream[1] * second_norm[1][0], axis=(0, 1, 2))
    cross_side_small = jnp.sum(upstream[1] * proj_norm[1][0], axis=(0, 1, 2))
    outer_big, cross_two_big, cross_side_big, outer_small, cross_two_small, cross_side_small = (
        lax.psum(
            (
                outer_big,
                cross_two_big,
                cross_side_big,
                outer_small,
                cross_two_small,
                cross_side_small,
            ),
            "batch",
        )
    )
    outer_sums = (outer_big, outer_small)
    cross_two = (cross_two_big, cross_two_small)
    cross_side = (cross_side_big, cross_side_small)
    slope_two = [
        norm_back(
            upstream[which],
            second_norm[which][0],
            second_norm[which][1],
            norm_params[2],
            outer_sums[which],
            cross_two[which],
            numbers[which],
        ).astype(bfloat)
        for which in range(2)
    ]
    slope_proj = [
        norm_back(
            upstream[which],
            proj_norm[which][0],
            proj_norm[which][1],
            norm_params[4],
            outer_sums[which],
            cross_side[which],
            numbers[which],
        ).astype(bfloat)
        for which in range(2)
    ]
    part_big = input_grad(slope_two[0], kernel_two, 1, hidden_big.shape[1])
    part_small = input_grad(slope_two[1], kernel_two, 1, hidden_small.shape[1])
    back_big, back_small = (
        lax.psum_scatter(part_big, "chan", scatter_dimension=3, tiled=True),
        lax.psum_scatter(part_small, "chan", scatter_dimension=3, tiled=True),
    )
    inner = [back_big * silu_slope(shaped[0]), back_small * silu_slope(shaped[1])]
    inner_big = jnp.sum(inner[0], axis=(0, 1, 2))
    cross_one_big = jnp.sum(inner[0] * first_norm[0][0], axis=(0, 1, 2))
    inner_small = jnp.sum(inner[1], axis=(0, 1, 2))
    cross_one_small = jnp.sum(inner[1] * first_norm[1][0], axis=(0, 1, 2))
    inner_big, cross_one_big, inner_small, cross_one_small = lax.psum(
        (inner_big, cross_one_big, inner_small, cross_one_small), "batch"
    )
    inner_sums = (inner_big, inner_small)
    cross_one = (cross_one_big, cross_one_small)
    slope_one = [
        norm_back(
            inner[which],
            first_norm[which][0],
            first_norm[which][1],
            norm_params[0],
            inner_sums[which],
            cross_one[which],
            numbers[which],
        ).astype(bfloat)
        for which in range(2)
    ]
    size_big = image_big.shape[1]
    size_small = image_small.shape[1]
    input_part_big = input_grad(slope_one[0], kernel_one, 2, size_big) + proj_input_grad(
        slope_proj[0], kernel_proj, size_big
    )
    input_part_small = input_grad(slope_one[1], kernel_one, 2, size_small) + proj_input_grad(
        slope_proj[1], kernel_proj, size_small
    )
    grad_big, grad_small = (
        lax.psum_scatter(input_part_big, "chan", scatter_dimension=0, tiled=True),
        lax.psum_scatter(input_part_small, "chan", scatter_dimension=0, tiled=True),
    )
    part_conv1 = kernel_grad(groups[0], slope_one[0], 2) + kernel_grad(groups[1], slope_one[1], 2)
    part_conv2 = kernel_grad(hidden_full[0], slope_two[0], 1) + kernel_grad(
        hidden_full[1], slope_two[1], 1
    )
    part_proj = jnp.einsum(
        "nhwc,nhwo->co",
        groups[0][:, ::2, ::2, :],
        slope_proj[0],
        preferred_element_type=jnp.float32,
    ) + jnp.einsum(
        "nhwc,nhwo->co",
        groups[1][:, ::2, ::2, :],
        slope_proj[1],
        preferred_element_type=jnp.float32,
    )
    grad_conv1, grad_conv2, grad_proj = (
        lax.psum_scatter(part_conv1, "batch", scatter_dimension=2, tiled=True),
        lax.psum_scatter(part_conv2, "batch", scatter_dimension=2, tiled=True),
        lax.psum_scatter(part_proj, "batch", scatter_dimension=0, tiled=True),
    )
    grad_norms = jnp.stack(
        [
            cross_one_big + cross_one_small,
            inner_big + inner_small,
            cross_two_big + cross_two_small,
            outer_big + outer_small,
            cross_side_big + cross_side_small,
            outer_big + outer_small,
        ]
    )
    new_conv1, moment_conv1, square_conv1 = adamw_step(
        conv1_weight, grad_conv1, first_conv1, second_conv1, (9.0 * C_IN) ** (-0.5), DECAY
    )
    new_conv2, moment_conv2, square_conv2 = adamw_step(
        conv2_weight, grad_conv2, first_conv2, second_conv2, (9.0 * C_OUT) ** (-0.5), DECAY
    )
    new_proj, moment_proj, square_proj = adamw_step(
        proj_weight, grad_proj, first_proj, second_proj, (1.0 * C_IN) ** (-0.5), DECAY
    )
    new_norms, moment_norms, square_norms = adamw_step(
        norm_params, grad_norms, first_norms, second_norms, NORM_RATE, 0.0
    )
    return (
        out_big,
        out_small,
        grad_big.astype(bfloat),
        grad_small.astype(bfloat),
        grad_conv1,
        grad_conv2,
        grad_proj,
        grad_norms,
        new_conv1,
        new_conv2,
        new_proj,
        new_norms,
        moment_conv1,
        moment_conv2,
        moment_proj,
        moment_norms,
        square_conv1,
        square_conv2,
        square_proj,
        square_norms,
    )


def update_kernel(*refs):
    passed, sums, states, rest = refs[:4], refs[4:7], refs[7:19], refs[19:]
    passed_out, outs, (sem,) = rest[:4], rest[4:20], rest[20:]
    g1, g2, gn = sums
    copies = [
        pltpu.make_async_copy(src, dst, sem.at[i])
        for i, (src, dst) in enumerate(zip(passed, passed_out))
    ]
    for copy in copies:
        copy.start()
    w1, w2 = states[0], states[1]
    grads = (g1[0:9].reshape(w1.shape), g2[...].reshape(w2.shape), g1[9], gn[...])
    rates = ((9.0 * C_IN) ** (-0.5), (9.0 * C_OUT) ** (-0.5), (1.0 * C_IN) ** (-0.5), NORM_RATE)
    for i in range(4):
        weight, first, second = (states[i + 4 * k][...] for k in range(3))
        new, moment, square = adamw_step(
            weight, grads[i], first, second, rates[i], DECAY if i < 3 else 0.0
        )
        for k, value in enumerate((grads[i], new, moment, square)):
            outs[i + 4 * k][...] = value
    for copy in copies:
        copy.wait()


def fused_body(
    devices,
    image_big, image_small, slope_big, slope_small,
    conv1_weight, conv2_weight, proj_weight, norm_params,
    first_conv1, first_conv2, first_proj, first_norms,
    second_conv1, second_conv2, second_proj, second_norms,
):
    nb_img, side_b = image_big.shape[0], image_big.shape[1]
    ns_img, side_s = image_small.shape[0], image_small.shape[1]
    ob, os_ = side_b // 2, side_s // 2
    rows = ob * ob * nb_img + os_ * os_ * ns_img
    cfg = (nb_img, ns_img, ob, os_, ob * ob * nb_img * devices, os_ * os_ * ns_img * devices)
    r1, r2 = conv1_weight.shape[2], conv2_weight.shape[2]

    def parity(images, side):
        images = jnp.transpose(images, (1, 2, 0, 3))
        return images.reshape(side // 2, 2, side // 2, 2, images.shape[2], C_IN)

    def flat(weight):
        return weight.reshape((9,) + weight.shape[2:])

    vmem = pl.BlockSpec(memory_space=pltpu.VMEM)
    anywhere = pl.BlockSpec(memory_space=pl.ANY)
    hbm = pl.BlockSpec(memory_space=pltpu.HBM)
    shape = jax.ShapeDtypeStruct
    out_shape = (
        pltpu.VMEM((ob, ob, slope_big.shape[0], 128), BF16),
        pltpu.VMEM((os_, os_, slope_small.shape[0], 128), BF16),
        pltpu.VMEM((ob, 2, ob, 2, nb_img, C_IN), BF16),
        pltpu.VMEM((os_, 2, os_, 2, ns_img, C_IN), BF16),
        pltpu.VMEM((10, r1, 128), F32),
        pltpu.VMEM((9, r2, 128), F32),
        pltpu.VMEM((6, 128), F32),
    )

    def sum_buffers(taps, r):
        return [
            pltpu.VMEM((taps, 2, 2, 2, r, 512), BF16),
            pltpu.VMEM((taps, 2, 2, r, 512), BF16),
            pltpu.VMEM((taps, 2, r, 256), BF16),
            pltpu.VMEM((taps, 2, r, 256), BF16),
            pltpu.VMEM((taps, r, 256), BF16),
            pltpu.VMEM((taps, r, 256), BF16),
            pltpu.VMEM((taps, r, 512), BF16),
            pltpu.VMEM((3, taps, r, 128), BF16),
        ]

    def maps(extra):
        return [
            pltpu.VMEM((ob + extra, ob + extra, nb_img, 512), BF16),
            pltpu.VMEM((os_ + extra, os_ + extra, ns_img, 512), BF16),
        ]

    scratch = (
        [
            pltpu.VMEM((9, r1, 128), F32),
            pltpu.VMEM((9, r2, 128), F32),
            pltpu.VMEM((r1, 128), F32),
            pltpu.VMEM((6, 128), F32),
            pltpu.VMEM((10, 2, 2, 2, r1, 512), BF16),
            pltpu.VMEM((9, 2, 2, 2, r2, 512), BF16),
            pltpu.VMEM((2, 2, ob + 1, ob + 1, nb_img, C_IN), BF16),
            pltpu.VMEM((2, 2, os_ + 1, os_ + 1, ns_img, C_IN), BF16),
        ]
        + maps(2)
        + [pltpu.VMEM((rows, 512), F32) for _ in range(5)]
        + maps(0)
        + maps(0)
        + maps(2)
        + maps(0)
        + maps(1)
        + [
            pltpu.VMEM((4, 8, 128), F32),
            pltpu.VMEM((8, 512), F32),
            pltpu.VMEM((5, 8, 8, 512), F32),
            pltpu.VMEM((5, 4, 8, 512), F32),
        ]
        + sum_buffers(10, r1)
        + sum_buffers(9, r2)
        + [
            pltpu.SemaphoreType.DMA((COPIES,)),
            pltpu.SemaphoreType.DMA((COPIES,)),
            pltpu.SemaphoreType.DMA((16,)),
        ]
    )
    macs = rows * 512 * (9 * C_IN + 9 * C_OUT + C_IN) * 3
    out_big, out_small, grad_big, grad_small, grad_one, grad_two, grad_norms = pl.pallas_call(
        functools.partial(block_kernel, cfg),
        out_shape=out_shape,
        in_specs=[hbm] * 8,
        out_specs=[anywhere] * 2 + [vmem] * 5,
        scratch_shapes=scratch,
        compiler_params=pltpu.CompilerParams(
            collective_id=0, has_side_effects=True, vmem_limit_bytes=VMEM_BYTES
        ),
        cost_estimate=pl.CostEstimate(flops=2 * macs, bytes_accessed=1 << 23, transcendentals=rows * 2048),
    )(
        parity(image_big, side_b),
        parity(image_small, side_s),
        jnp.transpose(slope_big, (1, 2, 0, 3)),
        jnp.transpose(slope_small, (1, 2, 0, 3)),
        flat(conv1_weight),
        flat(conv2_weight),
        proj_weight,
        norm_params,
    )
    weights = (conv1_weight, conv2_weight, proj_weight, norm_params)
    passed = (out_big, out_small, grad_big, grad_small)
    sums = (grad_one, grad_two, grad_norms)
    out_big, out_small, grad_big, grad_small, *updated = pl.pallas_call(
        update_kernel,
        out_shape=[shape(v.shape, v.dtype) for v in passed] + [shape(w.shape, F32) for w in weights] * 4,
        in_specs=[vmem] * 19,
        out_specs=[anywhere] * 4 + [vmem] * 16,
        scratch_shapes=[pltpu.SemaphoreType.DMA((4,))],
        compiler_params=pltpu.CompilerParams(vmem_limit_bytes=16 << 20),
    )(
        *passed, *sums, *weights,
        first_conv1, first_conv2, first_proj, first_norms,
        second_conv1, second_conv2, second_proj, second_norms,
    )

    def unparity(images, side):
        images = images.reshape(side, side, images.shape[4], C_IN)
        return jnp.transpose(images, (2, 0, 1, 3))

    return (
        jnp.transpose(out_big, (2, 0, 1, 3)),
        jnp.transpose(out_small, (2, 0, 1, 3)),
        unparity(grad_big, side_b),
        unparity(grad_small, side_s),
        *updated,
    )


def solution(mesh):
    images = P(("batch", "chan"), None, None, None)
    maps = P("batch", None, None, "chan")
    convs = P(None, None, "batch", "chan")
    proj = P("batch", "chan")
    norms = P(None, "chan")
    states = (convs, convs, proj, norms)
    fused = mesh.shape["batch"] == 8 and mesh.shape["chan"] == 4
    return jax.shard_map(
        functools.partial(fused_body, 32) if fused else plain_body,
        mesh=mesh,
        in_specs=(images, images, maps, maps) + states * 3,
        out_specs=(maps, maps, images, images) + states * 4,
        check_vma=False,
    )
```

```python
import functools

import jax
import jax.numpy as jnp
from jax import lax
from jax.experimental import pallas as pl
from jax.experimental.pallas import tpu as pltpu
from jax.sharding import PartitionSpec as P

C_IN = 256
C_OUT = 512
STEP = 5
NORM_EPS = 1e-05
BETA_ONE = 0.5
BETA_TWO = 0.5
ADAM_EPS = 1e-08
DECAY = 0.01
NORM_RATE = 0.3
MESH = pl.DeviceIdType.MESH
BF16 = jnp.bfloat16
F32 = jnp.float32
COPIES = 240
VMEM_BYTES = 56 << 20


def silu_slope(values):
    gate = jax.nn.sigmoid(values)
    return gate * (1.0 + values * (1.0 - gate))


def adamw_step(weight, gradient, first, second, rate, decay):
    first_new = BETA_ONE * first + (1.0 - BETA_ONE) * gradient
    second_new = BETA_TWO * second + (1.0 - BETA_TWO) * gradient * gradient
    first_hat = first_new / (1.0 - BETA_ONE**STEP)
    second_hat = second_new / (1.0 - BETA_TWO**STEP)
    updated = weight - rate * (first_hat / (jnp.sqrt(second_hat) + ADAM_EPS) + decay * weight)
    return (updated, first_new, second_new)


def fold(values):
    rows, channels = values.shape
    return jnp.sum(values.reshape(rows // 8, 8, channels), axis=0)


def block_kernel(
    cfg,
    img_big, img_small, slo_big, slo_small, w1_hbm, w2_hbm, wp_hbm, norms_hbm,
    f1_hbm, f2_hbm, fp_hbm, fn_hbm, s1_hbm, s2_hbm, sp_hbm, sn_hbm,
    out_big, out_small, grad_big, grad_small, grad_one_out, grad_two_out, grad_norms,
    w1_in, w2_in, wp_in, norms_in, f1, f2, fp, fn, s1, s2, sp, sn,
    w1, w2, x_big, x_small, h_big, h_small, first_pre, second_pre, proj_pre, work, act,
    sl_big, sl_small, os_big, os_small, t_big, t_small, p_big, p_small, s_big, s_small,
    norms, norm_rows, stat_a, stat_b, a1, r1, rx1, ry1, rxx1, ryy1, c1, rz1,
    a2, r2, rx2, ry2, rxx2, ryy2, c2, rz2,
    send_sem, recv_sem, local_sem,
):
    nb_img, ns_img, ob, os_, number_big, number_small = cfg
    rows_b, rows_s = ob * ob * nb_img, os_ * os_ * ns_img
    step_b, step_s = ob * nb_img, os_ * ns_img
    b = lax.axis_index("batch")
    z = lax.axis_index("chan")
    core = lax.rem(b, 2)
    x = lax.rem(lax.div(b, 2), 2)
    y = lax.div(b, 4)
    x_peer = (b + 2 - 4 * x, z)
    y_peer = (b + 4 - 8 * y, z)
    sibling = (b + 1 - 2 * core, z)
    odd, upper = lax.rem(z, 2), lax.div(z, 2)
    pair_peer, cross_peer = (b, z + 1 - 2 * odd), (b, lax.rem(z + 2, 4))
    z_peers = [(b, lax.rem(z + d, 4)) for d in (1, 2, 3)]
    b_peers = [(lax.rem(b + d, 8), z) for d in range(1, 8)]
    lanes = lambda which: pl.ds(pl.multiple_of(which * 128, 128), 128)
    mine = lanes(z)

    used = [0]
    started = []

    def send(src, dst, peer):
        slot = used[0]
        used[0] += 1
        copy = pltpu.make_async_remote_copy(
            src_ref=src,
            dst_ref=dst,
            send_sem=send_sem.at[slot],
            recv_sem=recv_sem.at[slot],
            device_id=peer,
            device_id_type=MESH,
        )
        copy.start()
        started.append(copy)
        return copy

    barrier = pltpu.get_barrier_semaphore()
    for peer in b_peers + z_peers:
        pl.semaphore_signal(barrier, inc=1, device_id=peer, device_id_type=MESH)

    loads = []

    def load(src, dst):
        copy = pltpu.make_async_copy(src, dst, local_sem.at[len(loads)])
        copy.start()
        loads.append(copy)

    for source, held in ((w1_hbm, w1_in), (w2_hbm, w2_in), (wp_hbm, wp_in), (norms_hbm, norms_in)):
        load(source, held)
    for hp in range(2):
        for wp in range(2):
            load(img_big.at[:, hp, :, wp], x_big.at[hp, wp, pl.ds(hp, ob), pl.ds(wp, ob)])
            load(img_small.at[:, hp, :, wp], x_small.at[hp, wp, pl.ds(hp, os_), pl.ds(wp, os_)])
    load(
        slo_big.at[:, :, pl.ds(pl.multiple_of(z * nb_img, nb_img), nb_img)],
        sl_big.at[:, :, :, mine],
    )
    load(
        slo_small.at[:, :, pl.ds(pl.multiple_of(z * ns_img, ns_img), ns_img)],
        sl_small.at[:, :, :, mine],
    )
    for source, held in (
        (f1_hbm, f1), (f2_hbm, f2), (fp_hbm, fp), (fn_hbm, fn),
        (s1_hbm, s1), (s2_hbm, s2), (sp_hbm, sp), (sn_hbm, sn),
    ):
        load(source, held)
    for copy in loads[:4]:
        copy.wait()
    w1[0:9, y, x, core, :, mine] = w1_in[...].astype(BF16)
    w1[9, y, x, core, :, mine] = wp_in[...].astype(BF16)
    w2[:, y, x, core, :, mine] = w2_in[...].astype(BF16)
    norms[z, 0:6] = norms_in[...]

    pl.semaphore_wait(barrier, 10)

    def finish(copies):
        for copy in copies:
            copy.wait_recv()

    class Gather:
        def __init__(self, w, lo, n):
            self.w, self.taps = w, pl.ds(lo, n)
            piece = w.at[self.taps, y, x, core, :, mine]
            self.over_z = [send(piece, piece, peer) for peer in z_peers]

        def near(self):
            finish(self.over_z)
            piece = self.w.at[self.taps, y, x, core]
            self.x_copy = send(piece, piece, x_peer)
            self.y_copy = send(piece, piece, y_peer)
            self.rest = [send(piece, piece, sibling)]

        def far(self):
            self.x_copy.wait_recv()
            part = self.w.at[self.taps, y, 1 - x, core, :, pl.ds(0, 256)]
            self.far_a = send(part, part, y_peer)
            self.y_copy.wait_recv()
            part = self.w.at[self.taps, 1 - y, x, core, :, pl.ds(256, 256)]
            self.far_b = send(part, part, x_peer)
            piece = self.w.at[self.taps, y, 1 - x, core]
            self.rest.append(send(piece, piece, sibling))
            piece = self.w.at[self.taps, 1 - y, x, core]
            self.rest.append(send(piece, piece, sibling))

        def early(self, count):
            finish(self.rest[:count])
            self.rest = self.rest[count:]

        def last(self):
            finish([self.far_a, self.far_b])
            piece = self.w.at[self.taps, 1 - y, 1 - x, core]
            self.rest.append(send(piece, piece, sibling))

        def done(self):
            finish(self.rest)

    one_a = Gather(w1, 0, 3)
    z_norms = [send(norms.at[z], norms.at[z], peer) for peer in z_peers]
    one_b, one_c = Gather(w1, 3, 3), Gather(w1, 6, 4)
    two_a, two_b, two_c = (Gather(w2, lo, 3) for lo in (0, 3, 6))

    zero = functools.partial(jnp.zeros, dtype=BF16)
    for wp in range(2):
        x_big[1, wp, 0] = zero((ob + 1, nb_img, 256))
        x_small[1, wp, 0] = zero((os_ + 1, ns_img, 256))
    for hp in range(2):
        x_big[hp, 1, :, 0] = zero((ob + 1, nb_img, 256))
        x_small[hp, 1, :, 0] = zero((os_ + 1, ns_img, 256))
    for ref, side, images in (
        (h_big, ob, nb_img), (t_big, ob, nb_img), (h_small, os_, ns_img), (t_small, os_, ns_img),
    ):
        ref[0] = zero((side + 2, images, 512))
        ref[side + 1] = zero((side + 2, images, 512))
        ref[:, 0] = zero((side + 2, images, 512))
        ref[:, side + 1] = zero((side + 2, images, 512))
    for ref, side, images in ((s_big, ob, nb_img), (s_small, os_, ns_img)):
        ref[side] = zero((side + 1, images, 512))
        ref[:, side] = zero((side + 1, images, 512))

    def both(big, small):
        return jnp.concatenate([big.reshape(rows_b, -1), small.reshape(rows_s, -1)], axis=0)

    def x_window(ta, tb):
        hp, wp, sa, sb = (ta + 1) % 2, (tb + 1) % 2, ta // 2, tb // 2
        return both(
            x_big[hp, wp, sa : sa + ob, sb : sb + ob],
            x_small[hp, wp, sa : sa + os_, sb : sb + os_],
        )

    def h_window(ta, tb, depth=slice(None)):
        return both(
            h_big[ta : ta + ob, tb : tb + ob, :, depth],
            h_small[ta : ta + os_, tb : tb + os_, :, depth],
        )

    def t_window(ta, tb):
        ta, tb = 2 - ta, 2 - tb
        return both(t_big[ta : ta + ob, tb : tb + ob], t_small[ta : ta + os_, tb : tb + os_])

    def s_window(sa, sb):
        return both(s_big[sa : sa + ob, sb : sb + ob], s_small[sa : sa + os_, sb : sb + os_])

    def row_of(window, ta):
        return jnp.concatenate([window(ta, tb) for tb in range(3)], axis=1)

    def dot(left, right):
        return jnp.dot(left, right, preferred_element_type=F32)

    def dot_t(left, right):
        return lax.dot_general(left, right, (((1,), (1,)), ((), ())), preferred_element_type=F32)

    def dot_rows(left, right):
        return lax.dot_general(left, right, (((0,), (0,)), ((), ())), preferred_element_type=F32)

    slope_copies = []

    def slopes_over_z(source, target, lo, n, images):
        for d in (1, 2, 3):
            to = lax.rem(z + d, 4)
            rows = pl.ds(pl.multiple_of(to * images, images), images)
            slope_copies.append(
                send(source.at[pl.ds(lo, n), :, rows], target.at[pl.ds(lo, n), :, :, mine], (b, to))
            )

    big_parts = ((0, 4), (4, ob - 4))
    out_parts = ((0, 3), (3, 2), (5, ob - 5))
    one_a.near()
    one_b.near()
    one_a.far()
    one_c.near()
    one_b.far()
    one_c.far()
    two_a.near()
    one_a.last()
    one_b.last()
    one_c.last()
    two_b.near()
    slopes_over_z(slo_big, sl_big, *big_parts[0], nb_img)
    finish(z_norms)
    gains = [
        jnp.concatenate([norms[q, r : r + 1, :] for q in range(4)], axis=1) for r in range(6)
    ]
    for copy in loads[4:]:
        copy.wait()
    one_a.done()
    one_b.done()
    one_c.done()

    def reduce_start(k, rows):
        for r, row in enumerate(rows):
            stat_a[k, b, r : r + 1, :] = jnp.sum(row, axis=0, keepdims=True)
        part = stat_a.at[k, b, pl.ds(0, len(rows))]
        return [send(part, part, peer) for peer in b_peers]

    def reduce_middle(k, n, copies):
        finish(copies)
        stat_b[k, z, 0:n] = jnp.sum(stat_a[k, :, 0:n], axis=0)
        part = stat_b.at[k, z, pl.ds(0, n)]
        return [send(part, part, peer) for peer in z_peers]

    def reduce_end(k, n, copies):
        finish(copies)
        total = jnp.sum(stat_b[k, :, 0:n], axis=0)
        return [total[r : r + 1, :] for r in range(n)]

    def chunk_big(i):
        return pl.ds(pl.multiple_of(i * step_b, 16), step_b)

    def chunk_small(i):
        return pl.ds(pl.multiple_of(rows_b + i * step_s, 16), step_s)

    def over_groups(body, count):
        start = tuple(jnp.zeros((8, 512), F32) for _ in range(count))
        big = lax.fori_loop(0, ob, lambda i, c: body(0, i, chunk_big(i), c), start)
        small = lax.fori_loop(0, os_, lambda i, c: body(1, i, chunk_small(i), c), start)
        return big, small

    def moments(ref):
        def body(group, i, rows, carry):
            v = ref[rows, :]
            return (carry[0] + fold(v), carry[1] + fold(v * v))

        return over_groups(body, 2)

    def conv_row(ref, window, w, depth, ta):
        term = dot(row_of(window, ta), w[3 * ta : 3 * ta + 3].reshape(3 * depth, 512))
        if ta == 0:
            ref[...] = term
        else:
            ref[...] += term

    conv_row(first_pre, x_window, w1, 256, 0)
    conv_row(first_pre, x_window, w1, 256, 1)
    two_a.far()
    conv_row(first_pre, x_window, w1, 256, 2)
    first_big, first_small = moments(first_pre)
    copies = reduce_start(0, first_big + first_small)
    proj_pre[...] = dot(x_window(1, 1), w1[9].reshape(256, 512))
    side_big, side_small = moments(proj_pre)
    two_c.near()
    two_b.far()
    copies = reduce_middle(0, 4, copies)
    slopes_over_z(slo_big, sl_big, *big_parts[1], nb_img)
    slopes_over_z(slo_small, sl_small, 0, os_, ns_img)
    two_a.last()
    two_c.far()
    sums = reduce_end(0, 4, copies)

    def centered(total, square, number):
        center = total / number
        return center, lax.rsqrt(square / number - center * center + NORM_EPS)

    numbers = (number_big, number_small)
    first_stat = [centered(sums[2 * g], sums[2 * g + 1], numbers[g]) for g in range(2)]
    side_copies = reduce_start(4, side_big + side_small)

    def place(group, i, value, big, small, shift):
        if group == 0:
            big[i + shift, shift : shift + ob] = value.reshape(ob, nb_img, 512)
        else:
            small[i + shift, shift : shift + os_] = value.reshape(os_, ns_img, 512)

    def normed(ref, stat, rows):
        return (ref[rows, :] - stat[0]) * stat[1]

    def hide(group, i, rows, carry):
        value = normed(first_pre, first_stat[group], rows)
        first_pre[rows, :] = value
        shaped = value * gains[0] + gains[1]
        place(group, i, (shaped * jax.nn.sigmoid(shaped)).astype(BF16), h_big, h_small, 1)
        return carry

    over_groups(hide, 0)

    two_a.done()
    conv_row(second_pre, h_window, w2, 512, 0)
    two_b.last()

    def conv_last(blocks):
        pairs = [(tb, yy, xx) for tb in range(3) for yy, xx in blocks]
        second_pre[...] += dot(
            jnp.concatenate([h_window(2, tb, lanes(2 * yy + xx)) for tb, yy, xx in pairs], axis=1),
            jnp.concatenate([w2[6 + tb, yy, xx].reshape(128, 512) for tb, yy, xx in pairs], axis=0),
        )

    two_c.early(3)
    conv_last([(y, x), (y, 1 - x), (1 - y, x)])
    two_c.last()
    two_b.done()
    conv_row(second_pre, h_window, w2, 512, 1)
    side_copies = reduce_middle(4, 4, side_copies)
    two_c.done()
    conv_last([(1 - y, 1 - x)])
    second_big, second_small = moments(second_pre)
    copies = reduce_start(1, second_big + second_small)

    def prepare(group, i, rows, carry):
        act[rows, :] = silu_slope(first_pre[rows, :] * gains[0] + gains[1])
        return carry

    over_groups(prepare, 0)
    copies = reduce_middle(1, 4, copies)
    sums = reduce_end(4, 4, side_copies)
    side_stat = [centered(sums[2 * g], sums[2 * g + 1], numbers[g]) for g in range(2)]

    def prepare_side(group, i, rows, carry):
        proj_pre[rows, :] = normed(proj_pre, side_stat[group], rows)
        return carry

    over_groups(prepare_side, 0)
    finish(slope_copies)
    sums = reduce_end(1, 4, copies)
    second_stat = [centered(sums[2 * g], sums[2 * g + 1], numbers[g]) for g in range(2)]

    def outer(group, i, rows, carry):
        two = normed(second_pre, second_stat[group], rows)
        second_pre[rows, :] = two
        side = proj_pre[rows, :]
        summed = two * gains[2] + gains[3] + side * gains[4] + gains[5]
        gate = jax.nn.sigmoid(summed)
        place(group, i, (summed * gate).astype(BF16), os_big, os_small, 0)
        slope = sl_big[i] if group == 0 else sl_small[i]
        slope = slope.astype(F32).reshape(two.shape)
        upstream = slope * (gate * (1.0 + summed * (1.0 - gate)))
        work[rows, :] = upstream
        return (carry[0] + fold(upstream), carry[1] + fold(upstream * two), carry[2] + fold(upstream * side))

    outer_big, outer_small = over_groups(outer, 3)
    copies = reduce_start(2, outer_big + outer_small)
    stores = []

    def outputs_over_z(staged, target, lo, n, images):
        rows = pl.ds(pl.multiple_of(z * images, images), images)
        for d in (1, 2, 3):
            to = lax.rem(z + d, 4)
            stores.append(
                send(staged.at[pl.ds(lo, n), :, :, lanes(to)], target.at[pl.ds(lo, n), :, rows], (b, to))
            )

    copies = reduce_middle(2, 6, copies)
    outputs_over_z(os_small, out_small, 0, os_, ns_img)
    for staged, target, images in ((os_big, out_big, nb_img), (os_small, out_small, ns_img)):
        load(
            staged.at[:, :, :, mine],
            target.at[:, :, pl.ds(pl.multiple_of(z * images, images), images)],
        )
    sums_outer = reduce_end(2, 6, copies)
    outputs_over_z(os_big, out_big, *out_parts[0], nb_img)

    def slopes(group, i, rows, carry):
        total, cross_two, cross_side = sums_outer[3 * group : 3 * group + 3]
        number = numbers[group]
        base = work[rows, :] - total / number
        slope_two = gains[2] * second_stat[group][1] * (base - second_pre[rows, :] * (cross_two / number))
        place(group, i, slope_two.astype(BF16), t_big, t_small, 1)
        return carry

    def slopes_side(group, i, rows, carry):
        total, cross_two, cross_side = sums_outer[3 * group : 3 * group + 3]
        number = numbers[group]
        base = work[rows, :] - total / number
        slope_side = gains[4] * side_stat[group][1] * (base - proj_pre[rows, :] * (cross_side / number))
        place(group, i, slope_side.astype(BF16), p_big, p_small, 0)
        return carry

    over_groups(slopes, 0)

    class Scatter:
        def __init__(self, bufs, lo, n, pairs=False):
            self.bufs, self.taps, self.pairs = bufs, pl.ds(lo, n), pairs
            self.loop = lambda body: lax.fori_loop(lo, lo + n, lambda t, c: (body(t), c)[1], 0)
            a, r = bufs[0], bufs[1]
            self.copies = [send(a.at[self.taps, :, :, 1 - core], r.at[self.taps], sibling)]

        def near(self):
            finish(self.copies)
            a, r, rx, ry = self.bufs[:4]

            def add(t):
                r[t] = (r[t].astype(F32) + a[t, :, :, core].astype(F32)).astype(BF16)

            self.loop(add)
            taps = self.taps
            self.copies = [
                send(r.at[taps, :, 1 - x, :, pl.ds(0, 256)], rx.at[taps], x_peer),
                send(r.at[taps, 1 - y, :, :, pl.ds(256, 256)], ry.at[taps], y_peer),
            ]

        def far(self):
            finish(self.copies)
            _, r, rx, ry, rxx, ryy = self.bufs[:6]

            def add(t):
                rx[t] = (rx[t].astype(F32) + r[t, :, x, :, 0:256].astype(F32)).astype(BF16)
                ry[t] = (ry[t].astype(F32) + r[t, y, :, :, 256:512].astype(F32)).astype(BF16)

            self.loop(add)
            taps = self.taps
            self.copies = [
                send(rx.at[taps, 1 - y], ryy.at[taps], y_peer),
                send(ry.at[taps, 1 - x], rxx.at[taps], x_peer),
            ]

        def over_z(self):
            finish(self.copies)
            rx, ry, rxx, ryy, c, rz = self.bufs[2:8]

            def add(t):
                c[t, :, 0:256] = (rx[t, y].astype(F32) + ryy[t].astype(F32)).astype(BF16)
                c[t, :, 256:512] = (ry[t, x].astype(F32) + rxx[t].astype(F32)).astype(BF16)

            self.loop(add)
            to_z = lambda d: c.at[self.taps, :, lanes(lax.rem(z + d, 4))]
            if self.pairs:
                self.copies = [
                    send(c.at[self.taps, :, lanes(2 * far + 1 - odd)], rz.at[far, self.taps], pair_peer)
                    for far in range(2)
                ]
            else:
                self.copies = [
                    send(to_z(d), rz.at[d - 1, self.taps], (b, lax.rem(z + d, 4))) for d in (1, 2, 3)
                ]

        def cross(self):
            finish(self.copies)
            c, rz = self.bufs[6:8]

            def add(t):
                kept = c[t, :, lanes(2 * (1 - upper) + odd)].astype(F32)
                rz[1 - upper, t] = (rz[1 - upper, t].astype(F32) + kept).astype(BF16)

            self.loop(add)
            self.copies = [send(rz.at[1 - upper, self.taps], rz.at[2, self.taps], cross_peer)]

        def end(self):
            finish(self.copies)
            c, rz, out = self.bufs[6:]

            def add(t):
                total = c[t, :, mine].astype(F32)
                if self.pairs:
                    total = total + rz[upper, t].astype(F32) + rz[2, t].astype(F32)
                else:
                    for d in range(3):
                        total = total + rz[d, t].astype(F32)
                out[t] = total

            self.loop(add)

    t_flat = lambda: both(t_big[1 : ob + 1, 1 : ob + 1], t_small[1 : os_ + 1, 1 : os_ + 1])
    s_flat = lambda: both(s_big[0:ob, 0:ob], s_small[0:os_, 0:os_])
    p_flat = lambda: both(p_big[...], p_small[...])

    def grad_two(lo, n, pairs=False):
        for t in range(lo, lo + n):
            a2[t] = dot_rows(h_window(t // 3, t % 3), t_flat()).astype(BF16).reshape(a2.shape[1:])
        return Scatter((a2, r2, rx2, ry2, rxx2, ryy2, c2, rz2, grad_two_out), lo, n, pairs)

    one_bufs = (a1, r1, rx1, ry1, rxx1, ryy1, c1, rz1, grad_one_out)

    def grad_one(lo, n):
        windows = jnp.concatenate([x_window(t // 3, t % 3) for t in range(lo, lo + n)], axis=1)
        a1[lo : lo + n] = dot_rows(windows, s_flat()).astype(BF16).reshape((n,) + a1.shape[1:])
        return Scatter(one_bufs, lo, n)

    def grad_proj():
        a1[9] = dot_rows(x_window(1, 1), p_flat()).astype(BF16).reshape(a1.shape[1:])
        return Scatter(one_bufs, 9, 1)

    def back_row(ta):
        term = None
        for tb in range(3):
            part = dot_t(t_window(ta, tb), w2[3 * ta + tb].reshape(512, 512))
            term = part if term is None else term + part
        if ta == 0:
            second_pre[...] = term
        else:
            second_pre[...] += term

    sum_a = grad_two(0, 1)
    sum_b = grad_two(1, 2)
    sum_a.near()
    back_row(0)
    sum_b.near()
    back_row(1)
    sum_a.far()
    back_row(2)

    def inner(group, i, rows, carry):
        e = second_pre[rows, :] * act[rows, :]
        second_pre[rows, :] = e
        return (carry[0] + fold(e), carry[1] + fold(e * first_pre[rows, :]))

    inner_big, inner_small = over_groups(inner, 2)
    copies = reduce_start(3, inner_big + inner_small)
    sum_c = grad_two(3, 2)
    sum_b.far()
    sum_d = grad_two(5, 2)
    copies = reduce_middle(3, 4, copies)
    outputs_over_z(os_big, out_big, *out_parts[1], nb_img)
    sum_c.near()
    sum_e = grad_two(7, 2)
    sum_d.near()
    over_groups(slopes_side, 0)
    sums_inner = reduce_end(3, 4, copies)
    sum_a.over_z()
    sum_b.over_z()
    outputs_over_z(os_big, out_big, *out_parts[2], nb_img)

    def slopes_one(group, i, rows, carry):
        total, cross = sums_inner[2 * group : 2 * group + 2]
        number = numbers[group]
        slope = gains[0] * first_stat[group][1] * (
            second_pre[rows, :] - total / number - first_pre[rows, :] * (cross / number)
        )
        place(group, i, slope.astype(BF16), s_big, s_small, 0)
        return carry

    over_groups(slopes_one, 0)

    sum_f = grad_one(0, 2)
    sum_e.near()
    sum_c.far()
    sum_g = grad_one(2, 3)
    sum_f.near()
    sum_d.far()
    sum_p = grad_proj()
    sum_h = grad_one(5, 3)
    sum_g.near()
    sum_p.near()
    sum_c.over_z()
    sum_e.far()
    sum_i = grad_one(8, 1)
    sum_f.far()
    sum_h.near()
    sum_i.near()
    sum_d.over_z()

    def back_one(hp, wp):
        total = dot_t(p_flat(), w1[9].reshape(256, 512)) if hp + wp == 0 else None
        for ta in ((1,), (2, 0))[hp]:
            for tb in ((1,), (2, 0))[wp]:
                term = dot_t(
                    s_window(int(ta == 0), int(tb == 0)), w1[3 * ta + tb].reshape(256, 512)
                )
                total = term if total is None else total + term
        total = total.astype(BF16)
        grad_big[:, hp, :, wp] = total[:rows_b].reshape(ob, ob, nb_img, 256)
        grad_small[:, hp, :, wp] = total[rows_b:].reshape(os_, os_, ns_img, 256)

    back_one(0, 0)
    sum_g.far()
    sum_p.far()
    sum_e.over_z()
    back_one(0, 1)
    sum_f.over_z()
    sum_h.far()
    sum_i.far()
    back_one(1, 0)
    sum_p.over_z()
    sum_g.over_z()
    sum_h.over_z()
    sum_i.over_z()
    back_one(1, 1)
    rows = [
        sums_inner[1] + sums_inner[3],
        sums_inner[0] + sums_inner[2],
        sums_outer[1] + sums_outer[4],
        sums_outer[0] + sums_outer[3],
        sums_outer[2] + sums_outer[5],
        sums_outer[0] + sums_outer[3],
    ]
    for r, row in enumerate(rows):
        norm_rows[r : r + 1, :] = row
    grad_norms[...] = norm_rows[0:6, mine]
    sum_a.end()
    sum_b.end()
    sum_c.end()
    sum_d.end()
    sum_e.end()
    sum_f.end()
    sum_p.end()
    sum_g.end()
    sum_h.end()
    sum_i.end()
    finish(stores)
    for copy in loads[22:]:
        copy.wait()
    for copy in started:
        copy.wait_send()
    assert used[0] <= COPIES


def tap_window(padded, tap_row, tap_col, stride, size_out):
    reach = stride * (size_out - 1) + 1
    return lax.slice(
        padded,
        (0, tap_row, tap_col, 0),
        (padded.shape[0], tap_row + reach, tap_col + reach, padded.shape[3]),
        (1, stride, stride, 1),
    )


def conv_taps(inputs, kernel, stride):
    size_out = (inputs.shape[1] - 1) // stride + 1
    padded = jnp.pad(inputs, ((0, 0), (1, 1), (1, 1), (0, 0)))
    summed = jnp.zeros((inputs.shape[0], size_out, size_out, kernel.shape[3]), jnp.float32)
    for tap_row in range(3):
        for tap_col in range(3):
            window = tap_window(padded, tap_row, tap_col, stride, size_out)
            summed = summed + jnp.einsum(
                "nhwc,co->nhwo",
                window,
                kernel[tap_row, tap_col],
                preferred_element_type=jnp.float32,
            )
    return summed


def kernel_grad(inputs, slope, stride):
    size_out = slope.shape[1]
    padded = jnp.pad(inputs, ((0, 0), (1, 1), (1, 1), (0, 0)))
    tap_rows = []
    for tap_row in range(3):
        across = []
        for tap_col in range(3):
            window = tap_window(padded, tap_row, tap_col, stride, size_out)
            across.append(
                jnp.einsum("nhwc,nhwo->co", window, slope, preferred_element_type=jnp.float32)
            )
        tap_rows.append(jnp.stack(across))
    return jnp.stack(tap_rows)


def input_grad(slope, kernel, stride, size_in):
    size_out = slope.shape[1]
    full_size = size_in + 2
    reach = stride * (size_out - 1) + 1
    summed = jnp.zeros((slope.shape[0], full_size, full_size, kernel.shape[2]), jnp.float32)
    for tap_row in range(3):
        for tap_col in range(3):
            term = jnp.einsum(
                "nhwo,co->nhwc", slope, kernel[tap_row, tap_col], preferred_element_type=jnp.float32
            )
            summed = summed + lax.pad(
                term,
                jnp.float32(0.0),
                (
                    (0, 0, 0),
                    (tap_row, full_size - tap_row - reach, stride - 1),
                    (tap_col, full_size - tap_col - reach, stride - 1),
                    (0, 0, 0),
                ),
            )
    return summed[:, 1:-1, 1:-1, :]


def proj_input_grad(slope, kernel, size_in):
    term = jnp.einsum("nhwo,co->nhwc", slope, kernel, preferred_element_type=jnp.float32)
    margin = size_in - 2 * slope.shape[1] + 1
    return lax.pad(term, jnp.float32(0.0), ((0, 0, 0), (0, margin, 1), (0, margin, 1), (0, 0, 0)))


def moments(values):
    return (jnp.sum(values, axis=(0, 1, 2)), jnp.sum(values * values, axis=(0, 1, 2)))


def normalize(values, total, square_total, number):
    center = total / number
    factor = lax.rsqrt(square_total / number - center * center + NORM_EPS)
    return ((values - center) * factor, factor)


def norm_back(upstream, normed, factor, gain, total, cross, number):
    return gain * factor * (upstream - total / number - normed * (cross / number))


def plain_body(
    image_big,
    image_small,
    slope_big,
    slope_small,
    conv1_weight,
    conv2_weight,
    proj_weight,
    norm_params,
    first_conv1,
    first_conv2,
    first_proj,
    first_norms,
    second_conv1,
    second_conv2,
    second_proj,
    second_norms,
):
    bfloat = jnp.bfloat16
    kernel_one, kernel_two, kernel_proj = (
        lax.all_gather(conv1_weight.astype(bfloat), "batch", axis=2, tiled=True),
        lax.all_gather(conv2_weight.astype(bfloat), "batch", axis=2, tiled=True),
        lax.all_gather(proj_weight.astype(bfloat), "batch", axis=0, tiled=True),
    )
    inputs_big, inputs_small = (
        lax.all_gather(image_big, "chan", axis=0, tiled=True),
        lax.all_gather(image_small, "chan", axis=0, tiled=True),
    )
    groups = (inputs_big, inputs_small)
    batch_width = lax.axis_size("batch")
    first_pre = [conv_taps(images, kernel_one, 2) for images in groups]
    numbers = [
        values.shape[0] * values.shape[1] * values.shape[2] * batch_width for values in first_pre
    ]
    sum_big, square_big = moments(first_pre[0])
    sum_small, square_small = moments(first_pre[1])
    sum_big, square_big, sum_small, square_small = lax.psum(
        (sum_big, square_big, sum_small, square_small), "batch"
    )
    first_norm = [
        normalize(first_pre[0], sum_big, square_big, numbers[0]),
        normalize(first_pre[1], sum_small, square_small, numbers[1]),
    ]
    shaped = [normed * norm_params[0] + norm_params[1] for normed, factor in first_norm]
    hidden = [jax.nn.silu(values).astype(bfloat) for values in shaped]
    hidden_big, hidden_small = (
        lax.all_gather(hidden[0], "chan", axis=3, tiled=True),
        lax.all_gather(hidden[1], "chan", axis=3, tiled=True),
    )
    hidden_full = (hidden_big, hidden_small)
    second_pre = [conv_taps(values, kernel_two, 1) for values in hidden_full]
    proj_pre = [
        jnp.einsum(
            "nhwc,co->nhwo", images[:, ::2, ::2, :], kernel_proj, preferred_element_type=jnp.float32
        )
        for images in groups
    ]
    two_big, two_sq_big = moments(second_pre[0])
    two_small, two_sq_small = moments(second_pre[1])
    side_big, side_sq_big = moments(proj_pre[0])
    side_small, side_sq_small = moments(proj_pre[1])
    (
        two_big,
        two_sq_big,
        two_small,
        two_sq_small,
        side_big,
        side_sq_big,
        side_small,
        side_sq_small,
    ) = lax.psum(
        (
            two_big,
            two_sq_big,
            two_small,
            two_sq_small,
            side_big,
            side_sq_big,
            side_small,
            side_sq_small,
        ),
        "batch",
    )
    second_norm = [
        normalize(second_pre[0], two_big, two_sq_big, numbers[0]),
        normalize(second_pre[1], two_small, two_sq_small, numbers[1]),
    ]
    proj_norm = [
        normalize(proj_pre[0], side_big, side_sq_big, numbers[0]),
        normalize(proj_pre[1], side_small, side_sq_small, numbers[1]),
    ]
    summed = [
        second_norm[which][0] * norm_params[2]
        + norm_params[3]
        + proj_norm[which][0] * norm_params[4]
        + norm_params[5]
        for which in range(2)
    ]
    out_big = jax.nn.silu(summed[0]).astype(bfloat)
    out_small = jax.nn.silu(summed[1]).astype(bfloat)
    slopes = (slope_big, slope_small)
    upstream = [slopes[which].astype(jnp.float32) * silu_slope(summed[which]) for which in range(2)]
    outer_big = jnp.sum(upstream[0], axis=(0, 1, 2))
    cross_two_big = jnp.sum(upstream[0] * second_norm[0][0], axis=(0, 1, 2))
    cross_side_big = jnp.sum(upstream[0] * proj_norm[0][0], axis=(0, 1, 2))
    outer_small = jnp.sum(upstream[1], axis=(0, 1, 2))
    cross_two_small = jnp.sum(upstream[1] * second_norm[1][0], axis=(0, 1, 2))
    cross_side_small = jnp.sum(upstream[1] * proj_norm[1][0], axis=(0, 1, 2))
    outer_big, cross_two_big, cross_side_big, outer_small, cross_two_small, cross_side_small = (
        lax.psum(
            (
                outer_big,
                cross_two_big,
                cross_side_big,
                outer_small,
                cross_two_small,
                cross_side_small,
            ),
            "batch",
        )
    )
    outer_sums = (outer_big, outer_small)
    cross_two = (cross_two_big, cross_two_small)
    cross_side = (cross_side_big, cross_side_small)
    slope_two = [
        norm_back(
            upstream[which],
            second_norm[which][0],
            second_norm[which][1],
            norm_params[2],
            outer_sums[which],
            cross_two[which],
            numbers[which],
        ).astype(bfloat)
        for which in range(2)
    ]
    slope_proj = [
        norm_back(
            upstream[which],
            proj_norm[which][0],
            proj_norm[which][1],
            norm_params[4],
            outer_sums[which],
            cross_side[which],
            numbers[which],
        ).astype(bfloat)
        for which in range(2)
    ]
    part_big = input_grad(slope_two[0], kernel_two, 1, hidden_big.shape[1])
    part_small = input_grad(slope_two[1], kernel_two, 1, hidden_small.shape[1])
    back_big, back_small = (
        lax.psum_scatter(part_big, "chan", scatter_dimension=3, tiled=True),
        lax.psum_scatter(part_small, "chan", scatter_dimension=3, tiled=True),
    )
    inner = [back_big * silu_slope(shaped[0]), back_small * silu_slope(shaped[1])]
    inner_big = jnp.sum(inner[0], axis=(0, 1, 2))
    cross_one_big = jnp.sum(inner[0] * first_norm[0][0], axis=(0, 1, 2))
    inner_small = jnp.sum(inner[1], axis=(0, 1, 2))
    cross_one_small = jnp.sum(inner[1] * first_norm[1][0], axis=(0, 1, 2))
    inner_big, cross_one_big, inner_small, cross_one_small = lax.psum(
        (inner_big, cross_one_big, inner_small, cross_one_small), "batch"
    )
    inner_sums = (inner_big, inner_small)
    cross_one = (cross_one_big, cross_one_small)
    slope_one = [
        norm_back(
            inner[which],
            first_norm[which][0],
            first_norm[which][1],
            norm_params[0],
            inner_sums[which],
            cross_one[which],
            numbers[which],
        ).astype(bfloat)
        for which in range(2)
    ]
    size_big = image_big.shape[1]
    size_small = image_small.shape[1]
    input_part_big = input_grad(slope_one[0], kernel_one, 2, size_big) + proj_input_grad(
        slope_proj[0], kernel_proj, size_big
    )
    input_part_small = input_grad(slope_one[1], kernel_one, 2, size_small) + proj_input_grad(
        slope_proj[1], kernel_proj, size_small
    )
    grad_big, grad_small = (
        lax.psum_scatter(input_part_big, "chan", scatter_dimension=0, tiled=True),
        lax.psum_scatter(input_part_small, "chan", scatter_dimension=0, tiled=True),
    )
    part_conv1 = kernel_grad(groups[0], slope_one[0], 2) + kernel_grad(groups[1], slope_one[1], 2)
    part_conv2 = kernel_grad(hidden_full[0], slope_two[0], 1) + kernel_grad(
        hidden_full[1], slope_two[1], 1
    )
    part_proj = jnp.einsum(
        "nhwc,nhwo->co",
        groups[0][:, ::2, ::2, :],
        slope_proj[0],
        preferred_element_type=jnp.float32,
    ) + jnp.einsum(
        "nhwc,nhwo->co",
        groups[1][:, ::2, ::2, :],
        slope_proj[1],
        preferred_element_type=jnp.float32,
    )
    grad_conv1, grad_conv2, grad_proj = (
        lax.psum_scatter(part_conv1, "batch", scatter_dimension=2, tiled=True),
        lax.psum_scatter(part_conv2, "batch", scatter_dimension=2, tiled=True),
        lax.psum_scatter(part_proj, "batch", scatter_dimension=0, tiled=True),
    )
    grad_norms = jnp.stack(
        [
            cross_one_big + cross_one_small,
            inner_big + inner_small,
            cross_two_big + cross_two_small,
            outer_big + outer_small,
            cross_side_big + cross_side_small,
            outer_big + outer_small,
        ]
    )
    new_conv1, moment_conv1, square_conv1 = adamw_step(
        conv1_weight, grad_conv1, first_conv1, second_conv1, (9.0 * C_IN) ** (-0.5), DECAY
    )
    new_conv2, moment_conv2, square_conv2 = adamw_step(
        conv2_weight, grad_conv2, first_conv2, second_conv2, (9.0 * C_OUT) ** (-0.5), DECAY
    )
    new_proj, moment_proj, square_proj = adamw_step(
        proj_weight, grad_proj, first_proj, second_proj, (1.0 * C_IN) ** (-0.5), DECAY
    )
    new_norms, moment_norms, square_norms = adamw_step(
        norm_params, grad_norms, first_norms, second_norms, NORM_RATE, 0.0
    )
    return (
        out_big,
        out_small,
        grad_big.astype(bfloat),
        grad_small.astype(bfloat),
        grad_conv1,
        grad_conv2,
        grad_proj,
        grad_norms,
        new_conv1,
        new_conv2,
        new_proj,
        new_norms,
        moment_conv1,
        moment_conv2,
        moment_proj,
        moment_norms,
        square_conv1,
        square_conv2,
        square_proj,
        square_norms,
    )


def update_kernel(*refs):
    passed, sums, states, rest = refs[:4], refs[4:7], refs[7:19], refs[19:]
    passed_out, outs, (sem,) = rest[:4], rest[4:20], rest[20:]
    g1, g2, gn = sums
    copies = [
        pltpu.make_async_copy(src, dst, sem.at[i])
        for i, (src, dst) in enumerate(zip(passed, passed_out))
    ]
    for copy in copies:
        copy.start()
    grads = (g1[0:9], g2[...], g1[9], gn[...])
    rates = ((9.0 * C_IN) ** (-0.5), (9.0 * C_OUT) ** (-0.5), (1.0 * C_IN) ** (-0.5), NORM_RATE)
    for i in range(4):
        weight, first, second = (states[i + 4 * k][...] for k in range(3))
        new, moment, square = adamw_step(
            weight, grads[i], first, second, rates[i], DECAY if i < 3 else 0.0
        )
        for k, value in enumerate((grads[i], new, moment, square)):
            outs[i + 4 * k][...] = value
    for copy in copies:
        copy.wait()


def fused_body(
    devices,
    image_big, image_small, slope_big, slope_small,
    conv1_weight, conv2_weight, proj_weight, norm_params,
    first_conv1, first_conv2, first_proj, first_norms,
    second_conv1, second_conv2, second_proj, second_norms,
):
    nb_img, side_b = image_big.shape[0], image_big.shape[1]
    ns_img, side_s = image_small.shape[0], image_small.shape[1]
    ob, os_ = side_b // 2, side_s // 2
    rows = ob * ob * nb_img + os_ * os_ * ns_img
    cfg = (nb_img, ns_img, ob, os_, ob * ob * nb_img * devices, os_ * os_ * ns_img * devices)
    r1, r2 = conv1_weight.shape[2], conv2_weight.shape[2]

    def parity(images, side):
        images = jnp.transpose(images, (1, 2, 0, 3))
        return images.reshape(side // 2, 2, side // 2, 2, images.shape[2], C_IN)

    def flat(weight):
        return weight.reshape((9,) + weight.shape[2:])

    vmem = pl.BlockSpec(memory_space=pltpu.VMEM)
    anywhere = pl.BlockSpec(memory_space=pl.ANY)
    hbm = pl.BlockSpec(memory_space=pltpu.HBM)
    shape = jax.ShapeDtypeStruct
    out_shape = (
        pltpu.VMEM((ob, ob, slope_big.shape[0], 128), BF16),
        pltpu.VMEM((os_, os_, slope_small.shape[0], 128), BF16),
        pltpu.VMEM((ob, 2, ob, 2, nb_img, C_IN), BF16),
        pltpu.VMEM((os_, 2, os_, 2, ns_img, C_IN), BF16),
        pltpu.VMEM((10, r1, 128), F32),
        pltpu.VMEM((9, r2, 128), F32),
        pltpu.VMEM((6, 128), F32),
    ) + tuple(pltpu.VMEM(s, F32) for s in ((9, r1, 128), (9, r2, 128), (r1, 128), (6, 128)) * 3)

    def sum_buffers(taps, r):
        return [
            pltpu.VMEM((taps, 2, 2, 2, r, 512), BF16),
            pltpu.VMEM((taps, 2, 2, r, 512), BF16),
            pltpu.VMEM((taps, 2, r, 256), BF16),
            pltpu.VMEM((taps, 2, r, 256), BF16),
            pltpu.VMEM((taps, r, 256), BF16),
            pltpu.VMEM((taps, r, 256), BF16),
            pltpu.VMEM((taps, r, 512), BF16),
            pltpu.VMEM((3, taps, r, 128), BF16),
        ]

    def maps(extra):
        return [
            pltpu.VMEM((ob + extra, ob + extra, nb_img, 512), BF16),
            pltpu.VMEM((os_ + extra, os_ + extra, ns_img, 512), BF16),
        ]

    scratch = (
        [
            pltpu.VMEM((10, 2, 2, 2, r1, 512), BF16),
            pltpu.VMEM((9, 2, 2, 2, r2, 512), BF16),
            pltpu.VMEM((2, 2, ob + 1, ob + 1, nb_img, C_IN), BF16),
            pltpu.VMEM((2, 2, os_ + 1, os_ + 1, ns_img, C_IN), BF16),
        ]
        + maps(2)
        + [pltpu.VMEM((rows, 512), F32) for _ in range(5)]
        + maps(0)
        + maps(0)
        + maps(2)
        + maps(0)
        + maps(1)
        + [
            pltpu.VMEM((4, 8, 128), F32),
            pltpu.VMEM((8, 512), F32),
            pltpu.VMEM((5, 8, 8, 512), F32),
            pltpu.VMEM((5, 4, 8, 512), F32),
        ]
        + sum_buffers(10, r1)
        + sum_buffers(9, r2)
        + [
            pltpu.SemaphoreType.DMA((COPIES,)),
            pltpu.SemaphoreType.DMA((COPIES,)),
            pltpu.SemaphoreType.DMA((24,)),
        ]
    )
    macs = rows * 512 * (9 * C_IN + 9 * C_OUT + C_IN) * 3
    out_big, out_small, grad_big, grad_small, grad_one, grad_two, grad_norms, *states = pl.pallas_call(
        functools.partial(block_kernel, cfg),
        out_shape=out_shape,
        in_specs=[hbm] * 16,
        out_specs=[anywhere] * 2 + [vmem] * 17,
        scratch_shapes=scratch,
        compiler_params=pltpu.CompilerParams(
            collective_id=0, has_side_effects=True, vmem_limit_bytes=VMEM_BYTES
        ),
        cost_estimate=pl.CostEstimate(flops=2 * macs, bytes_accessed=1 << 23, transcendentals=rows * 2048),
    )(
        parity(image_big, side_b),
        parity(image_small, side_s),
        jnp.transpose(slope_big, (1, 2, 0, 3)),
        jnp.transpose(slope_small, (1, 2, 0, 3)),
        flat(conv1_weight),
        flat(conv2_weight),
        proj_weight,
        norm_params,
        flat(first_conv1),
        flat(first_conv2),
        first_proj,
        first_norms,
        flat(second_conv1),
        flat(second_conv2),
        second_proj,
        second_norms,
    )
    passed = (out_big, out_small, grad_big, grad_small)
    sums = (grad_one, grad_two, grad_norms)
    out_big, out_small, grad_big, grad_small, *updated = pl.pallas_call(
        update_kernel,
        out_shape=[shape(v.shape, v.dtype) for v in passed] + [shape(w.shape, F32) for w in states[:4]] * 4,
        in_specs=[vmem] * 19,
        out_specs=[anywhere] * 4 + [vmem] * 16,
        scratch_shapes=[pltpu.SemaphoreType.DMA((4,))],
        compiler_params=pltpu.CompilerParams(vmem_limit_bytes=16 << 20),
    )(
        *passed, *sums, *states,
    )
    updated = [
        value.reshape((3, 3) + value.shape[1:]) if value.ndim == 3 else value for value in updated
    ]

    def unparity(images, side):
        images = images.reshape(side, side, images.shape[4], C_IN)
        return jnp.transpose(images, (2, 0, 1, 3))

    return (
        jnp.transpose(out_big, (2, 0, 1, 3)),
        jnp.transpose(out_small, (2, 0, 1, 3)),
        unparity(grad_big, side_b),
        unparity(grad_small, side_s),
        *updated,
    )


def solution(mesh):
    images = P(("batch", "chan"), None, None, None)
    maps = P("batch", None, None, "chan")
    convs = P(None, None, "batch", "chan")
    proj = P("batch", "chan")
    norms = P(None, "chan")
    states = (convs, convs, proj, norms)
    fused = mesh.shape["batch"] == 8 and mesh.shape["chan"] == 4
    return jax.shard_map(
        functools.partial(fused_body, 32) if fused else plain_body,
        mesh=mesh,
        in_specs=(images, images, maps, maps) + states * 3,
        out_specs=(maps, maps, images, images) + states * 4,
        check_vma=False,
    )
```

```python
import functools

import jax
import jax.numpy as jnp
from jax import lax
from jax.experimental import pallas as pl
from jax.experimental.pallas import tpu as pltpu
from jax.sharding import PartitionSpec as P

C_IN = 256
C_OUT = 512
STEP = 5
NORM_EPS = 1e-05
BETA_ONE = 0.5
BETA_TWO = 0.5
ADAM_EPS = 1e-08
DECAY = 0.01
NORM_RATE = 0.3
MESH = pl.DeviceIdType.MESH
BF16 = jnp.bfloat16
F32 = jnp.float32
COPIES = 240
VMEM_BYTES = 56 << 20


def silu_slope(values):
    gate = jax.nn.sigmoid(values)
    return gate * (1.0 + values * (1.0 - gate))


def adamw_step(weight, gradient, first, second, rate, decay):
    first_new = BETA_ONE * first + (1.0 - BETA_ONE) * gradient
    second_new = BETA_TWO * second + (1.0 - BETA_TWO) * gradient * gradient
    first_hat = first_new / (1.0 - BETA_ONE**STEP)
    second_hat = second_new / (1.0 - BETA_TWO**STEP)
    updated = weight - rate * (first_hat / (jnp.sqrt(second_hat) + ADAM_EPS) + decay * weight)
    return (updated, first_new, second_new)


def fold(values):
    rows, channels = values.shape
    return jnp.sum(values.reshape(rows // 8, 8, channels), axis=0)


def block_kernel(
    cfg,
    img_big, img_small, slo_big, slo_small, w1_hbm, w2_hbm, wp_hbm, norms_hbm,
    f1_hbm, f2_hbm, fp_hbm, fn_hbm, s1_hbm, s2_hbm, sp_hbm, sn_hbm,
    out_big, out_small, grad_big, grad_small, grad_one_out, grad_two_out, grad_norms,
    w1_in, w2_in, wp_in, norms_in, f1, f2, fp, fn, s1, s2, sp, sn,
    w1, w2, x_big, x_small, h_big, h_small, first_pre, second_pre, proj_pre, work, act,
    sl_big, sl_small, os_big, os_small, t_big, t_small, p_big, p_small, s_big, s_small,
    norms, norm_rows, stat_a, stat_b, a1, r1, rx1, ry1, rxx1, ryy1, c1, rz1,
    a2, r2, rx2, ry2, rxx2, ryy2, c2, rz2,
    send_sem, recv_sem, local_sem,
):
    nb_img, ns_img, ob, os_, number_big, number_small = cfg
    rows_b, rows_s = ob * ob * nb_img, os_ * os_ * ns_img
    step_b, step_s = ob * nb_img, os_ * ns_img
    b = lax.axis_index("batch")
    z = lax.axis_index("chan")
    core = lax.rem(b, 2)
    x = lax.rem(lax.div(b, 2), 2)
    y = lax.div(b, 4)
    x_peer = (b + 2 - 4 * x, z)
    y_peer = (b + 4 - 8 * y, z)
    sibling = (b + 1 - 2 * core, z)
    odd, upper = lax.rem(z, 2), lax.div(z, 2)
    pair_peer, cross_peer = (b, z + 1 - 2 * odd), (b, lax.rem(z + 2, 4))
    z_peers = [(b, lax.rem(z + d, 4)) for d in (1, 2, 3)]
    b_peers = [(lax.rem(b + d, 8), z) for d in range(1, 8)]
    lanes = lambda which: pl.ds(pl.multiple_of(which * 128, 128), 128)
    mine = lanes(z)

    used = [0]
    started = []

    def send(src, dst, peer):
        slot = used[0]
        used[0] += 1
        copy = pltpu.make_async_remote_copy(
            src_ref=src,
            dst_ref=dst,
            send_sem=send_sem.at[slot],
            recv_sem=recv_sem.at[slot],
            device_id=peer,
            device_id_type=MESH,
        )
        copy.start()
        started.append(copy)
        return copy

    barrier = pltpu.get_barrier_semaphore()
    for peer in b_peers + z_peers:
        pl.semaphore_signal(barrier, inc=1, device_id=peer, device_id_type=MESH)

    loads = []

    def load(src, dst):
        copy = pltpu.make_async_copy(src, dst, local_sem.at[len(loads)])
        copy.start()
        loads.append(copy)

    for source, held in ((w1_hbm, w1_in), (w2_hbm, w2_in), (wp_hbm, wp_in), (norms_hbm, norms_in)):
        load(source, held)
    for hp in range(2):
        for wp in range(2):
            load(img_big.at[:, hp, :, wp], x_big.at[hp, wp, pl.ds(hp, ob), pl.ds(wp, ob)])
            load(img_small.at[:, hp, :, wp], x_small.at[hp, wp, pl.ds(hp, os_), pl.ds(wp, os_)])
    load(
        slo_big.at[:, :, pl.ds(pl.multiple_of(z * nb_img, nb_img), nb_img)],
        sl_big.at[:, :, :, mine],
    )
    load(
        slo_small.at[:, :, pl.ds(pl.multiple_of(z * ns_img, ns_img), ns_img)],
        sl_small.at[:, :, :, mine],
    )
    for source, held in (
        (f1_hbm, f1), (f2_hbm, f2), (fp_hbm, fp), (fn_hbm, fn),
        (s1_hbm, s1), (s2_hbm, s2), (sp_hbm, sp), (sn_hbm, sn),
    ):
        load(source, held)
    for copy in loads[:4]:
        copy.wait()
    w1[0:9, y, x, core, :, mine] = w1_in[...].astype(BF16)
    w1[9, y, x, core, :, mine] = wp_in[...].astype(BF16)
    w2[:, y, x, core, :, mine] = w2_in[...].astype(BF16)
    norms[z, 0:6] = norms_in[...]

    pl.semaphore_wait(barrier, 10)

    def finish(copies):
        for copy in copies:
            copy.wait_recv()

    class Gather:
        def __init__(self, w, lo, n):
            self.w, self.taps = w, pl.ds(lo, n)
            piece = w.at[self.taps, y, x, core, :, mine]
            self.over_z = [send(piece, piece, peer) for peer in z_peers]

        def near(self):
            finish(self.over_z)
            piece = self.w.at[self.taps, y, x, core]
            self.x_copy = send(piece, piece, x_peer)
            self.y_copy = send(piece, piece, y_peer)
            self.rest = [send(piece, piece, sibling)]

        def far(self):
            self.x_copy.wait_recv()
            part = self.w.at[self.taps, y, 1 - x, core, :, pl.ds(0, 256)]
            self.far_a = send(part, part, y_peer)
            self.y_copy.wait_recv()
            part = self.w.at[self.taps, 1 - y, x, core, :, pl.ds(256, 256)]
            self.far_b = send(part, part, x_peer)
            piece = self.w.at[self.taps, y, 1 - x, core]
            self.rest.append(send(piece, piece, sibling))
            piece = self.w.at[self.taps, 1 - y, x, core]
            self.rest.append(send(piece, piece, sibling))

        def early(self, count):
            finish(self.rest[:count])
            self.rest = self.rest[count:]

        def last(self):
            finish([self.far_a, self.far_b])
            piece = self.w.at[self.taps, 1 - y, 1 - x, core]
            self.rest.append(send(piece, piece, sibling))

        def done(self):
            finish(self.rest)

    one_a = Gather(w1, 0, 3)
    z_norms = [send(norms.at[z], norms.at[z], peer) for peer in z_peers]
    one_b, one_c = Gather(w1, 3, 3), Gather(w1, 6, 4)
    two_a, two_b, two_c = (Gather(w2, lo, 3) for lo in (0, 3, 6))

    zero = functools.partial(jnp.zeros, dtype=BF16)
    for wp in range(2):
        x_big[1, wp, 0] = zero((ob + 1, nb_img, 256))
        x_small[1, wp, 0] = zero((os_ + 1, ns_img, 256))
    for hp in range(2):
        x_big[hp, 1, :, 0] = zero((ob + 1, nb_img, 256))
        x_small[hp, 1, :, 0] = zero((os_ + 1, ns_img, 256))
    for ref, side, images in (
        (h_big, ob, nb_img), (t_big, ob, nb_img), (h_small, os_, ns_img), (t_small, os_, ns_img),
    ):
        ref[0] = zero((side + 2, images, 512))
        ref[side + 1] = zero((side + 2, images, 512))
        ref[:, 0] = zero((side + 2, images, 512))
        ref[:, side + 1] = zero((side + 2, images, 512))
    for ref, side, images in ((s_big, ob, nb_img), (s_small, os_, ns_img)):
        ref[side] = zero((side + 1, images, 512))
        ref[:, side] = zero((side + 1, images, 512))

    def both(big, small):
        return jnp.concatenate([big.reshape(rows_b, -1), small.reshape(rows_s, -1)], axis=0)

    def x_window(ta, tb):
        hp, wp, sa, sb = (ta + 1) % 2, (tb + 1) % 2, ta // 2, tb // 2
        return both(
            x_big[hp, wp, sa : sa + ob, sb : sb + ob],
            x_small[hp, wp, sa : sa + os_, sb : sb + os_],
        )

    def h_window(ta, tb, depth=slice(None)):
        return both(
            h_big[ta : ta + ob, tb : tb + ob, :, depth],
            h_small[ta : ta + os_, tb : tb + os_, :, depth],
        )

    def t_window(ta, tb):
        ta, tb = 2 - ta, 2 - tb
        return both(t_big[ta : ta + ob, tb : tb + ob], t_small[ta : ta + os_, tb : tb + os_])

    def s_window(sa, sb):
        return both(s_big[sa : sa + ob, sb : sb + ob], s_small[sa : sa + os_, sb : sb + os_])

    def row_of(window, ta):
        return jnp.concatenate([window(ta, tb) for tb in range(3)], axis=1)

    def dot(left, right):
        return jnp.dot(left, right, preferred_element_type=F32)

    def dot_t(left, right):
        return lax.dot_general(left, right, (((1,), (1,)), ((), ())), preferred_element_type=F32)

    def dot_rows(left, right):
        return lax.dot_general(left, right, (((0,), (0,)), ((), ())), preferred_element_type=F32)

    slope_copies = []

    def slopes_over_z(source, target, lo, n, images):
        for d in (1, 2, 3):
            to = lax.rem(z + d, 4)
            rows = pl.ds(pl.multiple_of(to * images, images), images)
            slope_copies.append(
                send(source.at[pl.ds(lo, n), :, rows], target.at[pl.ds(lo, n), :, :, mine], (b, to))
            )

    big_parts = ((0, 4), (4, ob - 4))
    out_parts = ((0, 3), (3, 2), (5, ob - 5))
    one_a.near()
    one_b.near()
    one_a.far()
    one_c.near()
    one_b.far()
    one_c.far()
    two_a.near()
    one_a.last()
    one_b.last()
    one_c.last()
    two_b.near()
    slopes_over_z(slo_big, sl_big, *big_parts[0], nb_img)
    finish(z_norms)
    gains = [
        jnp.concatenate([norms[q, r : r + 1, :] for q in range(4)], axis=1) for r in range(6)
    ]
    for copy in loads[4:]:
        copy.wait()
    one_a.done()
    one_b.done()
    one_c.done()

    def reduce_start(k, rows):
        for r, row in enumerate(rows):
            stat_a[k, b, r : r + 1, :] = jnp.sum(row, axis=0, keepdims=True)
        part = stat_a.at[k, b, pl.ds(0, len(rows))]
        return [send(part, part, peer) for peer in b_peers]

    def reduce_middle(k, n, copies):
        finish(copies)
        stat_b[k, z, 0:n] = jnp.sum(stat_a[k, :, 0:n], axis=0)
        part = stat_b.at[k, z, pl.ds(0, n)]
        return [send(part, part, peer) for peer in z_peers]

    def reduce_end(k, n, copies):
        finish(copies)
        total = jnp.sum(stat_b[k, :, 0:n], axis=0)
        return [total[r : r + 1, :] for r in range(n)]

    def chunk_big(i):
        return pl.ds(pl.multiple_of(i * step_b, 16), step_b)

    def chunk_small(i):
        return pl.ds(pl.multiple_of(rows_b + i * step_s, 16), step_s)

    def over_groups(body, count):
        start = tuple(jnp.zeros((8, 512), F32) for _ in range(count))
        big = lax.fori_loop(0, ob, lambda i, c: body(0, i, chunk_big(i), c), start)
        small = lax.fori_loop(0, os_, lambda i, c: body(1, i, chunk_small(i), c), start)
        return big, small

    def moments(ref):
        def body(group, i, rows, carry):
            v = ref[rows, :]
            return (carry[0] + fold(v), carry[1] + fold(v * v))

        return over_groups(body, 2)

    def conv_row(ref, window, w, depth, ta):
        term = dot(row_of(window, ta), w[3 * ta : 3 * ta + 3].reshape(3 * depth, 512))
        if ta == 0:
            ref[...] = term
        else:
            ref[...] += term

    conv_row(first_pre, x_window, w1, 256, 0)
    conv_row(first_pre, x_window, w1, 256, 1)
    two_a.far()
    conv_row(first_pre, x_window, w1, 256, 2)
    first_big, first_small = moments(first_pre)
    copies = reduce_start(0, first_big + first_small)
    proj_pre[...] = dot(x_window(1, 1), w1[9].reshape(256, 512))
    side_big, side_small = moments(proj_pre)
    two_c.near()
    two_b.far()
    copies = reduce_middle(0, 4, copies)
    slopes_over_z(slo_big, sl_big, *big_parts[1], nb_img)
    slopes_over_z(slo_small, sl_small, 0, os_, ns_img)
    two_a.last()
    two_c.far()
    sums = reduce_end(0, 4, copies)

    def centered(total, square, number):
        center = total / number
        return center, lax.rsqrt(square / number - center * center + NORM_EPS)

    numbers = (number_big, number_small)
    first_stat = [centered(sums[2 * g], sums[2 * g + 1], numbers[g]) for g in range(2)]
    side_copies = reduce_start(4, side_big + side_small)

    def place(group, i, value, big, small, shift):
        if group == 0:
            big[i + shift, shift : shift + ob] = value.reshape(ob, nb_img, 512)
        else:
            small[i + shift, shift : shift + os_] = value.reshape(os_, ns_img, 512)

    def normed(ref, stat, rows):
        return (ref[rows, :] - stat[0]) * stat[1]

    def hide(group, i, rows, carry):
        value = normed(first_pre, first_stat[group], rows)
        first_pre[rows, :] = value
        shaped = value * gains[0] + gains[1]
        place(group, i, (shaped * jax.nn.sigmoid(shaped)).astype(BF16), h_big, h_small, 1)
        return carry

    over_groups(hide, 0)

    two_a.done()
    conv_row(second_pre, h_window, w2, 512, 0)
    two_b.last()

    def conv_last(blocks):
        pairs = [(tb, yy, xx) for tb in range(3) for yy, xx in blocks]
        second_pre[...] += dot(
            jnp.concatenate([h_window(2, tb, lanes(2 * yy + xx)) for tb, yy, xx in pairs], axis=1),
            jnp.concatenate([w2[6 + tb, yy, xx].reshape(128, 512) for tb, yy, xx in pairs], axis=0),
        )

    two_c.early(3)
    conv_last([(y, x), (y, 1 - x), (1 - y, x)])
    two_c.last()
    two_b.done()
    conv_row(second_pre, h_window, w2, 512, 1)
    side_copies = reduce_middle(4, 4, side_copies)
    two_c.done()
    conv_last([(1 - y, 1 - x)])
    second_big, second_small = moments(second_pre)
    copies = reduce_start(1, second_big + second_small)

    def prepare(group, i, rows, carry):
        act[rows, :] = silu_slope(first_pre[rows, :] * gains[0] + gains[1])
        return carry

    over_groups(prepare, 0)
    copies = reduce_middle(1, 4, copies)
    sums = reduce_end(4, 4, side_copies)
    side_stat = [centered(sums[2 * g], sums[2 * g + 1], numbers[g]) for g in range(2)]

    def prepare_side(group, i, rows, carry):
        proj_pre[rows, :] = normed(proj_pre, side_stat[group], rows)
        return carry

    over_groups(prepare_side, 0)
    finish(slope_copies)
    sums = reduce_end(1, 4, copies)
    second_stat = [centered(sums[2 * g], sums[2 * g + 1], numbers[g]) for g in range(2)]

    def outer(group, i, rows, carry):
        two = normed(second_pre, second_stat[group], rows)
        second_pre[rows, :] = two
        side = proj_pre[rows, :]
        summed = two * gains[2] + gains[3] + side * gains[4] + gains[5]
        gate = jax.nn.sigmoid(summed)
        place(group, i, (summed * gate).astype(BF16), os_big, os_small, 0)
        slope = sl_big[i] if group == 0 else sl_small[i]
        slope = slope.astype(F32).reshape(two.shape)
        upstream = slope * (gate * (1.0 + summed * (1.0 - gate)))
        work[rows, :] = upstream
        return (carry[0] + fold(upstream), carry[1] + fold(upstream * two), carry[2] + fold(upstream * side))

    outer_big, outer_small = over_groups(outer, 3)
    copies = reduce_start(2, outer_big + outer_small)
    stores = []

    def outputs_over_z(staged, target, lo, n, images):
        rows = pl.ds(pl.multiple_of(z * images, images), images)
        for d in (1, 2, 3):
            to = lax.rem(z + d, 4)
            stores.append(
                send(staged.at[pl.ds(lo, n), :, :, lanes(to)], target.at[pl.ds(lo, n), :, rows], (b, to))
            )

    copies = reduce_middle(2, 6, copies)
    outputs_over_z(os_small, out_small, 0, os_, ns_img)
    for staged, target, images in ((os_big, out_big, nb_img), (os_small, out_small, ns_img)):
        load(
            staged.at[:, :, :, mine],
            target.at[:, :, pl.ds(pl.multiple_of(z * images, images), images)],
        )
    sums_outer = reduce_end(2, 6, copies)
    outputs_over_z(os_big, out_big, *out_parts[0], nb_img)

    def slopes(group, i, rows, carry):
        total, cross_two, cross_side = sums_outer[3 * group : 3 * group + 3]
        number = numbers[group]
        base = work[rows, :] - total / number
        slope_two = gains[2] * second_stat[group][1] * (base - second_pre[rows, :] * (cross_two / number))
        place(group, i, slope_two.astype(BF16), t_big, t_small, 1)
        return carry

    def slopes_side(group, i, rows, carry):
        total, cross_two, cross_side = sums_outer[3 * group : 3 * group + 3]
        number = numbers[group]
        base = work[rows, :] - total / number
        slope_side = gains[4] * side_stat[group][1] * (base - proj_pre[rows, :] * (cross_side / number))
        place(group, i, slope_side.astype(BF16), p_big, p_small, 0)
        return carry

    over_groups(slopes, 0)

    class Scatter:
        def __init__(self, bufs, lo, n, pairs=False):
            self.bufs, self.taps, self.pairs = bufs, pl.ds(lo, n), pairs
            self.loop = lambda body: lax.fori_loop(lo, lo + n, lambda t, c: (body(t), c)[1], 0)
            a, r = bufs[0], bufs[1]
            self.copies = [send(a.at[self.taps, :, :, 1 - core], r.at[self.taps], sibling)]

        def near(self):
            finish(self.copies)
            a, r, rx, ry = self.bufs[:4]

            def add(t):
                r[t] = (r[t].astype(F32) + a[t, :, :, core].astype(F32)).astype(BF16)

            self.loop(add)
            taps = self.taps
            self.copies = [
                send(r.at[taps, :, 1 - x, :, pl.ds(0, 256)], rx.at[taps], x_peer),
                send(r.at[taps, 1 - y, :, :, pl.ds(256, 256)], ry.at[taps], y_peer),
            ]

        def far(self):
            finish(self.copies)
            _, r, rx, ry, rxx, ryy = self.bufs[:6]

            def add(t):
                rx[t] = (rx[t].astype(F32) + r[t, :, x, :, 0:256].astype(F32)).astype(BF16)
                ry[t] = (ry[t].astype(F32) + r[t, y, :, :, 256:512].astype(F32)).astype(BF16)

            self.loop(add)
            taps = self.taps
            self.copies = [
                send(rx.at[taps, 1 - y], ryy.at[taps], y_peer),
                send(ry.at[taps, 1 - x], rxx.at[taps], x_peer),
            ]

        def over_z(self):
            finish(self.copies)
            rx, ry, rxx, ryy, c, rz = self.bufs[2:8]

            def add(t):
                c[t, :, 0:256] = (rx[t, y].astype(F32) + ryy[t].astype(F32)).astype(BF16)
                c[t, :, 256:512] = (ry[t, x].astype(F32) + rxx[t].astype(F32)).astype(BF16)

            self.loop(add)
            to_z = lambda d: c.at[self.taps, :, lanes(lax.rem(z + d, 4))]
            if self.pairs:
                self.copies = [
                    send(c.at[self.taps, :, lanes(2 * far + 1 - odd)], rz.at[far, self.taps], pair_peer)
                    for far in range(2)
                ]
            else:
                self.copies = [
                    send(to_z(d), rz.at[d - 1, self.taps], (b, lax.rem(z + d, 4))) for d in (1, 2, 3)
                ]

        def cross(self):
            finish(self.copies)
            c, rz = self.bufs[6:8]

            def add(t):
                kept = c[t, :, lanes(2 * (1 - upper) + odd)].astype(F32)
                rz[1 - upper, t] = (rz[1 - upper, t].astype(F32) + kept).astype(BF16)

            self.loop(add)
            self.copies = [send(rz.at[1 - upper, self.taps], rz.at[2, self.taps], cross_peer)]

        def end(self):
            finish(self.copies)
            c, rz, out = self.bufs[6:]

            def add(t):
                total = c[t, :, mine].astype(F32)
                if self.pairs:
                    total = total + rz[upper, t].astype(F32) + rz[2, t].astype(F32)
                else:
                    for d in range(3):
                        total = total + rz[d, t].astype(F32)
                out[t] = total

            self.loop(add)

    t_flat = lambda: both(t_big[1 : ob + 1, 1 : ob + 1], t_small[1 : os_ + 1, 1 : os_ + 1])
    s_flat = lambda: both(s_big[0:ob, 0:ob], s_small[0:os_, 0:os_])
    p_flat = lambda: both(p_big[...], p_small[...])

    def grad_two(lo, n, pairs=False):
        for t in range(lo, lo + n):
            a2[t] = dot_rows(h_window(t // 3, t % 3), t_flat()).astype(BF16).reshape(a2.shape[1:])
        return Scatter((a2, r2, rx2, ry2, rxx2, ryy2, c2, rz2, grad_two_out), lo, n, pairs)

    one_bufs = (a1, r1, rx1, ry1, rxx1, ryy1, c1, rz1, grad_one_out)

    def grad_one(lo, n):
        windows = jnp.concatenate([x_window(t // 3, t % 3) for t in range(lo, lo + n)], axis=1)
        a1[lo : lo + n] = dot_rows(windows, s_flat()).astype(BF16).reshape((n,) + a1.shape[1:])
        return Scatter(one_bufs, lo, n)

    def grad_proj():
        a1[9] = dot_rows(x_window(1, 1), p_flat()).astype(BF16).reshape(a1.shape[1:])
        return Scatter(one_bufs, 9, 1)

    def back_row(ta):
        term = None
        for tb in range(3):
            part = dot_t(t_window(ta, tb), w2[3 * ta + tb].reshape(512, 512))
            term = part if term is None else term + part
        if ta == 0:
            second_pre[...] = term
        else:
            second_pre[...] += term

    sum_a = grad_two(0, 1)
    sum_b = grad_two(1, 2)
    sum_a.near()
    back_row(0)
    sum_b.near()
    back_row(1)
    sum_a.far()
    back_row(2)

    def inner(group, i, rows, carry):
        e = second_pre[rows, :] * act[rows, :]
        second_pre[rows, :] = e
        return (carry[0] + fold(e), carry[1] + fold(e * first_pre[rows, :]))

    inner_big, inner_small = over_groups(inner, 2)
    copies = reduce_start(3, inner_big + inner_small)
    sum_c = grad_two(3, 2)
    sum_b.far()
    sum_d = grad_two(5, 2)
    copies = reduce_middle(3, 4, copies)
    outputs_over_z(os_big, out_big, *out_parts[1], nb_img)
    sum_c.near()
    sum_e = grad_two(7, 2)
    sum_d.near()
    over_groups(slopes_side, 0)
    sums_inner = reduce_end(3, 4, copies)
    sum_a.over_z()
    sum_b.over_z()
    outputs_over_z(os_big, out_big, *out_parts[2], nb_img)

    def slopes_one(group, i, rows, carry):
        total, cross = sums_inner[2 * group : 2 * group + 2]
        number = numbers[group]
        slope = gains[0] * first_stat[group][1] * (
            second_pre[rows, :] - total / number - first_pre[rows, :] * (cross / number)
        )
        place(group, i, slope.astype(BF16), s_big, s_small, 0)
        return carry

    over_groups(slopes_one, 0)

    sum_f = grad_one(0, 2)
    sum_e.near()
    sum_c.far()
    sum_g = grad_one(2, 3)
    sum_f.near()
    sum_d.far()
    sum_p = grad_proj()
    sum_h = grad_one(5, 3)
    sum_g.near()
    sum_p.near()
    sum_c.over_z()
    sum_e.far()
    sum_i = grad_one(8, 1)
    sum_f.far()
    sum_h.near()
    sum_i.near()
    sum_d.over_z()

    def back_one(hp, wp):
        total = dot_t(p_flat(), w1[9].reshape(256, 512)) if hp + wp == 0 else None
        for ta in ((1,), (2, 0))[hp]:
            for tb in ((1,), (2, 0))[wp]:
                term = dot_t(
                    s_window(int(ta == 0), int(tb == 0)), w1[3 * ta + tb].reshape(256, 512)
                )
                total = term if total is None else total + term
        total = total.astype(BF16)
        grad_big[:, hp, :, wp] = total[:rows_b].reshape(ob, ob, nb_img, 256)
        grad_small[:, hp, :, wp] = total[rows_b:].reshape(os_, os_, ns_img, 256)

    back_one(0, 0)
    sum_g.far()
    sum_p.far()
    sum_e.over_z()
    back_one(0, 1)
    sum_f.over_z()
    sum_h.far()
    sum_i.far()
    back_one(1, 0)
    sum_p.over_z()
    sum_g.over_z()
    sum_h.over_z()
    sum_i.over_z()
    back_one(1, 1)
    rows = [
        sums_inner[1] + sums_inner[3],
        sums_inner[0] + sums_inner[2],
        sums_outer[1] + sums_outer[4],
        sums_outer[0] + sums_outer[3],
        sums_outer[2] + sums_outer[5],
        sums_outer[0] + sums_outer[3],
    ]
    for r, row in enumerate(rows):
        norm_rows[r : r + 1, :] = row
    grad_norms[...] = norm_rows[0:6, mine]
    early = len(started) - 40
    for copy in started[:early]:
        copy.wait_send()
    sum_a.end()
    sum_b.end()
    sum_c.end()
    sum_d.end()
    sum_e.end()
    sum_f.end()
    sum_p.end()
    sum_g.end()
    sum_h.end()
    sum_i.end()
    finish(stores)
    for copy in loads[22:]:
        copy.wait()
    for copy in started[early:]:
        copy.wait_send()
    assert used[0] <= COPIES


def tap_window(padded, tap_row, tap_col, stride, size_out):
    reach = stride * (size_out - 1) + 1
    return lax.slice(
        padded,
        (0, tap_row, tap_col, 0),
        (padded.shape[0], tap_row + reach, tap_col + reach, padded.shape[3]),
        (1, stride, stride, 1),
    )


def conv_taps(inputs, kernel, stride):
    size_out = (inputs.shape[1] - 1) // stride + 1
    padded = jnp.pad(inputs, ((0, 0), (1, 1), (1, 1), (0, 0)))
    summed = jnp.zeros((inputs.shape[0], size_out, size_out, kernel.shape[3]), jnp.float32)
    for tap_row in range(3):
        for tap_col in range(3):
            window = tap_window(padded, tap_row, tap_col, stride, size_out)
            summed = summed + jnp.einsum(
                "nhwc,co->nhwo",
                window,
                kernel[tap_row, tap_col],
                preferred_element_type=jnp.float32,
            )
    return summed


def kernel_grad(inputs, slope, stride):
    size_out = slope.shape[1]
    padded = jnp.pad(inputs, ((0, 0), (1, 1), (1, 1), (0, 0)))
    tap_rows = []
    for tap_row in range(3):
        across = []
        for tap_col in range(3):
            window = tap_window(padded, tap_row, tap_col, stride, size_out)
            across.append(
                jnp.einsum("nhwc,nhwo->co", window, slope, preferred_element_type=jnp.float32)
            )
        tap_rows.append(jnp.stack(across))
    return jnp.stack(tap_rows)


def input_grad(slope, kernel, stride, size_in):
    size_out = slope.shape[1]
    full_size = size_in + 2
    reach = stride * (size_out - 1) + 1
    summed = jnp.zeros((slope.shape[0], full_size, full_size, kernel.shape[2]), jnp.float32)
    for tap_row in range(3):
        for tap_col in range(3):
            term = jnp.einsum(
                "nhwo,co->nhwc", slope, kernel[tap_row, tap_col], preferred_element_type=jnp.float32
            )
            summed = summed + lax.pad(
                term,
                jnp.float32(0.0),
                (
                    (0, 0, 0),
                    (tap_row, full_size - tap_row - reach, stride - 1),
                    (tap_col, full_size - tap_col - reach, stride - 1),
                    (0, 0, 0),
                ),
            )
    return summed[:, 1:-1, 1:-1, :]


def proj_input_grad(slope, kernel, size_in):
    term = jnp.einsum("nhwo,co->nhwc", slope, kernel, preferred_element_type=jnp.float32)
    margin = size_in - 2 * slope.shape[1] + 1
    return lax.pad(term, jnp.float32(0.0), ((0, 0, 0), (0, margin, 1), (0, margin, 1), (0, 0, 0)))


def moments(values):
    return (jnp.sum(values, axis=(0, 1, 2)), jnp.sum(values * values, axis=(0, 1, 2)))


def normalize(values, total, square_total, number):
    center = total / number
    factor = lax.rsqrt(square_total / number - center * center + NORM_EPS)
    return ((values - center) * factor, factor)


def norm_back(upstream, normed, factor, gain, total, cross, number):
    return gain * factor * (upstream - total / number - normed * (cross / number))


def plain_body(
    image_big,
    image_small,
    slope_big,
    slope_small,
    conv1_weight,
    conv2_weight,
    proj_weight,
    norm_params,
    first_conv1,
    first_conv2,
    first_proj,
    first_norms,
    second_conv1,
    second_conv2,
    second_proj,
    second_norms,
):
    bfloat = jnp.bfloat16
    kernel_one, kernel_two, kernel_proj = (
        lax.all_gather(conv1_weight.astype(bfloat), "batch", axis=2, tiled=True),
        lax.all_gather(conv2_weight.astype(bfloat), "batch", axis=2, tiled=True),
        lax.all_gather(proj_weight.astype(bfloat), "batch", axis=0, tiled=True),
    )
    inputs_big, inputs_small = (
        lax.all_gather(image_big, "chan", axis=0, tiled=True),
        lax.all_gather(image_small, "chan", axis=0, tiled=True),
    )
    groups = (inputs_big, inputs_small)
    batch_width = lax.axis_size("batch")
    first_pre = [conv_taps(images, kernel_one, 2) for images in groups]
    numbers = [
        values.shape[0] * values.shape[1] * values.shape[2] * batch_width for values in first_pre
    ]
    sum_big, square_big = moments(first_pre[0])
    sum_small, square_small = moments(first_pre[1])
    sum_big, square_big, sum_small, square_small = lax.psum(
        (sum_big, square_big, sum_small, square_small), "batch"
    )
    first_norm = [
        normalize(first_pre[0], sum_big, square_big, numbers[0]),
        normalize(first_pre[1], sum_small, square_small, numbers[1]),
    ]
    shaped = [normed * norm_params[0] + norm_params[1] for normed, factor in first_norm]
    hidden = [jax.nn.silu(values).astype(bfloat) for values in shaped]
    hidden_big, hidden_small = (
        lax.all_gather(hidden[0], "chan", axis=3, tiled=True),
        lax.all_gather(hidden[1], "chan", axis=3, tiled=True),
    )
    hidden_full = (hidden_big, hidden_small)
    second_pre = [conv_taps(values, kernel_two, 1) for values in hidden_full]
    proj_pre = [
        jnp.einsum(
            "nhwc,co->nhwo", images[:, ::2, ::2, :], kernel_proj, preferred_element_type=jnp.float32
        )
        for images in groups
    ]
    two_big, two_sq_big = moments(second_pre[0])
    two_small, two_sq_small = moments(second_pre[1])
    side_big, side_sq_big = moments(proj_pre[0])
    side_small, side_sq_small = moments(proj_pre[1])
    (
        two_big,
        two_sq_big,
        two_small,
        two_sq_small,
        side_big,
        side_sq_big,
        side_small,
        side_sq_small,
    ) = lax.psum(
        (
            two_big,
            two_sq_big,
            two_small,
            two_sq_small,
            side_big,
            side_sq_big,
            side_small,
            side_sq_small,
        ),
        "batch",
    )
    second_norm = [
        normalize(second_pre[0], two_big, two_sq_big, numbers[0]),
        normalize(second_pre[1], two_small, two_sq_small, numbers[1]),
    ]
    proj_norm = [
        normalize(proj_pre[0], side_big, side_sq_big, numbers[0]),
        normalize(proj_pre[1], side_small, side_sq_small, numbers[1]),
    ]
    summed = [
        second_norm[which][0] * norm_params[2]
        + norm_params[3]
        + proj_norm[which][0] * norm_params[4]
        + norm_params[5]
        for which in range(2)
    ]
    out_big = jax.nn.silu(summed[0]).astype(bfloat)
    out_small = jax.nn.silu(summed[1]).astype(bfloat)
    slopes = (slope_big, slope_small)
    upstream = [slopes[which].astype(jnp.float32) * silu_slope(summed[which]) for which in range(2)]
    outer_big = jnp.sum(upstream[0], axis=(0, 1, 2))
    cross_two_big = jnp.sum(upstream[0] * second_norm[0][0], axis=(0, 1, 2))
    cross_side_big = jnp.sum(upstream[0] * proj_norm[0][0], axis=(0, 1, 2))
    outer_small = jnp.sum(upstream[1], axis=(0, 1, 2))
    cross_two_small = jnp.sum(upstream[1] * second_norm[1][0], axis=(0, 1, 2))
    cross_side_small = jnp.sum(upstream[1] * proj_norm[1][0], axis=(0, 1, 2))
    outer_big, cross_two_big, cross_side_big, outer_small, cross_two_small, cross_side_small = (
        lax.psum(
            (
                outer_big,
                cross_two_big,
                cross_side_big,
                outer_small,
                cross_two_small,
                cross_side_small,
            ),
            "batch",
        )
    )
    outer_sums = (outer_big, outer_small)
    cross_two = (cross_two_big, cross_two_small)
    cross_side = (cross_side_big, cross_side_small)
    slope_two = [
        norm_back(
            upstream[which],
            second_norm[which][0],
            second_norm[which][1],
            norm_params[2],
            outer_sums[which],
            cross_two[which],
            numbers[which],
        ).astype(bfloat)
        for which in range(2)
    ]
    slope_proj = [
        norm_back(
            upstream[which],
            proj_norm[which][0],
            proj_norm[which][1],
            norm_params[4],
            outer_sums[which],
            cross_side[which],
            numbers[which],
        ).astype(bfloat)
        for which in range(2)
    ]
    part_big = input_grad(slope_two[0], kernel_two, 1, hidden_big.shape[1])
    part_small = input_grad(slope_two[1], kernel_two, 1, hidden_small.shape[1])
    back_big, back_small = (
        lax.psum_scatter(part_big, "chan", scatter_dimension=3, tiled=True),
        lax.psum_scatter(part_small, "chan", scatter_dimension=3, tiled=True),
    )
    inner = [back_big * silu_slope(shaped[0]), back_small * silu_slope(shaped[1])]
    inner_big = jnp.sum(inner[0], axis=(0, 1, 2))
    cross_one_big = jnp.sum(inner[0] * first_norm[0][0], axis=(0, 1, 2))
    inner_small = jnp.sum(inner[1], axis=(0, 1, 2))
    cross_one_small = jnp.sum(inner[1] * first_norm[1][0], axis=(0, 1, 2))
    inner_big, cross_one_big, inner_small, cross_one_small = lax.psum(
        (inner_big, cross_one_big, inner_small, cross_one_small), "batch"
    )
    inner_sums = (inner_big, inner_small)
    cross_one = (cross_one_big, cross_one_small)
    slope_one = [
        norm_back(
            inner[which],
            first_norm[which][0],
            first_norm[which][1],
            norm_params[0],
            inner_sums[which],
            cross_one[which],
            numbers[which],
        ).astype(bfloat)
        for which in range(2)
    ]
    size_big = image_big.shape[1]
    size_small = image_small.shape[1]
    input_part_big = input_grad(slope_one[0], kernel_one, 2, size_big) + proj_input_grad(
        slope_proj[0], kernel_proj, size_big
    )
    input_part_small = input_grad(slope_one[1], kernel_one, 2, size_small) + proj_input_grad(
        slope_proj[1], kernel_proj, size_small
    )
    grad_big, grad_small = (
        lax.psum_scatter(input_part_big, "chan", scatter_dimension=0, tiled=True),
        lax.psum_scatter(input_part_small, "chan", scatter_dimension=0, tiled=True),
    )
    part_conv1 = kernel_grad(groups[0], slope_one[0], 2) + kernel_grad(groups[1], slope_one[1], 2)
    part_conv2 = kernel_grad(hidden_full[0], slope_two[0], 1) + kernel_grad(
        hidden_full[1], slope_two[1], 1
    )
    part_proj = jnp.einsum(
        "nhwc,nhwo->co",
        groups[0][:, ::2, ::2, :],
        slope_proj[0],
        preferred_element_type=jnp.float32,
    ) + jnp.einsum(
        "nhwc,nhwo->co",
        groups[1][:, ::2, ::2, :],
        slope_proj[1],
        preferred_element_type=jnp.float32,
    )
    grad_conv1, grad_conv2, grad_proj = (
        lax.psum_scatter(part_conv1, "batch", scatter_dimension=2, tiled=True),
        lax.psum_scatter(part_conv2, "batch", scatter_dimension=2, tiled=True),
        lax.psum_scatter(part_proj, "batch", scatter_dimension=0, tiled=True),
    )
    grad_norms = jnp.stack(
        [
            cross_one_big + cross_one_small,
            inner_big + inner_small,
            cross_two_big + cross_two_small,
            outer_big + outer_small,
            cross_side_big + cross_side_small,
            outer_big + outer_small,
        ]
    )
    new_conv1, moment_conv1, square_conv1 = adamw_step(
        conv1_weight, grad_conv1, first_conv1, second_conv1, (9.0 * C_IN) ** (-0.5), DECAY
    )
    new_conv2, moment_conv2, square_conv2 = adamw_step(
        conv2_weight, grad_conv2, first_conv2, second_conv2, (9.0 * C_OUT) ** (-0.5), DECAY
    )
    new_proj, moment_proj, square_proj = adamw_step(
        proj_weight, grad_proj, first_proj, second_proj, (1.0 * C_IN) ** (-0.5), DECAY
    )
    new_norms, moment_norms, square_norms = adamw_step(
        norm_params, grad_norms, first_norms, second_norms, NORM_RATE, 0.0
    )
    return (
        out_big,
        out_small,
        grad_big.astype(bfloat),
        grad_small.astype(bfloat),
        grad_conv1,
        grad_conv2,
        grad_proj,
        grad_norms,
        new_conv1,
        new_conv2,
        new_proj,
        new_norms,
        moment_conv1,
        moment_conv2,
        moment_proj,
        moment_norms,
        square_conv1,
        square_conv2,
        square_proj,
        square_norms,
    )


def update_kernel(*refs):
    passed, (g1, g2, gn), states, rest = refs[:4], refs[4:7], refs[7:19], refs[19:]
    passed_out, outs, made, sem = rest[:4], rest[4:20], rest[20:32], rest[32]
    gradients = (g1.at[pl.ds(0, 9)], g2, g1.at[9], gn)
    copies = []

    def store(src, dst):
        copy = pltpu.make_async_copy(src, dst, sem.at[len(copies)])
        copy.start()
        copies.append(copy)

    for src, dst in zip(passed + gradients, passed_out + outs[:4]):
        store(src, dst)
    rates = ((9.0 * C_IN) ** (-0.5), (9.0 * C_OUT) ** (-0.5), (1.0 * C_IN) ** (-0.5), NORM_RATE)
    for i in range(4):
        weight, first, second = (states[i + 4 * k][...] for k in range(3))
        values = adamw_step(
            weight, gradients[i][...], first, second, rates[i], DECAY if i < 3 else 0.0
        )
        for k, value in enumerate(values):
            made[i + 4 * k][...] = value
            store(made[i + 4 * k], outs[4 + i + 4 * k])
    for copy in copies:
        copy.wait()


def fused_body(
    devices,
    image_big, image_small, slope_big, slope_small,
    conv1_weight, conv2_weight, proj_weight, norm_params,
    first_conv1, first_conv2, first_proj, first_norms,
    second_conv1, second_conv2, second_proj, second_norms,
):
    nb_img, side_b = image_big.shape[0], image_big.shape[1]
    ns_img, side_s = image_small.shape[0], image_small.shape[1]
    ob, os_ = side_b // 2, side_s // 2
    rows = ob * ob * nb_img + os_ * os_ * ns_img
    cfg = (nb_img, ns_img, ob, os_, ob * ob * nb_img * devices, os_ * os_ * ns_img * devices)
    r1, r2 = conv1_weight.shape[2], conv2_weight.shape[2]

    def parity(images, side):
        images = jnp.transpose(images, (1, 2, 0, 3))
        return images.reshape(side // 2, 2, side // 2, 2, images.shape[2], C_IN)

    def flat(weight):
        return weight.reshape((9,) + weight.shape[2:])

    vmem = pl.BlockSpec(memory_space=pltpu.VMEM)
    anywhere = pl.BlockSpec(memory_space=pl.ANY)
    hbm = pl.BlockSpec(memory_space=pltpu.HBM)
    shape = jax.ShapeDtypeStruct
    out_shape = (
        pltpu.VMEM((ob, ob, slope_big.shape[0], 128), BF16),
        pltpu.VMEM((os_, os_, slope_small.shape[0], 128), BF16),
        pltpu.VMEM((ob, 2, ob, 2, nb_img, C_IN), BF16),
        pltpu.VMEM((os_, 2, os_, 2, ns_img, C_IN), BF16),
        pltpu.VMEM((10, r1, 128), F32),
        pltpu.VMEM((9, r2, 128), F32),
        pltpu.VMEM((6, 128), F32),
    ) + tuple(pltpu.VMEM(s, F32) for s in ((9, r1, 128), (9, r2, 128), (r1, 128), (6, 128)) * 3)

    def sum_buffers(taps, r):
        return [
            pltpu.VMEM((taps, 2, 2, 2, r, 512), BF16),
            pltpu.VMEM((taps, 2, 2, r, 512), BF16),
            pltpu.VMEM((taps, 2, r, 256), BF16),
            pltpu.VMEM((taps, 2, r, 256), BF16),
            pltpu.VMEM((taps, r, 256), BF16),
            pltpu.VMEM((taps, r, 256), BF16),
            pltpu.VMEM((taps, r, 512), BF16),
            pltpu.VMEM((3, taps, r, 128), BF16),
        ]

    def maps(extra):
        return [
            pltpu.VMEM((ob + extra, ob + extra, nb_img, 512), BF16),
            pltpu.VMEM((os_ + extra, os_ + extra, ns_img, 512), BF16),
        ]

    scratch = (
        [
            pltpu.VMEM((10, 2, 2, 2, r1, 512), BF16),
            pltpu.VMEM((9, 2, 2, 2, r2, 512), BF16),
            pltpu.VMEM((2, 2, ob + 1, ob + 1, nb_img, C_IN), BF16),
            pltpu.VMEM((2, 2, os_ + 1, os_ + 1, ns_img, C_IN), BF16),
        ]
        + maps(2)
        + [pltpu.VMEM((rows, 512), F32) for _ in range(5)]
        + maps(0)
        + maps(0)
        + maps(2)
        + maps(0)
        + maps(1)
        + [
            pltpu.VMEM((4, 8, 128), F32),
            pltpu.VMEM((8, 512), F32),
            pltpu.VMEM((5, 8, 8, 512), F32),
            pltpu.VMEM((5, 4, 8, 512), F32),
        ]
        + sum_buffers(10, r1)
        + sum_buffers(9, r2)
        + [
            pltpu.SemaphoreType.DMA((COPIES,)),
            pltpu.SemaphoreType.DMA((COPIES,)),
            pltpu.SemaphoreType.DMA((24,)),
        ]
    )
    macs = rows * 512 * (9 * C_IN + 9 * C_OUT + C_IN) * 3
    out_big, out_small, grad_big, grad_small, grad_one, grad_two, grad_norms, *states = pl.pallas_call(
        functools.partial(block_kernel, cfg),
        out_shape=out_shape,
        in_specs=[hbm] * 16,
        out_specs=[anywhere] * 2 + [vmem] * 17,
        scratch_shapes=scratch,
        compiler_params=pltpu.CompilerParams(
            collective_id=0, has_side_effects=True, vmem_limit_bytes=VMEM_BYTES
        ),
        cost_estimate=pl.CostEstimate(flops=2 * macs, bytes_accessed=1 << 23, transcendentals=rows * 2048),
    )(
        parity(image_big, side_b),
        parity(image_small, side_s),
        jnp.transpose(slope_big, (1, 2, 0, 3)),
        jnp.transpose(slope_small, (1, 2, 0, 3)),
        flat(conv1_weight),
        flat(conv2_weight),
        proj_weight,
        norm_params,
        flat(first_conv1),
        flat(first_conv2),
        first_proj,
        first_norms,
        flat(second_conv1),
        flat(second_conv2),
        second_proj,
        second_norms,
    )
    passed = (out_big, out_small, grad_big, grad_small)
    sums = (grad_one, grad_two, grad_norms)
    out_big, out_small, grad_big, grad_small, *updated = pl.pallas_call(
        update_kernel,
        out_shape=[shape(v.shape, v.dtype) for v in passed] + [shape(w.shape, F32) for w in states[:4]] * 4,
        in_specs=[vmem] * 19,
        out_specs=[hbm] * 20,
        scratch_shapes=[pltpu.VMEM(w.shape, F32) for w in states[:4]] * 3 + [pltpu.SemaphoreType.DMA((20,))],
        compiler_params=pltpu.CompilerParams(vmem_limit_bytes=16 << 20),
    )(
        *passed, *sums, *states,
    )
    updated = [
        value.reshape((3, 3) + value.shape[1:]) if value.ndim == 3 else value for value in updated
    ]

    def unparity(images, side):
        images = images.reshape(side, side, images.shape[4], C_IN)
        return jnp.transpose(images, (2, 0, 1, 3))

    return (
        jnp.transpose(out_big, (2, 0, 1, 3)),
        jnp.transpose(out_small, (2, 0, 1, 3)),
        unparity(grad_big, side_b),
        unparity(grad_small, side_s),
        *updated,
    )


def solution(mesh):
    images = P(("batch", "chan"), None, None, None)
    maps = P("batch", None, None, "chan")
    convs = P(None, None, "batch", "chan")
    proj = P("batch", "chan")
    norms = P(None, "chan")
    states = (convs, convs, proj, norms)
    fused = mesh.shape["batch"] == 8 and mesh.shape["chan"] == 4
    return jax.shard_map(
        functools.partial(fused_body, 32) if fused else plain_body,
        mesh=mesh,
        in_specs=(images, images, maps, maps) + states * 3,
        out_specs=(maps, maps, images, images) + states * 4,
        check_vma=False,
    )
```

```python
import functools

import jax
import jax.numpy as jnp
from jax import lax
from jax.experimental import pallas as pl
from jax.experimental.pallas import tpu as pltpu
from jax.sharding import PartitionSpec as P

C_IN = 256
C_OUT = 512
STEP = 5
NORM_EPS = 1e-05
BETA_ONE = 0.5
BETA_TWO = 0.5
ADAM_EPS = 1e-08
DECAY = 0.01
NORM_RATE = 0.3
MESH = pl.DeviceIdType.MESH
BF16 = jnp.bfloat16
F32 = jnp.float32
COPIES = 240
VMEM_BYTES = 56 << 20


def silu_slope(values):
    gate = jax.nn.sigmoid(values)
    return gate * (1.0 + values * (1.0 - gate))


def adamw_step(weight, gradient, first, second, rate, decay):
    first_new = BETA_ONE * first + (1.0 - BETA_ONE) * gradient
    second_new = BETA_TWO * second + (1.0 - BETA_TWO) * gradient * gradient
    first_hat = first_new / (1.0 - BETA_ONE**STEP)
    second_hat = second_new / (1.0 - BETA_TWO**STEP)
    updated = weight - rate * (first_hat / (jnp.sqrt(second_hat) + ADAM_EPS) + decay * weight)
    return (updated, first_new, second_new)


def fold(values):
    rows, channels = values.shape
    return jnp.sum(values.reshape(rows // 8, 8, channels), axis=0)


def block_kernel(
    cfg,
    img_big, img_small, slo_big, slo_small, w1_hbm, w2_hbm, wp_hbm, norms_hbm,
    f1_hbm, f2_hbm, fp_hbm, fn_hbm, s1_hbm, s2_hbm, sp_hbm, sn_hbm,
    out_big, out_small, grad_big, grad_small, grad_one_out, grad_two_out, grad_norms,
    w1_in, w2_in, wp_in, norms_in, f1, f2, fp, fn, s1, s2, sp, sn,
    w1, w2, x_big, x_small, h_big, h_small, first_pre, second_pre, proj_pre, work, act,
    sl_big, sl_small, os_big, os_small, t_big, t_small, p_big, p_small, s_big, s_small,
    norms, norm_rows, stat_a, stat_b, a1, r1, rx1, ry1, rxx1, ryy1, c1, rz1,
    a2, r2, rx2, ry2, rxx2, ryy2, c2, rz2,
    send_sem, recv_sem, local_sem,
):
    nb_img, ns_img, ob, os_, number_big, number_small = cfg
    rows_b, rows_s = ob * ob * nb_img, os_ * os_ * ns_img
    step_b, step_s = ob * nb_img, os_ * ns_img
    b = lax.axis_index("batch")
    z = lax.axis_index("chan")
    core = lax.rem(b, 2)
    x = lax.rem(lax.div(b, 2), 2)
    y = lax.div(b, 4)
    x_peer = (b + 2 - 4 * x, z)
    y_peer = (b + 4 - 8 * y, z)
    sibling = (b + 1 - 2 * core, z)
    odd, upper = lax.rem(z, 2), lax.div(z, 2)
    pair_peer, cross_peer = (b, z + 1 - 2 * odd), (b, lax.rem(z + 2, 4))
    z_peers = [(b, lax.rem(z + d, 4)) for d in (1, 2, 3)]
    b_peers = [(lax.rem(b + d, 8), z) for d in range(1, 8)]
    lanes = lambda which: pl.ds(pl.multiple_of(which * 128, 128), 128)
    mine = lanes(z)

    used = [0]
    started = []

    def send(src, dst, peer):
        slot = used[0]
        used[0] += 1
        copy = pltpu.make_async_remote_copy(
            src_ref=src,
            dst_ref=dst,
            send_sem=send_sem.at[slot],
            recv_sem=recv_sem.at[slot],
            device_id=peer,
            device_id_type=MESH,
        )
        copy.start()
        started.append(copy)
        return copy

    barrier = pltpu.get_barrier_semaphore()
    for peer in b_peers + z_peers:
        pl.semaphore_signal(barrier, inc=1, device_id=peer, device_id_type=MESH)

    loads = []

    def load(src, dst):
        copy = pltpu.make_async_copy(src, dst, local_sem.at[len(loads)])
        copy.start()
        loads.append(copy)

    for source, held in ((w1_hbm, w1_in), (w2_hbm, w2_in), (wp_hbm, wp_in), (norms_hbm, norms_in)):
        load(source, held)
    for hp in range(2):
        for wp in range(2):
            load(img_big.at[:, hp, :, wp], x_big.at[hp, wp, pl.ds(hp, ob), pl.ds(wp, ob)])
            load(img_small.at[:, hp, :, wp], x_small.at[hp, wp, pl.ds(hp, os_), pl.ds(wp, os_)])
    load(
        slo_big.at[:, :, pl.ds(pl.multiple_of(z * nb_img, nb_img), nb_img)],
        sl_big.at[:, :, :, mine],
    )
    load(
        slo_small.at[:, :, pl.ds(pl.multiple_of(z * ns_img, ns_img), ns_img)],
        sl_small.at[:, :, :, mine],
    )
    for source, held in (
        (f1_hbm, f1), (f2_hbm, f2), (fp_hbm, fp), (fn_hbm, fn),
        (s1_hbm, s1), (s2_hbm, s2), (sp_hbm, sp), (sn_hbm, sn),
    ):
        load(source, held)
    for copy in loads[:4]:
        copy.wait()
    w1[0:9, y, x, core, :, mine] = w1_in[...].astype(BF16)
    w1[9, y, x, core, :, mine] = wp_in[...].astype(BF16)
    w2[:, y, x, core, :, mine] = w2_in[...].astype(BF16)
    norms[z, 0:6] = norms_in[...]

    pl.semaphore_wait(barrier, 10)

    def finish(copies):
        for copy in copies:
            copy.wait_recv()

    class Gather:
        def __init__(self, w, lo, n):
            self.w, self.taps = w, pl.ds(lo, n)
            piece = w.at[self.taps, y, x, core, :, mine]
            self.over_z = [send(piece, piece, peer) for peer in z_peers]

        def near(self):
            finish(self.over_z)
            piece = self.w.at[self.taps, y, x, core]
            self.x_copy = send(piece, piece, x_peer)
            self.y_copy = send(piece, piece, y_peer)
            self.rest = [send(piece, piece, sibling)]

        def far(self):
            self.x_copy.wait_recv()
            part = self.w.at[self.taps, y, 1 - x, core, :, pl.ds(0, 256)]
            self.far_a = send(part, part, y_peer)
            self.y_copy.wait_recv()
            part = self.w.at[self.taps, 1 - y, x, core, :, pl.ds(256, 256)]
            self.far_b = send(part, part, x_peer)
            piece = self.w.at[self.taps, y, 1 - x, core]
            self.rest.append(send(piece, piece, sibling))
            piece = self.w.at[self.taps, 1 - y, x, core]
            self.rest.append(send(piece, piece, sibling))

        def early(self, count):
            finish(self.rest[:count])
            self.rest = self.rest[count:]

        def last(self):
            finish([self.far_a, self.far_b])
            piece = self.w.at[self.taps, 1 - y, 1 - x, core]
            self.rest.append(send(piece, piece, sibling))

        def done(self):
            finish(self.rest)

    one_a = Gather(w1, 0, 3)
    z_norms = [send(norms.at[z], norms.at[z], peer) for peer in z_peers]
    one_b, one_c = Gather(w1, 3, 3), Gather(w1, 6, 4)
    two_a, two_b, two_c = (Gather(w2, lo, 3) for lo in (0, 3, 6))

    zero = functools.partial(jnp.zeros, dtype=BF16)
    for wp in range(2):
        x_big[1, wp, 0] = zero((ob + 1, nb_img, 256))
        x_small[1, wp, 0] = zero((os_ + 1, ns_img, 256))
    for hp in range(2):
        x_big[hp, 1, :, 0] = zero((ob + 1, nb_img, 256))
        x_small[hp, 1, :, 0] = zero((os_ + 1, ns_img, 256))
    for ref, side, images in (
        (h_big, ob, nb_img), (t_big, ob, nb_img), (h_small, os_, ns_img), (t_small, os_, ns_img),
    ):
        ref[0] = zero((side + 2, images, 512))
        ref[side + 1] = zero((side + 2, images, 512))
        ref[:, 0] = zero((side + 2, images, 512))
        ref[:, side + 1] = zero((side + 2, images, 512))
    for ref, side, images in ((s_big, ob, nb_img), (s_small, os_, ns_img)):
        ref[side] = zero((side + 1, images, 512))
        ref[:, side] = zero((side + 1, images, 512))

    def both(big, small):
        return jnp.concatenate([big.reshape(rows_b, -1), small.reshape(rows_s, -1)], axis=0)

    def x_window(ta, tb):
        hp, wp, sa, sb = (ta + 1) % 2, (tb + 1) % 2, ta // 2, tb // 2
        return both(
            x_big[hp, wp, sa : sa + ob, sb : sb + ob],
            x_small[hp, wp, sa : sa + os_, sb : sb + os_],
        )

    def h_window(ta, tb, depth=slice(None)):
        return both(
            h_big[ta : ta + ob, tb : tb + ob, :, depth],
            h_small[ta : ta + os_, tb : tb + os_, :, depth],
        )

    def t_window(ta, tb):
        ta, tb = 2 - ta, 2 - tb
        return both(t_big[ta : ta + ob, tb : tb + ob], t_small[ta : ta + os_, tb : tb + os_])

    def s_window(sa, sb):
        return both(s_big[sa : sa + ob, sb : sb + ob], s_small[sa : sa + os_, sb : sb + os_])

    def row_of(window, ta):
        return jnp.concatenate([window(ta, tb) for tb in range(3)], axis=1)

    def dot(left, right):
        return jnp.dot(left, right, preferred_element_type=F32)

    def dot_t(left, right):
        return lax.dot_general(left, right, (((1,), (1,)), ((), ())), preferred_element_type=F32)

    def dot_rows(left, right):
        return lax.dot_general(left, right, (((0,), (0,)), ((), ())), preferred_element_type=F32)

    slope_copies = []

    def slopes_over_z(source, target, lo, n, images):
        for d in (1, 2, 3):
            to = lax.rem(z + d, 4)
            rows = pl.ds(pl.multiple_of(to * images, images), images)
            slope_copies.append(
                send(source.at[pl.ds(lo, n), :, rows], target.at[pl.ds(lo, n), :, :, mine], (b, to))
            )

    big_parts = ((0, 4), (4, ob - 4))
    out_parts = ((0, 4), (4, 1), (5, ob - 5))
    one_a.near()
    one_b.near()
    one_a.far()
    one_c.near()
    one_b.far()
    one_c.far()
    two_a.near()
    one_a.last()
    one_b.last()
    one_c.last()
    two_b.near()
    slopes_over_z(slo_big, sl_big, *big_parts[0], nb_img)
    finish(z_norms)
    gains = [
        jnp.concatenate([norms[q, r : r + 1, :] for q in range(4)], axis=1) for r in range(6)
    ]
    for copy in loads[4:]:
        copy.wait()
    one_a.done()
    one_b.done()
    one_c.done()

    def reduce_start(k, rows):
        for r, row in enumerate(rows):
            stat_a[k, b, r : r + 1, :] = jnp.sum(row, axis=0, keepdims=True)
        part = stat_a.at[k, b, pl.ds(0, len(rows))]
        return [send(part, part, peer) for peer in b_peers]

    def reduce_middle(k, n, copies):
        finish(copies)
        stat_b[k, z, 0:n] = jnp.sum(stat_a[k, :, 0:n], axis=0)
        part = stat_b.at[k, z, pl.ds(0, n)]
        return [send(part, part, peer) for peer in z_peers]

    def reduce_end(k, n, copies):
        finish(copies)
        total = jnp.sum(stat_b[k, :, 0:n], axis=0)
        return [total[r : r + 1, :] for r in range(n)]

    def chunk_big(i):
        return pl.ds(pl.multiple_of(i * step_b, 16), step_b)

    def chunk_small(i):
        return pl.ds(pl.multiple_of(rows_b + i * step_s, 16), step_s)

    def over_groups(body, count):
        start = tuple(jnp.zeros((8, 512), F32) for _ in range(count))
        big = lax.fori_loop(0, ob, lambda i, c: body(0, i, chunk_big(i), c), start)
        small = lax.fori_loop(0, os_, lambda i, c: body(1, i, chunk_small(i), c), start)
        return big, small

    def moments(ref):
        def body(group, i, rows, carry):
            v = ref[rows, :]
            return (carry[0] + fold(v), carry[1] + fold(v * v))

        return over_groups(body, 2)

    def conv_row(ref, window, w, depth, ta):
        term = dot(row_of(window, ta), w[3 * ta : 3 * ta + 3].reshape(3 * depth, 512))
        if ta == 0:
            ref[...] = term
        else:
            ref[...] += term

    conv_row(first_pre, x_window, w1, 256, 0)
    conv_row(first_pre, x_window, w1, 256, 1)
    two_a.far()
    conv_row(first_pre, x_window, w1, 256, 2)
    first_big, first_small = moments(first_pre)
    copies = reduce_start(0, first_big + first_small)
    proj_pre[...] = dot(x_window(1, 1), w1[9].reshape(256, 512))
    side_big, side_small = moments(proj_pre)
    two_c.near()
    two_b.far()
    copies = reduce_middle(0, 4, copies)
    slopes_over_z(slo_big, sl_big, *big_parts[1], nb_img)
    slopes_over_z(slo_small, sl_small, 0, os_, ns_img)
    two_a.last()
    two_c.far()
    sums = reduce_end(0, 4, copies)

    def centered(total, square, number):
        center = total / number
        return center, lax.rsqrt(square / number - center * center + NORM_EPS)

    numbers = (number_big, number_small)
    first_stat = [centered(sums[2 * g], sums[2 * g + 1], numbers[g]) for g in range(2)]
    side_copies = reduce_start(4, side_big + side_small)

    def place(group, i, value, big, small, shift):
        if group == 0:
            big[i + shift, shift : shift + ob] = value.reshape(ob, nb_img, 512)
        else:
            small[i + shift, shift : shift + os_] = value.reshape(os_, ns_img, 512)

    def normed(ref, stat, rows):
        return (ref[rows, :] - stat[0]) * stat[1]

    def hide(group, i, rows, carry):
        value = normed(first_pre, first_stat[group], rows)
        first_pre[rows, :] = value
        shaped = value * gains[0] + gains[1]
        place(group, i, (shaped * jax.nn.sigmoid(shaped)).astype(BF16), h_big, h_small, 1)
        return carry

    over_groups(hide, 0)

    two_a.done()
    conv_row(second_pre, h_window, w2, 512, 0)
    two_b.last()

    def conv_last(blocks):
        pairs = [(tb, yy, xx) for tb in range(3) for yy, xx in blocks]
        second_pre[...] += dot(
            jnp.concatenate([h_window(2, tb, lanes(2 * yy + xx)) for tb, yy, xx in pairs], axis=1),
            jnp.concatenate([w2[6 + tb, yy, xx].reshape(128, 512) for tb, yy, xx in pairs], axis=0),
        )

    two_c.early(3)
    conv_last([(y, x), (y, 1 - x), (1 - y, x)])
    two_c.last()
    two_b.done()
    conv_row(second_pre, h_window, w2, 512, 1)
    side_copies = reduce_middle(4, 4, side_copies)
    two_c.done()
    conv_last([(1 - y, 1 - x)])
    second_big, second_small = moments(second_pre)
    copies = reduce_start(1, second_big + second_small)

    def prepare(group, i, rows, carry):
        act[rows, :] = silu_slope(first_pre[rows, :] * gains[0] + gains[1])
        return carry

    over_groups(prepare, 0)
    copies = reduce_middle(1, 4, copies)
    sums = reduce_end(4, 4, side_copies)
    side_stat = [centered(sums[2 * g], sums[2 * g + 1], numbers[g]) for g in range(2)]

    def prepare_side(group, i, rows, carry):
        proj_pre[rows, :] = normed(proj_pre, side_stat[group], rows)
        return carry

    over_groups(prepare_side, 0)
    finish(slope_copies)
    sums = reduce_end(1, 4, copies)
    second_stat = [centered(sums[2 * g], sums[2 * g + 1], numbers[g]) for g in range(2)]

    def outer(group, i, rows, carry):
        two = normed(second_pre, second_stat[group], rows)
        second_pre[rows, :] = two
        side = proj_pre[rows, :]
        summed = two * gains[2] + gains[3] + side * gains[4] + gains[5]
        gate = jax.nn.sigmoid(summed)
        place(group, i, (summed * gate).astype(BF16), os_big, os_small, 0)
        slope = sl_big[i] if group == 0 else sl_small[i]
        slope = slope.astype(F32).reshape(two.shape)
        upstream = slope * (gate * (1.0 + summed * (1.0 - gate)))
        work[rows, :] = upstream
        return (carry[0] + fold(upstream), carry[1] + fold(upstream * two), carry[2] + fold(upstream * side))

    outer_big, outer_small = over_groups(outer, 3)
    copies = reduce_start(2, outer_big + outer_small)
    stores = []

    def outputs_over_z(staged, target, lo, n, images):
        rows = pl.ds(pl.multiple_of(z * images, images), images)
        for d in (1, 2, 3):
            to = lax.rem(z + d, 4)
            stores.append(
                send(staged.at[pl.ds(lo, n), :, :, lanes(to)], target.at[pl.ds(lo, n), :, rows], (b, to))
            )

    copies = reduce_middle(2, 6, copies)
    outputs_over_z(os_small, out_small, 0, os_, ns_img)
    for staged, target, images in ((os_big, out_big, nb_img), (os_small, out_small, ns_img)):
        load(
            staged.at[:, :, :, mine],
            target.at[:, :, pl.ds(pl.multiple_of(z * images, images), images)],
        )
    sums_outer = reduce_end(2, 6, copies)
    outputs_over_z(os_big, out_big, *out_parts[0], nb_img)

    def slopes(group, i, rows, carry):
        total, cross_two, cross_side = sums_outer[3 * group : 3 * group + 3]
        number = numbers[group]
        base = work[rows, :] - total / number
        slope_two = gains[2] * second_stat[group][1] * (base - second_pre[rows, :] * (cross_two / number))
        place(group, i, slope_two.astype(BF16), t_big, t_small, 1)
        return carry

    def slopes_side(group, i, rows, carry):
        total, cross_two, cross_side = sums_outer[3 * group : 3 * group + 3]
        number = numbers[group]
        base = work[rows, :] - total / number
        slope_side = gains[4] * side_stat[group][1] * (base - proj_pre[rows, :] * (cross_side / number))
        place(group, i, slope_side.astype(BF16), p_big, p_small, 0)
        return carry

    over_groups(slopes, 0)

    class Scatter:
        def __init__(self, bufs, lo, n, pairs=False):
            self.bufs, self.taps, self.pairs = bufs, pl.ds(lo, n), pairs
            self.loop = lambda body: lax.fori_loop(lo, lo + n, lambda t, c: (body(t), c)[1], 0)
            a, r = bufs[0], bufs[1]
            self.copies = [send(a.at[self.taps, :, :, 1 - core], r.at[self.taps], sibling)]

        def near(self):
            finish(self.copies)
            a, r, rx, ry = self.bufs[:4]

            def add(t):
                r[t] = (r[t].astype(F32) + a[t, :, :, core].astype(F32)).astype(BF16)

            self.loop(add)
            taps = self.taps
            self.copies = [
                send(r.at[taps, :, 1 - x, :, pl.ds(0, 256)], rx.at[taps], x_peer),
                send(r.at[taps, 1 - y, :, :, pl.ds(256, 256)], ry.at[taps], y_peer),
            ]

        def far(self):
            finish(self.copies)
            _, r, rx, ry, rxx, ryy = self.bufs[:6]

            def add(t):
                rx[t] = (rx[t].astype(F32) + r[t, :, x, :, 0:256].astype(F32)).astype(BF16)
                ry[t] = (ry[t].astype(F32) + r[t, y, :, :, 256:512].astype(F32)).astype(BF16)

            self.loop(add)
            taps = self.taps
            self.copies = [
                send(rx.at[taps, 1 - y], ryy.at[taps], y_peer),
                send(ry.at[taps, 1 - x], rxx.at[taps], x_peer),
            ]

        def over_z(self):
            finish(self.copies)
            rx, ry, rxx, ryy, c, rz = self.bufs[2:8]

            def add(t):
                c[t, :, 0:256] = (rx[t, y].astype(F32) + ryy[t].astype(F32)).astype(BF16)
                c[t, :, 256:512] = (ry[t, x].astype(F32) + rxx[t].astype(F32)).astype(BF16)

            self.loop(add)
            to_z = lambda d: c.at[self.taps, :, lanes(lax.rem(z + d, 4))]
            if self.pairs:
                self.copies = [
                    send(c.at[self.taps, :, lanes(2 * far + 1 - odd)], rz.at[far, self.taps], pair_peer)
                    for far in range(2)
                ]
            else:
                self.copies = [
                    send(to_z(d), rz.at[d - 1, self.taps], (b, lax.rem(z + d, 4))) for d in (1, 2, 3)
                ]

        def cross(self):
            finish(self.copies)
            c, rz = self.bufs[6:8]

            def add(t):
                kept = c[t, :, lanes(2 * (1 - upper) + odd)].astype(F32)
                rz[1 - upper, t] = (rz[1 - upper, t].astype(F32) + kept).astype(BF16)

            self.loop(add)
            self.copies = [send(rz.at[1 - upper, self.taps], rz.at[2, self.taps], cross_peer)]

        def end(self):
            finish(self.copies)
            c, rz, out = self.bufs[6:]

            def add(t):
                total = c[t, :, mine].astype(F32)
                if self.pairs:
                    total = total + rz[upper, t].astype(F32) + rz[2, t].astype(F32)
                else:
                    for d in range(3):
                        total = total + rz[d, t].astype(F32)
                out[t] = total

            self.loop(add)

    t_flat = lambda: both(t_big[1 : ob + 1, 1 : ob + 1], t_small[1 : os_ + 1, 1 : os_ + 1])
    s_flat = lambda: both(s_big[0:ob, 0:ob], s_small[0:os_, 0:os_])
    p_flat = lambda: both(p_big[...], p_small[...])

    def grad_two(lo, n, pairs=False):
        for t in range(lo, lo + n):
            a2[t] = dot_rows(h_window(t // 3, t % 3), t_flat()).astype(BF16).reshape(a2.shape[1:])
        return Scatter((a2, r2, rx2, ry2, rxx2, ryy2, c2, rz2, grad_two_out), lo, n, pairs)

    one_bufs = (a1, r1, rx1, ry1, rxx1, ryy1, c1, rz1, grad_one_out)

    def grad_one(lo, n):
        windows = jnp.concatenate([x_window(t // 3, t % 3) for t in range(lo, lo + n)], axis=1)
        a1[lo : lo + n] = dot_rows(windows, s_flat()).astype(BF16).reshape((n,) + a1.shape[1:])
        return Scatter(one_bufs, lo, n)

    def grad_proj():
        a1[9] = dot_rows(x_window(1, 1), p_flat()).astype(BF16).reshape(a1.shape[1:])
        return Scatter(one_bufs, 9, 1)

    def back_row(ta):
        term = None
        for tb in range(3):
            part = dot_t(t_window(ta, tb), w2[3 * ta + tb].reshape(512, 512))
            term = part if term is None else term + part
        if ta == 0:
            second_pre[...] = term
        else:
            second_pre[...] += term

    sum_a = grad_two(0, 1)
    sum_b = grad_two(1, 2)
    sum_a.near()
    back_row(0)
    sum_b.near()
    back_row(1)
    sum_a.far()
    back_row(2)

    def inner(group, i, rows, carry):
        e = second_pre[rows, :] * act[rows, :]
        second_pre[rows, :] = e
        return (carry[0] + fold(e), carry[1] + fold(e * first_pre[rows, :]))

    inner_big, inner_small = over_groups(inner, 2)
    copies = reduce_start(3, inner_big + inner_small)
    sum_c = grad_two(3, 2)
    sum_b.far()
    sum_d = grad_two(5, 2)
    copies = reduce_middle(3, 4, copies)
    outputs_over_z(os_big, out_big, *out_parts[1], nb_img)
    sum_c.near()
    sum_e = grad_two(7, 2)
    sum_d.near()
    over_groups(slopes_side, 0)
    sums_inner = reduce_end(3, 4, copies)
    sum_a.over_z()
    sum_b.over_z()
    outputs_over_z(os_big, out_big, *out_parts[2], nb_img)

    def slopes_one(group, i, rows, carry):
        total, cross = sums_inner[2 * group : 2 * group + 2]
        number = numbers[group]
        slope = gains[0] * first_stat[group][1] * (
            second_pre[rows, :] - total / number - first_pre[rows, :] * (cross / number)
        )
        place(group, i, slope.astype(BF16), s_big, s_small, 0)
        return carry

    over_groups(slopes_one, 0)

    sum_f = grad_one(0, 2)
    sum_e.near()
    sum_c.far()
    sum_g = grad_one(2, 3)
    sum_f.near()
    sum_d.far()
    sum_p = grad_proj()
    sum_h = grad_one(5, 3)
    sum_g.near()
    sum_p.near()
    sum_c.over_z()
    sum_e.far()
    sum_i = grad_one(8, 1)
    sum_f.far()
    sum_h.near()
    sum_i.near()
    sum_d.over_z()

    def back_one(hp, wp):
        total = dot_t(p_flat(), w1[9].reshape(256, 512)) if hp + wp == 0 else None
        for ta in ((1,), (2, 0))[hp]:
            for tb in ((1,), (2, 0))[wp]:
                term = dot_t(
                    s_window(int(ta == 0), int(tb == 0)), w1[3 * ta + tb].reshape(256, 512)
                )
                total = term if total is None else total + term
        total = total.astype(BF16)
        grad_big[:, hp, :, wp] = total[:rows_b].reshape(ob, ob, nb_img, 256)
        grad_small[:, hp, :, wp] = total[rows_b:].reshape(os_, os_, ns_img, 256)

    back_one(0, 0)
    sum_g.far()
    sum_p.far()
    sum_e.over_z()
    back_one(0, 1)
    sum_f.over_z()
    sum_h.far()
    sum_i.far()
    back_one(1, 0)
    sum_p.over_z()
    sum_g.over_z()
    sum_h.over_z()
    sum_i.over_z()
    back_one(1, 1)
    rows = [
        sums_inner[1] + sums_inner[3],
        sums_inner[0] + sums_inner[2],
        sums_outer[1] + sums_outer[4],
        sums_outer[0] + sums_outer[3],
        sums_outer[2] + sums_outer[5],
        sums_outer[0] + sums_outer[3],
    ]
    for r, row in enumerate(rows):
        norm_rows[r : r + 1, :] = row
    grad_norms[...] = norm_rows[0:6, mine]
    early = len(started) - 40
    for copy in started[:early]:
        copy.wait_send()
    sum_a.end()
    sum_b.end()
    sum_c.end()
    sum_d.end()
    sum_e.end()
    sum_f.end()
    sum_p.end()
    sum_g.end()
    sum_h.end()
    sum_i.end()
    finish(stores)
    for copy in loads[22:]:
        copy.wait()
    for copy in started[early:]:
        copy.wait_send()
    assert used[0] <= COPIES


def tap_window(padded, tap_row, tap_col, stride, size_out):
    reach = stride * (size_out - 1) + 1
    return lax.slice(
        padded,
        (0, tap_row, tap_col, 0),
        (padded.shape[0], tap_row + reach, tap_col + reach, padded.shape[3]),
        (1, stride, stride, 1),
    )


def conv_taps(inputs, kernel, stride):
    size_out = (inputs.shape[1] - 1) // stride + 1
    padded = jnp.pad(inputs, ((0, 0), (1, 1), (1, 1), (0, 0)))
    summed = jnp.zeros((inputs.shape[0], size_out, size_out, kernel.shape[3]), jnp.float32)
    for tap_row in range(3):
        for tap_col in range(3):
            window = tap_window(padded, tap_row, tap_col, stride, size_out)
            summed = summed + jnp.einsum(
                "nhwc,co->nhwo",
                window,
                kernel[tap_row, tap_col],
                preferred_element_type=jnp.float32,
            )
    return summed


def kernel_grad(inputs, slope, stride):
    size_out = slope.shape[1]
    padded = jnp.pad(inputs, ((0, 0), (1, 1), (1, 1), (0, 0)))
    tap_rows = []
    for tap_row in range(3):
        across = []
        for tap_col in range(3):
            window = tap_window(padded, tap_row, tap_col, stride, size_out)
            across.append(
                jnp.einsum("nhwc,nhwo->co", window, slope, preferred_element_type=jnp.float32)
            )
        tap_rows.append(jnp.stack(across))
    return jnp.stack(tap_rows)


def input_grad(slope, kernel, stride, size_in):
    size_out = slope.shape[1]
    full_size = size_in + 2
    reach = stride * (size_out - 1) + 1
    summed = jnp.zeros((slope.shape[0], full_size, full_size, kernel.shape[2]), jnp.float32)
    for tap_row in range(3):
        for tap_col in range(3):
            term = jnp.einsum(
                "nhwo,co->nhwc", slope, kernel[tap_row, tap_col], preferred_element_type=jnp.float32
            )
            summed = summed + lax.pad(
                term,
                jnp.float32(0.0),
                (
                    (0, 0, 0),
                    (tap_row, full_size - tap_row - reach, stride - 1),
                    (tap_col, full_size - tap_col - reach, stride - 1),
                    (0, 0, 0),
                ),
            )
    return summed[:, 1:-1, 1:-1, :]


def proj_input_grad(slope, kernel, size_in):
    term = jnp.einsum("nhwo,co->nhwc", slope, kernel, preferred_element_type=jnp.float32)
    margin = size_in - 2 * slope.shape[1] + 1
    return lax.pad(term, jnp.float32(0.0), ((0, 0, 0), (0, margin, 1), (0, margin, 1), (0, 0, 0)))


def moments(values):
    return (jnp.sum(values, axis=(0, 1, 2)), jnp.sum(values * values, axis=(0, 1, 2)))


def normalize(values, total, square_total, number):
    center = total / number
    factor = lax.rsqrt(square_total / number - center * center + NORM_EPS)
    return ((values - center) * factor, factor)


def norm_back(upstream, normed, factor, gain, total, cross, number):
    return gain * factor * (upstream - total / number - normed * (cross / number))


def plain_body(
    image_big,
    image_small,
    slope_big,
    slope_small,
    conv1_weight,
    conv2_weight,
    proj_weight,
    norm_params,
    first_conv1,
    first_conv2,
    first_proj,
    first_norms,
    second_conv1,
    second_conv2,
    second_proj,
    second_norms,
):
    bfloat = jnp.bfloat16
    kernel_one, kernel_two, kernel_proj = (
        lax.all_gather(conv1_weight.astype(bfloat), "batch", axis=2, tiled=True),
        lax.all_gather(conv2_weight.astype(bfloat), "batch", axis=2, tiled=True),
        lax.all_gather(proj_weight.astype(bfloat), "batch", axis=0, tiled=True),
    )
    inputs_big, inputs_small = (
        lax.all_gather(image_big, "chan", axis=0, tiled=True),
        lax.all_gather(image_small, "chan", axis=0, tiled=True),
    )
    groups = (inputs_big, inputs_small)
    batch_width = lax.axis_size("batch")
    first_pre = [conv_taps(images, kernel_one, 2) for images in groups]
    numbers = [
        values.shape[0] * values.shape[1] * values.shape[2] * batch_width for values in first_pre
    ]
    sum_big, square_big = moments(first_pre[0])
    sum_small, square_small = moments(first_pre[1])
    sum_big, square_big, sum_small, square_small = lax.psum(
        (sum_big, square_big, sum_small, square_small), "batch"
    )
    first_norm = [
        normalize(first_pre[0], sum_big, square_big, numbers[0]),
        normalize(first_pre[1], sum_small, square_small, numbers[1]),
    ]
    shaped = [normed * norm_params[0] + norm_params[1] for normed, factor in first_norm]
    hidden = [jax.nn.silu(values).astype(bfloat) for values in shaped]
    hidden_big, hidden_small = (
        lax.all_gather(hidden[0], "chan", axis=3, tiled=True),
        lax.all_gather(hidden[1], "chan", axis=3, tiled=True),
    )
    hidden_full = (hidden_big, hidden_small)
    second_pre = [conv_taps(values, kernel_two, 1) for values in hidden_full]
    proj_pre = [
        jnp.einsum(
            "nhwc,co->nhwo", images[:, ::2, ::2, :], kernel_proj, preferred_element_type=jnp.float32
        )
        for images in groups
    ]
    two_big, two_sq_big = moments(second_pre[0])
    two_small, two_sq_small = moments(second_pre[1])
    side_big, side_sq_big = moments(proj_pre[0])
    side_small, side_sq_small = moments(proj_pre[1])
    (
        two_big,
        two_sq_big,
        two_small,
        two_sq_small,
        side_big,
        side_sq_big,
        side_small,
        side_sq_small,
    ) = lax.psum(
        (
            two_big,
            two_sq_big,
            two_small,
            two_sq_small,
            side_big,
            side_sq_big,
            side_small,
            side_sq_small,
        ),
        "batch",
    )
    second_norm = [
        normalize(second_pre[0], two_big, two_sq_big, numbers[0]),
        normalize(second_pre[1], two_small, two_sq_small, numbers[1]),
    ]
    proj_norm = [
        normalize(proj_pre[0], side_big, side_sq_big, numbers[0]),
        normalize(proj_pre[1], side_small, side_sq_small, numbers[1]),
    ]
    summed = [
        second_norm[which][0] * norm_params[2]
        + norm_params[3]
        + proj_norm[which][0] * norm_params[4]
        + norm_params[5]
        for which in range(2)
    ]
    out_big = jax.nn.silu(summed[0]).astype(bfloat)
    out_small = jax.nn.silu(summed[1]).astype(bfloat)
    slopes = (slope_big, slope_small)
    upstream = [slopes[which].astype(jnp.float32) * silu_slope(summed[which]) for which in range(2)]
    outer_big = jnp.sum(upstream[0], axis=(0, 1, 2))
    cross_two_big = jnp.sum(upstream[0] * second_norm[0][0], axis=(0, 1, 2))
    cross_side_big = jnp.sum(upstream[0] * proj_norm[0][0], axis=(0, 1, 2))
    outer_small = jnp.sum(upstream[1], axis=(0, 1, 2))
    cross_two_small = jnp.sum(upstream[1] * second_norm[1][0], axis=(0, 1, 2))
    cross_side_small = jnp.sum(upstream[1] * proj_norm[1][0], axis=(0, 1, 2))
    outer_big, cross_two_big, cross_side_big, outer_small, cross_two_small, cross_side_small = (
        lax.psum(
            (
                outer_big,
                cross_two_big,
                cross_side_big,
                outer_small,
                cross_two_small,
                cross_side_small,
            ),
            "batch",
        )
    )
    outer_sums = (outer_big, outer_small)
    cross_two = (cross_two_big, cross_two_small)
    cross_side = (cross_side_big, cross_side_small)
    slope_two = [
        norm_back(
            upstream[which],
            second_norm[which][0],
            second_norm[which][1],
            norm_params[2],
            outer_sums[which],
            cross_two[which],
            numbers[which],
        ).astype(bfloat)
        for which in range(2)
    ]
    slope_proj = [
        norm_back(
            upstream[which],
            proj_norm[which][0],
            proj_norm[which][1],
            norm_params[4],
            outer_sums[which],
            cross_side[which],
            numbers[which],
        ).astype(bfloat)
        for which in range(2)
    ]
    part_big = input_grad(slope_two[0], kernel_two, 1, hidden_big.shape[1])
    part_small = input_grad(slope_two[1], kernel_two, 1, hidden_small.shape[1])
    back_big, back_small = (
        lax.psum_scatter(part_big, "chan", scatter_dimension=3, tiled=True),
        lax.psum_scatter(part_small, "chan", scatter_dimension=3, tiled=True),
    )
    inner = [back_big * silu_slope(shaped[0]), back_small * silu_slope(shaped[1])]
    inner_big = jnp.sum(inner[0], axis=(0, 1, 2))
    cross_one_big = jnp.sum(inner[0] * first_norm[0][0], axis=(0, 1, 2))
    inner_small = jnp.sum(inner[1], axis=(0, 1, 2))
    cross_one_small = jnp.sum(inner[1] * first_norm[1][0], axis=(0, 1, 2))
    inner_big, cross_one_big, inner_small, cross_one_small = lax.psum(
        (inner_big, cross_one_big, inner_small, cross_one_small), "batch"
    )
    inner_sums = (inner_big, inner_small)
    cross_one = (cross_one_big, cross_one_small)
    slope_one = [
        norm_back(
            inner[which],
            first_norm[which][0],
            first_norm[which][1],
            norm_params[0],
            inner_sums[which],
            cross_one[which],
            numbers[which],
        ).astype(bfloat)
        for which in range(2)
    ]
    size_big = image_big.shape[1]
    size_small = image_small.shape[1]
    input_part_big = input_grad(slope_one[0], kernel_one, 2, size_big) + proj_input_grad(
        slope_proj[0], kernel_proj, size_big
    )
    input_part_small = input_grad(slope_one[1], kernel_one, 2, size_small) + proj_input_grad(
        slope_proj[1], kernel_proj, size_small
    )
    grad_big, grad_small = (
        lax.psum_scatter(input_part_big, "chan", scatter_dimension=0, tiled=True),
        lax.psum_scatter(input_part_small, "chan", scatter_dimension=0, tiled=True),
    )
    part_conv1 = kernel_grad(groups[0], slope_one[0], 2) + kernel_grad(groups[1], slope_one[1], 2)
    part_conv2 = kernel_grad(hidden_full[0], slope_two[0], 1) + kernel_grad(
        hidden_full[1], slope_two[1], 1
    )
    part_proj = jnp.einsum(
        "nhwc,nhwo->co",
        groups[0][:, ::2, ::2, :],
        slope_proj[0],
        preferred_element_type=jnp.float32,
    ) + jnp.einsum(
        "nhwc,nhwo->co",
        groups[1][:, ::2, ::2, :],
        slope_proj[1],
        preferred_element_type=jnp.float32,
    )
    grad_conv1, grad_conv2, grad_proj = (
        lax.psum_scatter(part_conv1, "batch", scatter_dimension=2, tiled=True),
        lax.psum_scatter(part_conv2, "batch", scatter_dimension=2, tiled=True),
        lax.psum_scatter(part_proj, "batch", scatter_dimension=0, tiled=True),
    )
    grad_norms = jnp.stack(
        [
            cross_one_big + cross_one_small,
            inner_big + inner_small,
            cross_two_big + cross_two_small,
            outer_big + outer_small,
            cross_side_big + cross_side_small,
            outer_big + outer_small,
        ]
    )
    new_conv1, moment_conv1, square_conv1 = adamw_step(
        conv1_weight, grad_conv1, first_conv1, second_conv1, (9.0 * C_IN) ** (-0.5), DECAY
    )
    new_conv2, moment_conv2, square_conv2 = adamw_step(
        conv2_weight, grad_conv2, first_conv2, second_conv2, (9.0 * C_OUT) ** (-0.5), DECAY
    )
    new_proj, moment_proj, square_proj = adamw_step(
        proj_weight, grad_proj, first_proj, second_proj, (1.0 * C_IN) ** (-0.5), DECAY
    )
    new_norms, moment_norms, square_norms = adamw_step(
        norm_params, grad_norms, first_norms, second_norms, NORM_RATE, 0.0
    )
    return (
        out_big,
        out_small,
        grad_big.astype(bfloat),
        grad_small.astype(bfloat),
        grad_conv1,
        grad_conv2,
        grad_proj,
        grad_norms,
        new_conv1,
        new_conv2,
        new_proj,
        new_norms,
        moment_conv1,
        moment_conv2,
        moment_proj,
        moment_norms,
        square_conv1,
        square_conv2,
        square_proj,
        square_norms,
    )


def update_kernel(*refs):
    passed, (g1, g2, gn), states, rest = refs[:4], refs[4:7], refs[7:19], refs[19:]
    passed_out, outs, made, sem = rest[:4], rest[4:20], rest[20:32], rest[32]
    gradients = (g1.at[pl.ds(0, 9)], g2, g1.at[9], gn)
    copies = []

    def store(src, dst):
        copy = pltpu.make_async_copy(src, dst, sem.at[len(copies)])
        copy.start()
        copies.append(copy)

    for src, dst in zip(passed + gradients, passed_out + outs[:4]):
        store(src, dst)
    rates = ((9.0 * C_IN) ** (-0.5), (9.0 * C_OUT) ** (-0.5), (1.0 * C_IN) ** (-0.5), NORM_RATE)
    for i in range(4):
        weight, first, second = (states[i + 4 * k][...] for k in range(3))
        values = adamw_step(
            weight, gradients[i][...], first, second, rates[i], DECAY if i < 3 else 0.0
        )
        for k, value in enumerate(values):
            made[i + 4 * k][...] = value
            store(made[i + 4 * k], outs[4 + i + 4 * k])
    for copy in copies:
        copy.wait()


def fused_body(
    devices,
    image_big, image_small, slope_big, slope_small,
    conv1_weight, conv2_weight, proj_weight, norm_params,
    first_conv1, first_conv2, first_proj, first_norms,
    second_conv1, second_conv2, second_proj, second_norms,
):
    nb_img, side_b = image_big.shape[0], image_big.shape[1]
    ns_img, side_s = image_small.shape[0], image_small.shape[1]
    ob, os_ = side_b // 2, side_s // 2
    rows = ob * ob * nb_img + os_ * os_ * ns_img
    cfg = (nb_img, ns_img, ob, os_, ob * ob * nb_img * devices, os_ * os_ * ns_img * devices)
    r1, r2 = conv1_weight.shape[2], conv2_weight.shape[2]

    def parity(images, side):
        images = jnp.transpose(images, (1, 2, 0, 3))
        return images.reshape(side // 2, 2, side // 2, 2, images.shape[2], C_IN)

    def flat(weight):
        return weight.reshape((9,) + weight.shape[2:])

    vmem = pl.BlockSpec(memory_space=pltpu.VMEM)
    anywhere = pl.BlockSpec(memory_space=pl.ANY)
    hbm = pl.BlockSpec(memory_space=pltpu.HBM)
    shape = jax.ShapeDtypeStruct
    out_shape = (
        pltpu.VMEM((ob, ob, slope_big.shape[0], 128), BF16),
        pltpu.VMEM((os_, os_, slope_small.shape[0], 128), BF16),
        pltpu.VMEM((ob, 2, ob, 2, nb_img, C_IN), BF16),
        pltpu.VMEM((os_, 2, os_, 2, ns_img, C_IN), BF16),
        pltpu.VMEM((10, r1, 128), F32),
        pltpu.VMEM((9, r2, 128), F32),
        pltpu.VMEM((6, 128), F32),
    ) + tuple(pltpu.VMEM(s, F32) for s in ((9, r1, 128), (9, r2, 128), (r1, 128), (6, 128)) * 3)

    def sum_buffers(taps, r):
        return [
            pltpu.VMEM((taps, 2, 2, 2, r, 512), BF16),
            pltpu.VMEM((taps, 2, 2, r, 512), BF16),
            pltpu.VMEM((taps, 2, r, 256), BF16),
            pltpu.VMEM((taps, 2, r, 256), BF16),
            pltpu.VMEM((taps, r, 256), BF16),
            pltpu.VMEM((taps, r, 256), BF16),
            pltpu.VMEM((taps, r, 512), BF16),
            pltpu.VMEM((3, taps, r, 128), BF16),
        ]

    def maps(extra):
        return [
            pltpu.VMEM((ob + extra, ob + extra, nb_img, 512), BF16),
            pltpu.VMEM((os_ + extra, os_ + extra, ns_img, 512), BF16),
        ]

    scratch = (
        [
            pltpu.VMEM((10, 2, 2, 2, r1, 512), BF16),
            pltpu.VMEM((9, 2, 2, 2, r2, 512), BF16),
            pltpu.VMEM((2, 2, ob + 1, ob + 1, nb_img, C_IN), BF16),
            pltpu.VMEM((2, 2, os_ + 1, os_ + 1, ns_img, C_IN), BF16),
        ]
        + maps(2)
        + [pltpu.VMEM((rows, 512), F32) for _ in range(5)]
        + maps(0)
        + maps(0)
        + maps(2)
        + maps(0)
        + maps(1)
        + [
            pltpu.VMEM((4, 8, 128), F32),
            pltpu.VMEM((8, 512), F32),
            pltpu.VMEM((5, 8, 8, 512), F32),
            pltpu.VMEM((5, 4, 8, 512), F32),
        ]
        + sum_buffers(10, r1)
        + sum_buffers(9, r2)
        + [
            pltpu.SemaphoreType.DMA((COPIES,)),
            pltpu.SemaphoreType.DMA((COPIES,)),
            pltpu.SemaphoreType.DMA((24,)),
        ]
    )
    macs = rows * 512 * (9 * C_IN + 9 * C_OUT + C_IN) * 3
    out_big, out_small, grad_big, grad_small, grad_one, grad_two, grad_norms, *states = pl.pallas_call(
        functools.partial(block_kernel, cfg),
        out_shape=out_shape,
        in_specs=[hbm] * 16,
        out_specs=[anywhere] * 2 + [vmem] * 17,
        scratch_shapes=scratch,
        compiler_params=pltpu.CompilerParams(
            collective_id=0, has_side_effects=True, vmem_limit_bytes=VMEM_BYTES
        ),
        cost_estimate=pl.CostEstimate(flops=2 * macs, bytes_accessed=1 << 23, transcendentals=rows * 2048),
    )(
        parity(image_big, side_b),
        parity(image_small, side_s),
        jnp.transpose(slope_big, (1, 2, 0, 3)),
        jnp.transpose(slope_small, (1, 2, 0, 3)),
        flat(conv1_weight),
        flat(conv2_weight),
        proj_weight,
        norm_params,
        flat(first_conv1),
        flat(first_conv2),
        first_proj,
        first_norms,
        flat(second_conv1),
        flat(second_conv2),
        second_proj,
        second_norms,
    )
    passed = (out_big, out_small, grad_big, grad_small)
    sums = (grad_one, grad_two, grad_norms)
    out_big, out_small, grad_big, grad_small, *updated = pl.pallas_call(
        update_kernel,
        out_shape=[shape(v.shape, v.dtype) for v in passed] + [shape(w.shape, F32) for w in states[:4]] * 4,
        in_specs=[vmem] * 19,
        out_specs=[hbm] * 20,
        scratch_shapes=[pltpu.VMEM(w.shape, F32) for w in states[:4]] * 3 + [pltpu.SemaphoreType.DMA((20,))],
        compiler_params=pltpu.CompilerParams(vmem_limit_bytes=16 << 20),
    )(
        *passed, *sums, *states,
    )
    updated = [
        value.reshape((3, 3) + value.shape[1:]) if value.ndim == 3 else value for value in updated
    ]

    def unparity(images, side):
        images = images.reshape(side, side, images.shape[4], C_IN)
        return jnp.transpose(images, (2, 0, 1, 3))

    return (
        jnp.transpose(out_big, (2, 0, 1, 3)),
        jnp.transpose(out_small, (2, 0, 1, 3)),
        unparity(grad_big, side_b),
        unparity(grad_small, side_s),
        *updated,
    )


def solution(mesh):
    images = P(("batch", "chan"), None, None, None)
    maps = P("batch", None, None, "chan")
    convs = P(None, None, "batch", "chan")
    proj = P("batch", "chan")
    norms = P(None, "chan")
    states = (convs, convs, proj, norms)
    fused = mesh.shape["batch"] == 8 and mesh.shape["chan"] == 4
    return jax.shard_map(
        functools.partial(fused_body, 32) if fused else plain_body,
        mesh=mesh,
        in_specs=(images, images, maps, maps) + states * 3,
        out_specs=(maps, maps, images, images) + states * 4,
        check_vma=False,
    )
```
